32 devices in a mesh: dp: 16 (over z, y, x), tp: 2 (over core).
Axes of the slice: x: 2, y: 2, z: 4, core: 2. Of those that a mesh axis runs over, the one named last changes fastest.
Arguments:
- x_visible: bfloat16 [25088, 384], P('dp'), may hold values from -6 to 6
- patch_order: int32 [256, 196], P('dp'), may hold values from 0 to 195, each once within a row
- enc_qkv: bfloat16 [3, 384, 384], P(None, None, 'tp'), may hold values from -0.3125 to 0.3125
- enc_head_bias: float32 [2, 384], P(None, 'tp'), may hold values from -1.8 to 1.8
- enc_proj: bfloat16 [384, 384], P('tp'), may hold values from -1.25 to 1.25
- enc_fc1: bfloat16 [384, 1536], P(None, 'tp'), may hold values from -0.3125 to 0.3125
- enc_fc1_bias: float32 [1536], P('tp'), may hold values from -1.8 to 1.8
- enc_fc2: bfloat16 [1536, 384], P('tp'), may hold values from -0.15625 to 0.15625
- enc_gains: float32 [4, 384], replicated, may hold values from 0.25 to 1.75
- enc_shifts: float32 [4, 384], replicated, may hold values from -1.8 to 1.8
- reg_qkv: bfloat16 [3, 384, 384], P(None, None, 'tp'), may hold values from -0.3125 to 0.3125
- reg_head_bias: float32 [2, 384], P(None, 'tp'), may hold values from -1.8 to 1.8
- reg_proj: bfloat16 [384, 384], P('tp'), may hold values from -1.25 to 1.25
- reg_fc1: bfloat16 [384, 1536], P(None, 'tp'), may hold values from -0.3125 to 0.3125
- reg_fc1_bias: float32 [1536], P('tp'), may hold values from -1.8 to 1.8
- reg_fc2: bfloat16 [1536, 384], P('tp'), may hold values from -0.15625 to 0.15625
- reg_gains: float32 [5, 384], replicated, may hold values from 0.25 to 1.75
- reg_shifts: float32 [5, 384], replicated, may hold values from -1.8 to 1.8
- pos_embed: float32 [196, 384], replicated, may hold values from -3 to 3
- mask_token: float32 [384], replicated, may hold values from -3 to 3
- enc_cot: bfloat16 [25088, 384], P('dp'), may hold values from -6 to 6
- reg_cot: bfloat16 [25088, 384], P('dp'), may hold values from -6 to 6
Outputs:
- encoded: bfloat16 [25088, 384], P('dp')
- predicted: bfloat16 [25088, 384], P('dp')
- input_grad: float32 [25088, 384], P('dp')
- grad_enc_qkv: float32 [3, 384, 384], P(None, None, 'tp')
- grad_enc_head_bias: float32 [2, 384], P(None, 'tp')
- grad_enc_proj: float32 [384, 384], P('tp')
- grad_enc_fc1: float32 [384, 1536], P(None, 'tp')
- grad_enc_fc1_bias: float32 [1536], P('tp')
- grad_enc_fc2: float32 [1536, 384], P('tp')
- grad_enc_gains: float32 [4, 384], replicated
- grad_enc_shifts: float32 [4, 384], replicated
- grad_reg_qkv: float32 [3, 384, 384], P(None, None, 'tp')
- grad_reg_head_bias: float32 [2, 384], P(None, 'tp')
- grad_reg_proj: float32 [384, 384], P('tp')
- grad_reg_fc1: float32 [384, 1536], P(None, 'tp')
- grad_reg_fc1_bias: float32 [1536], P('tp')
- grad_reg_fc2: float32 [1536, 384], P('tp')
- grad_reg_gains: float32 [5, 384], replicated
- grad_reg_shifts: float32 [5, 384], replicated
- grad_pos_embed: float32 [196, 384], replicated
- grad_mask_token: float32 [384], replicated
The draws below stay inside these ranges and needn't reach their ends.
Inputs may be any that keep to these rules, and one draw needn't show every extreme that they name: `patch_order`: each row is a permutation of the 196 patch indices: the first 98 entries are the visible patches, the others the masked ones.
All inputs are finite; a program needn't handle non-finite values.
Results may differ from the reference program's by a relative error of at most 0.023.
Values may be sent and summed in bfloat16 or wider, within the bound.
No kernel may reach another device: no remote copies, remote signals or barrier semaphores. Data moves between devices by JAX's collectives and lax.ppermute only.
A program may use at most 192 MiB of HBM per device.

```python
import jax
import jax.numpy as jnp
from jax import lax

D = 384
HEAD_DIM = 64
MLP = 1536
PATCHES = 196
IMG_DEV = 16
VISIBLE = 98
IMAGES = 256
TOKENS = 25088
N_DP = 16
N_TP = 2


def shard_levels(key, shape, pieces, low, largest):
    loudness, own = 1.0, jax.random.fold_in(key, 6)
    for position, shards_of in pieces:
        draws = jnp.exp(jax.random.uniform(jax.random.fold_in(own, position), (shards_of,), jnp.float32, low / len(pieces), largest / len(pieces)))
        loudness = loudness * jnp.repeat(draws, shape[position] // shards_of).reshape([-1 if axis == position else 1 for axis in range(len(shape))])
    return loudness


def scatter_about(key, dims, deviation, limit, pieces=(), dtype=jnp.bfloat16):
    loudness = shard_levels(key, dims, pieces, -0.22, 0.18) if pieces else 1.0
    entries = jax.random.normal(key, dims, jnp.float32) * deviation * loudness
    return jnp.minimum(jnp.maximum(entries, -limit), limit).astype(dtype)


def setup_inputs(seed: int = 0) -> dict:
    arg_keys = jax.random.split(jax.random.key(seed), 23)
    return {
        "x_visible": scatter_about(arg_keys[0], (TOKENS, D), 1.0, 6.0, ((0, 16),)),
        "patch_order": jax.vmap(lambda own: jax.random.permutation(own, PATCHES))(jax.random.split(arg_keys[1], IMAGES)).reshape((IMAGES, PATCHES)).astype(jnp.int32),
        "enc_qkv": scatter_about(arg_keys[2], (3, D, D), D ** -0.5, 0.3125, ((2, 2),)),
        "enc_head_bias": scatter_about(arg_keys[3], (2, D), 0.3, 1.8, ((1, 2),), jnp.float32),
        "enc_proj": scatter_about(arg_keys[4], (D, D), (D // 16) ** -0.5, 1.25, ((0, 2),)),
        "enc_fc1": scatter_about(arg_keys[5], (D, MLP), D ** -0.5, 0.3125, ((1, 2),)),
        "enc_fc1_bias": scatter_about(arg_keys[6], (MLP,), 0.3, 1.8, ((0, 2),), jnp.float32),
        "enc_fc2": scatter_about(arg_keys[7], (MLP, D), MLP ** -0.5, 0.15625, ((0, 2),)),
        "enc_gains": jnp.clip(1.0 + 0.15 * jax.random.normal(arg_keys[8], (4, D), jnp.float32), 0.25, 1.75),
        "enc_shifts": scatter_about(arg_keys[9], (4, D), 0.3, 1.8, (), jnp.float32),
        "reg_qkv": scatter_about(arg_keys[10], (3, D, D), D ** -0.5, 0.3125, ((2, 2),)),
        "reg_head_bias": scatter_about(arg_keys[11], (2, D), 0.3, 1.8, ((1, 2),), jnp.float32),
        "reg_proj": scatter_about(arg_keys[12], (D, D), (D // 16) ** -0.5, 1.25, ((0, 2),)),
        "reg_fc1": scatter_about(arg_keys[13], (D, MLP), D ** -0.5, 0.3125, ((1, 2),)),
        "reg_fc1_bias": scatter_about(arg_keys[14], (MLP,), 0.3, 1.8, ((0, 2),), jnp.float32),
        "reg_fc2": scatter_about(arg_keys[15], (MLP, D), MLP ** -0.5, 0.15625, ((0, 2),)),
        "reg_gains": jnp.clip(1.0 + 0.15 * jax.random.normal(arg_keys[16], (5, D), jnp.float32), 0.25, 1.75),
        "reg_shifts": scatter_about(arg_keys[17], (5, D), 0.3, 1.8, (), jnp.float32),
        "pos_embed": scatter_about(arg_keys[18], (PATCHES, D), 0.5, 3.0, (), jnp.float32),
        "mask_token": scatter_about(arg_keys[19], (D,), 0.5, 3.0, (), jnp.float32),
        "enc_cot": scatter_about(arg_keys[20], (TOKENS, D), 1.0, 6.0, ((0, 16),)),
        "reg_cot": scatter_about(arg_keys[21], (TOKENS, D), 1.0, 6.0, ((0, 16),)),
    }


@jax.custom_vjp
def low(v):
    return lax.optimization_barrier(v.astype(jnp.bfloat16)).astype(jnp.float32)

@jax.custom_vjp
def low_back(v):
    return v

def low_keep(v):
    return (low(v), None)

def low_pass(kept, grad):
    return (grad,)

def back_keep(v):
    return (v, None)

def back_low(kept, grad):
    return (low(grad),)
low.defvjp(low_keep, low_pass)
low_back.defvjp(back_keep, back_low)
highest = lax.Precision.HIGHEST
epsilon = 1e-06

def both_ways(values):
    return low_back(low(values))

def layer_norm(values, gain_row, shift_row):
    centred = values - lax.optimization_barrier(jnp.mean(values, axis=-1, keepdims=True))
    variance = lax.optimization_barrier(jnp.mean(centred * centred, axis=-1, keepdims=True))
    return centred * lax.rsqrt(variance + epsilon) * gain_row + shift_row

def project(left_side, right_side):
    return jnp.einsum('bli,ij->blj', left_side, right_side, precision=highest)

def attend(queries, key_rows, value_rows):
    batch_size, row_count, feat_width = queries.shape
    head_count = feat_width // HEAD_DIM
    q_heads = queries.reshape(batch_size, row_count, head_count, HEAD_DIM)
    k_heads = key_rows.reshape(batch_size, -1, head_count, HEAD_DIM)
    v_heads = value_rows.reshape(batch_size, -1, head_count, HEAD_DIM)
    scores = low_back(jnp.einsum('bqhd,bkhd->bhqk', q_heads, k_heads, precision=highest) * HEAD_DIM ** (-0.5))
    weights = low(jax.nn.softmax(scores, axis=-1))
    output = jnp.einsum('bhqk,bkhd->bqhd', weights, v_heads, precision=highest)
    return both_ways(output.reshape(batch_size, row_count, feat_width))

def attention_branch(query_in, context_in, shared, qkv, head_bias, proj, proj_bias):
    share = proj.shape[0] // N_TP
    summed = jnp.zeros(query_in.shape[:-1] + (proj.shape[1],), jnp.float32)
    for group_index in range(N_TP):
        col_range = slice(group_index * share, (group_index + 1) * share)
        query_side = low_back(query_in)
        context_side = query_side if shared else low_back(context_in)
        queries = both_ways(project(query_side, qkv[0][:, col_range]) + head_bias[0, col_range])
        key_rows = both_ways(project(context_side, qkv[1][:, col_range]))
        value_rows = both_ways(project(context_side, qkv[2][:, col_range]) + head_bias[1, col_range])
        mixed_rows = attend(queries, key_rows, value_rows)
        summed = summed + low(project(mixed_rows, proj[col_range, :]))
    return low_back(summed) + proj_bias

def mlp_branch(act_in, w_first, first_bias, w_second, second_bias):
    share = w_first.shape[1] // N_TP
    summed = jnp.zeros(act_in.shape, jnp.float32)
    for group_index in range(N_TP):
        col_range = slice(group_index * share, (group_index + 1) * share)
        input_side = low_back(act_in)
        before = low_back(project(input_side, w_first[:, col_range]) + first_bias[col_range])
        hidden = low(jax.nn.gelu(before, approximate=False))
        summed = summed + low(project(hidden, w_second[col_range, :]))
    return low_back(summed) + second_bias

def forward(params, visible, order):
    enc_qkv, enc_head_bias, enc_proj, enc_fc1, enc_fc1_bias, enc_fc2, enc_gains, enc_shifts, reg_qkv, reg_head_bias, reg_proj, reg_fc1, reg_fc1_bias, reg_fc2, reg_gains, reg_shifts, pos_embed, mask_token = params
    image_count = order.shape[0]
    inputs = visible.reshape(image_count, VISIBLE, D)
    norm_one = low(layer_norm(inputs, enc_gains[0], enc_shifts[0]))
    state_one = inputs + enc_gains[2] * attention_branch(norm_one, norm_one, True, enc_qkv, enc_head_bias, enc_proj, enc_shifts[2])
    norm_two = low(layer_norm(state_one, enc_gains[1], enc_shifts[1]))
    encoded = state_one + enc_gains[3] * mlp_branch(norm_two, enc_fc1, enc_fc1_bias, enc_fc2, enc_shifts[3])
    seen_pos = jnp.take(pos_embed, order[:, :VISIBLE], axis=0)
    masked_pos = jnp.take(pos_embed, order[:, VISIBLE:], axis=0)
    mask_rows = mask_token + masked_pos
    context = jnp.concatenate([encoded + seen_pos, mask_rows], axis=1)
    norm_three = low(layer_norm(mask_rows, reg_gains[0], reg_shifts[0]))
    norm_four = low(layer_norm(context, reg_gains[1], reg_shifts[1]))
    state_three = mask_rows + reg_gains[3] * attention_branch(norm_three, norm_four, False, reg_qkv, reg_head_bias, reg_proj, reg_shifts[3])
    norm_five = low(layer_norm(state_three, reg_gains[2], reg_shifts[2]))
    predicted = state_three + reg_gains[4] * mlp_branch(norm_five, reg_fc1, reg_fc1_bias, reg_fc2, reg_shifts[4])
    return (encoded.reshape(-1, D), predicted.reshape(-1, D))

def reference(x_visible, patch_order, enc_qkv, enc_head_bias, enc_proj, enc_fc1, enc_fc1_bias, enc_fc2, enc_gains, enc_shifts, reg_qkv, reg_head_bias, reg_proj, reg_fc1, reg_fc1_bias, reg_fc2, reg_gains, reg_shifts, pos_embed, mask_token, enc_cot, reg_cot):
    params = tuple((item.astype(jnp.float32) for item in (enc_qkv, enc_head_bias, enc_proj, enc_fc1, enc_fc1_bias, enc_fc2, enc_gains, enc_shifts, reg_qkv, reg_head_bias, reg_proj, reg_fc1, reg_fc1_bias, reg_fc2, reg_gains, reg_shifts, pos_embed, mask_token)))
    group_rows = IMG_DEV * VISIBLE
    visible_all = x_visible.astype(jnp.float32).reshape(N_DP, group_rows, D)
    order_all = patch_order.reshape(N_DP, IMG_DEV, PATCHES)
    enc_all = enc_cot.astype(jnp.float32).reshape(N_DP, group_rows, D)
    reg_all = reg_cot.astype(jnp.float32).reshape(N_DP, group_rows, D)

    def step(totals, item):
        visible, order, enc_grad, reg_grad = item
        outputs, pull = jax.vjp(lambda prm, vis: forward(prm, vis, order), params, visible)
        grads, visible_grad = pull((enc_grad, reg_grad))
        totals = jax.tree.map(lambda left_side, right_side: left_side + right_side, totals, grads)
        return (totals, (outputs[0], outputs[1], visible_grad))
    zeros = jax.tree.map(jnp.zeros_like, params)
    totals, (encoded, predicted, visible_grad) = lax.scan(step, zeros, (visible_all, order_all, enc_all, reg_all))
    return (encoded.reshape(-1, D).astype(jnp.bfloat16), predicted.reshape(-1, D).astype(jnp.bfloat16), visible_grad.reshape(-1, D), totals[0], totals[1], totals[2], totals[3], totals[4], totals[5], totals[6], totals[7], totals[8], totals[9], totals[10], totals[11], totals[12], totals[13], totals[14], totals[15], totals[16], totals[17])
```

```python
import functools

import jax
import jax.numpy as jnp
from jax import lax
from jax.experimental import pallas as pl
from jax.experimental.pallas import tpu as pltpu
from jax.sharding import PartitionSpec as P

HEAD_DIM = 64
EPSILON = 1e-06
F32 = jnp.float32
BF16 = jnp.bfloat16
LANES = 128
STEP = 96
QUERY = 112
KEYS = 128
CHUNK = 112
VMEM_LIMIT = 56 << 20


def dot(a, b, ca=1, cb=0):
    return lax.dot_general(a, b, (((ca,), (cb,)), ((), ())), preferred_element_type=F32)


def mean_row(v):
    return jnp.mean(v, axis=-1, keepdims=True)


def unit_rows(v):
    centred = v - mean_row(v)
    scale = lax.rsqrt(mean_row(centred * centred) + EPSILON)
    return centred * scale, scale


def norm_back(grad, unit, scale, gain):
    grad_unit = grad * gain
    return scale * (grad_unit - mean_row(grad_unit) - unit * mean_row(grad_unit * unit))


def fold(v):
    return jnp.sum(v.reshape(v.shape[0] // 8, 8, v.shape[1]), axis=0)


def total(v):
    return jnp.sum(v, axis=0, keepdims=True)


def gelu_pair(f):
    bell = jnp.exp(f * f * -0.5)
    t = 1.0 / (1.0 + 0.23164188 * jnp.abs(f))
    poly = t * (0.127414796 + t * (-0.142248368 + t * (0.7107068705 + t * (-0.7265760135 + t * 0.5307027145))))
    tail = poly * bell
    cdf = jnp.where(f >= 0.0, 1.0 - tail, tail)
    return f * cdf, cdf + f * bell * 0.3989422804014327


def rows_loop(rows, step):
    def go(c, carry):
        step(pl.ds(pl.multiple_of(c * CHUNK, 16), CHUNK))
        return carry

    lax.fori_loop(0, rows // CHUNK, go, 0)


def transposed(dst, src, rows):
    width = src.shape[1]
    dst[0:width, :] = src[0:rows, :].T
    dst[width:, :] = jnp.ones((16, rows), BF16)


def window(i):
    return pl.multiple_of(i * STEP, 32)


def head_masks():
    lane = lax.broadcasted_iota(jnp.int32, (KEYS, LANES), 1)
    return lane < HEAD_DIM


def split_pair(v, low):
    zero = jnp.zeros_like(v)
    return jnp.where(low, v, zero), jnp.where(low, zero, v)


def softmax_blocks(scores, i, vis, per_head):
    rows, width = scores.shape
    lane = lax.broadcasted_iota(jnp.int32, (rows, LANES), 1)
    row = lax.broadcasted_iota(jnp.int32, (rows, LANES), 0)
    low = 2 * i
    keys = (lane >= low) & (lane < low + vis)
    queries = (row >= low) & (row < low + vis)
    outs = []
    for h in range(2):
        blocks = []
        for b in range(per_head):
            at = (h * per_head + b) * LANES
            blocks.append(jnp.where(keys, scores[:, at : at + LANES], -1e30))
        top = functools.reduce(jnp.maximum, blocks)
        top = jnp.max(top, axis=-1, keepdims=True)
        blocks = [jnp.exp(b - top) for b in blocks]
        weight = 1.0 / jnp.sum(functools.reduce(jnp.add, blocks), axis=-1, keepdims=True)
        outs += [jnp.where(queries, b * weight, 0.0).astype(BF16) for b in blocks]
    return jnp.concatenate(outs, axis=1)


def put_window(ref, start, lanes, value):
    head = pl.ds(start, 16)
    ref[head, lanes] = ref[head, lanes] + value[:16]
    ref[pl.ds(start + 16, QUERY - 16), lanes] = value[16:QUERY]


def attend_back(chance, grad_out, value_stack, per_head):
    grad_chance = dot(grad_out, value_stack, 1, 1)
    p = chance.astype(F32)
    weighted = p * grad_chance
    outs = []
    for h in range(2):
        at = h * per_head * LANES
        parts = [weighted[:, at + b * LANES : at + (b + 1) * LANES] for b in range(per_head)]
        row = jnp.sum(functools.reduce(jnp.add, parts), axis=-1, keepdims=True)
        outs += [
            parts[b] - p[:, at + b * LANES : at + (b + 1) * LANES] * row for b in range(per_head)
        ]
    return jnp.concatenate(outs, axis=1).astype(BF16)


def join_columns(dst, own, other, count):
    half = own.shape[-1]
    for k in range(count):
        dst[:, 2 * half * k : 2 * half * (k + 1)] = jnp.concatenate([own[k], other[k]], axis=-1)


def head_bias_row(own, other):
    q = jnp.concatenate([own[0:1, :], other[0:1, :]], axis=-1)
    v = jnp.concatenate([own[1:2, :], other[1:2, :]], axis=-1)
    return q, v


def enc_attn_kernel(
    vis, tp, x_hbm, own_qkv, oth_qkv, own_proj, oth_proj, own_bias, oth_bias, gains, shifts,
    x1, act_t, qkv, chance, mixed, branch, weight,
    x_s, act_s, u_s, sem,
):
    rows, width = x1.shape
    images = rows // vis
    start = pl.multiple_of(tp[0] * rows, 16)
    copy = pltpu.make_async_copy(x_hbm.at[pl.ds(start, rows), :], x_s, sem)
    copy.start()
    join_columns(weight, own_qkv, oth_qkv, 3)
    copy.wait()

    def norm(at):
        unit, _ = unit_rows(x_s[at, :].astype(F32))
        act_s[at, :] = (unit * gains[0:1, :] + shifts[0:1, :]).astype(BF16)

    rows_loop(rows, norm)
    transposed(act_t, act_s, rows)
    bias_q, bias_v = head_bias_row(own_bias, oth_bias)
    qkv[rows:, :] = jnp.zeros((16, 3 * width), BF16)
    act = act_s[...]
    qkv[0:rows, 0:width] = ((dot(act, weight[:, 0:width]) + bias_q) * HEAD_DIM**-0.5).astype(BF16)
    qkv[0:rows, width : 2 * width] = dot(act, weight[:, width : 2 * width]).astype(BF16)
    qkv[0:rows, 2 * width :] = (dot(act, weight[:, 2 * width :]) + bias_v).astype(BF16)
    mixed[0:16, :] = jnp.zeros((16, width), BF16)
    low = head_masks()
    pairs = width // LANES

    def image(i, carry):
        at = window(i)
        for p in range(pairs):
            lanes = slice(p * LANES, (p + 1) * LANES)
            q = qkv[pl.ds(at, QUERY), lanes]
            k = qkv[pl.ds(at, KEYS), width + p * LANES : width + (p + 1) * LANES]
            v = qkv[pl.ds(at, KEYS), 2 * width + p * LANES : 2 * width + (p + 1) * LANES]
            scores = dot(q, jnp.concatenate(split_pair(k, low), axis=0), 1, 1)
            chosen = softmax_blocks(scores, i, vis, 1)
            chance[i * pairs + p] = chosen
            out = dot(chosen, jnp.concatenate(split_pair(v, low), axis=0)).astype(BF16)
            put_window(mixed, at, lanes, out)
        return carry

    lax.fori_loop(0, images, image, 0)
    half = own_proj.shape[0]
    u_s[...] = dot(mixed[:, 0:half], own_proj[...]) + dot(mixed[:, half:], oth_proj[...])

    def finish(at):
        u = u_s[at, :]
        branch[at, :] = u.astype(BF16)
        x1[at, :] = x_s[at, :].astype(F32) + gains[2:3, :] * (u + shifts[2:3, :])

    rows_loop(rows, finish)


def feed_forward(act_s, own_fc1, oth_fc1, own_b1, oth_b1, own_fc2, oth_fc2, hid, slope):
    half = own_fc1.shape[1]
    piece = 256

    def go(j, carry):
        at = pl.multiple_of(j * piece, piece)
        for w, b, base in ((own_fc1, own_b1, 0), (oth_fc1, oth_b1, half)):
            f = dot(act_s[...], w[:, pl.ds(at, piece)]) + b[:, pl.ds(at, piece)]
            h, g = gelu_pair(f)
            to = pl.ds(pl.multiple_of(base + at, piece), piece)
            hid[:, to] = h.astype(BF16)
            slope[:, to] = g.astype(BF16)
        return carry

    lax.fori_loop(0, half // piece, go, 0)
    return dot(hid[:, 0:half], own_fc2[...]) + dot(hid[:, half:], oth_fc2[...])


def feed_forward_back(
    d_low, act_t, own_fc1, oth_fc1, own_fc2, oth_fc2, hid, slope, d_before, own_out, oth_out, bias
):
    width, half = own_fc1.shape
    piece = 256
    for side, (w2, out) in enumerate(((own_fc2, own_out), (oth_fc2, oth_out))):
        base = side * half

        def go(j, carry, w2=w2, out=out, base=base):
            at = pl.multiple_of(j * piece, piece)
            cols = pl.ds(pl.multiple_of(base + at, piece), piece)
            grad_hid = dot(d_low[...], w2[pl.ds(at, piece), :], 1, 1)
            d_before[:, cols] = (grad_hid * slope[:, cols].astype(F32)).astype(BF16)
            out[pl.ds(pl.multiple_of(half + at, piece), piece), :] = dot(
                hid[:, cols], d_low[...], 0, 0
            ).astype(BF16)
            return carry

        lax.fori_loop(0, half // piece, go, 0)
        for c in range(half // width):
            cols = slice(base + c * width, base + (c + 1) * width)
            g = dot(act_t[...], d_before[:, cols])
            out[c * width : (c + 1) * width, :] = g[:width].astype(BF16)
            bias(side * (half // width) + c, g[width : width + 1])
    return dot(d_before[:, 0:half], own_fc1[...], 1, 1) + dot(d_before[:, half:], oth_fc1[...], 1, 1)


def enc_ffn_kernel(
    x1, own_fc1, oth_fc1, own_b1, oth_b1, own_fc2, oth_fc2, gains, shifts,
    state, encoded, act_t, hid, slope, branch,
    act_s, u_s,
):
    rows, width = x1.shape

    def norm(at):
        unit, _ = unit_rows(x1[at, :])
        act_s[at, :] = (unit * gains[1:2, :] + shifts[1:2, :]).astype(BF16)

    rows_loop(rows, norm)
    transposed(act_t, act_s, rows)
    u_s[...] = feed_forward(act_s, own_fc1, oth_fc1, own_b1, oth_b1, own_fc2, oth_fc2, hid, slope)

    def finish(at):
        u = u_s[at, :]
        branch[at, :] = u.astype(BF16)
        e = x1[at, :] + gains[3:4, :] * (u + shifts[3:4, :])
        state[at, :] = e
        encoded[at, :] = e.astype(BF16)

    rows_loop(rows, finish)


def one_hot(index, patches):
    lane = lax.broadcasted_iota(jnp.int32, (index.shape[0], patches), 1)
    return jnp.where(lane == index[...], 1.0, 0.0).astype(BF16)


def reg_attn_kernel(
    vis, state, seen, masked, pos, token, own_qkv, oth_qkv, own_proj, oth_proj, own_bias, oth_bias,
    gains, shifts,
    context, y1, act3_t, act4_t, query, kv, chance, mixed, branch, weight,
    act3_s, act4_s, u_s, picked,
):
    rows, width = state.shape
    images = rows // vis
    patches = pos.shape[0]
    high = pos[...].astype(BF16)
    rest = (pos[...] - high.astype(F32)).astype(BF16)
    table = jnp.concatenate([high, rest], axis=1)
    picked[0:rows, :] = dot(one_hot(seen, patches), table)
    picked[rows:, :] = dot(one_hot(masked, patches), table)
    join_columns(weight, own_qkv, oth_qkv, 3)

    def norm_seen(at):
        c = state[at, :] + picked[at, 0:width] + picked[at, width:]
        context[at, :] = c
        unit, _ = unit_rows(c)
        act4_s[at, :] = (unit * gains[1:2, :] + shifts[1:2, :]).astype(BF16)

    rows_loop(rows, norm_seen)

    def norm_masked(c, carry):
        at = pl.ds(pl.multiple_of(c * CHUNK, 16), CHUNK)
        below = pl.ds(pl.multiple_of(rows + c * CHUNK, 16), CHUNK)
        z = token[...] + (picked[below, 0:width] + picked[below, width:])
        context[below, :] = z
        unit, _ = unit_rows(z)
        act3_s[at, :] = (unit * gains[0:1, :] + shifts[0:1, :]).astype(BF16)
        act4_s[below, :] = (unit * gains[1:2, :] + shifts[1:2, :]).astype(BF16)
        return carry

    lax.fori_loop(0, rows // CHUNK, norm_masked, 0)
    transposed(act3_t, act3_s, rows)
    transposed(act4_t, act4_s, 2 * rows)
    bias_q, bias_v = head_bias_row(own_bias, oth_bias)
    query[...] = ((dot(act3_s[...], weight[:, 0:width]) + bias_q) * HEAD_DIM**-0.5).astype(BF16)
    kv[2 * rows :, :] = jnp.zeros((16, 2 * width), BF16)
    kv[0 : 2 * rows, 0:width] = dot(act4_s[...], weight[:, width : 2 * width]).astype(BF16)
    kv[0 : 2 * rows, width:] = (dot(act4_s[...], weight[:, 2 * width :]) + bias_v).astype(BF16)
    mixed[0:16, :] = jnp.zeros((16, width), BF16)
    low = head_masks()
    pairs = width // LANES

    def image(i, carry):
        at = window(i)
        below = pl.multiple_of(rows + at, 16)
        for p in range(pairs):
            lanes = slice(p * LANES, (p + 1) * LANES)
            more = slice(width + p * LANES, width + (p + 1) * LANES)
            q = query[pl.ds(at, QUERY), lanes]
            ks0, ks1 = split_pair(kv[pl.ds(at, KEYS), lanes], low)
            km0, km1 = split_pair(kv[pl.ds(below, KEYS), lanes], low)
            scores = dot(q, jnp.concatenate([ks0, km0, ks1, km1], axis=0), 1, 1)
            chosen = softmax_blocks(scores, i, vis, 2)
            chance[i * pairs + p] = chosen
            vs0, vs1 = split_pair(kv[pl.ds(at, KEYS), more], low)
            vm0, vm1 = split_pair(kv[pl.ds(below, KEYS), more], low)
            out = dot(chosen, jnp.concatenate([vs0, vm0, vs1, vm1], axis=0)).astype(BF16)
            put_window(mixed, at, lanes, out)
        return carry

    lax.fori_loop(0, images, image, 0)
    half = own_proj.shape[0]
    u_s[...] = dot(mixed[:, 0:half], own_proj[...]) + dot(mixed[:, half:], oth_proj[...])

    def finish(c, carry):
        at = pl.ds(pl.multiple_of(c * CHUNK, 16), CHUNK)
        below = pl.ds(pl.multiple_of(rows + c * CHUNK, 16), CHUNK)
        u = u_s[at, :]
        branch[at, :] = u.astype(BF16)
        y1[at, :] = context[below, :] + gains[3:4, :] * (u + shifts[3:4, :])
        return carry

    lax.fori_loop(0, rows // CHUNK, finish, 0)


def reg_ffn_kernel(
    tp, cot_hbm, y1, own_fc1, oth_fc1, own_b1, oth_b1, own_fc2, oth_fc2, gains, shifts,
    predicted, d_state, own_out, oth_out, small,
    act_s, act_t, hid, slope, d_before, u_s, cot_s, d_low, sums, sem,
):
    rows, width = y1.shape
    start = pl.multiple_of(tp[0] * rows, 16)
    copy = pltpu.make_async_copy(cot_hbm.at[pl.ds(start, rows), :], cot_s, sem)
    copy.start()
    sums[...] = jnp.zeros_like(sums)

    def norm(at):
        unit, _ = unit_rows(y1[at, :])
        act_s[at, :] = (unit * gains[2:3, :] + shifts[2:3, :]).astype(BF16)

    rows_loop(rows, norm)
    transposed(act_t, act_s, rows)
    u_s[...] = feed_forward(act_s, own_fc1, oth_fc1, own_b1, oth_b1, own_fc2, oth_fc2, hid, slope)
    copy.wait()

    def finish(at):
        branch = u_s[at, :] + shifts[4:5, :]
        predicted[at, :] = (y1[at, :] + gains[4:5, :] * branch).astype(BF16)
        grad = cot_s[at, :].astype(F32)
        sums[0:8, :] += fold(grad * branch)
        sums[8:16, :] += fold(grad)
        d_low[at, :] = (grad * gains[4:5, :]).astype(BF16)

    rows_loop(rows, finish)
    small[...] = jnp.zeros_like(small)

    def bias(k, row):
        small[8 + k : 9 + k, :] = row

    u_s[...] = feed_forward_back(
        d_low, act_t, own_fc1, oth_fc1, own_fc2, oth_fc2, hid, slope, d_before, own_out, oth_out, bias
    )

    def back(at):
        unit, scale = unit_rows(y1[at, :])
        grad = u_s[at, :]
        sums[16:24, :] += fold(grad * unit)
        sums[24:32, :] += fold(grad)
        d_state[at, :] = cot_s[at, :].astype(F32) + norm_back(grad, unit, scale, gains[2:3, :])

    rows_loop(rows, back)
    small[0:1, :] = total(sums[0:8, :])
    small[1:2, :] = total(sums[8:16, :]) * gains[4:5, :]
    small[2:3, :] = total(sums[16:24, :])
    small[3:4, :] = total(sums[24:32, :])


def pack_heads(grad, own_out, oth_out, at_q, at_v):
    width = grad.shape[0]
    half = width // 2
    for side, out in ((0, own_out), (1, oth_out)):
        lanes = slice(side * half, (side + 1) * half)
        q = grad[:, 0:width][:, lanes]
        k = grad[:, width : 2 * width][:, lanes]
        v = grad[:, 2 * width :][:, lanes]
        out[at_q : at_q + width, :] = jnp.concatenate([q, k], axis=1).astype(BF16)
        out[at_v : at_v + half, :] = jnp.concatenate([v[:half], v[half:]], axis=1).astype(BF16)


def pack_small(small, own_out, oth_out, bias_q, bias_v, ffn_small, at):
    width = small.shape[1]
    half = width // 2
    n_b1 = 2
    for side, out in ((0, own_out), (1, oth_out)):
        lanes = slice(side * half, (side + 1) * half)
        small[at : at + 1, :] = jnp.concatenate([bias_q[:, lanes], bias_v[:, lanes]], axis=1)
        small[at + 1 : at + 1 + n_b1, :] = ffn_small[8 + side * n_b1 : 8 + (side + 1) * n_b1, :]
        out[2 * width : 2 * width + small.shape[0], :] = small[...].astype(BF16)


def reg_attn_back_kernel(
    vis, patches, tp, cot_hbm, d_state, branch, mixed, query, kv, chance, weight, own_proj, oth_proj,
    context, act3_t, act4_t, seen, masked, gains, shifts, ffn_small,
    d_enc, own_out, oth_out,
    cot_s, d_low, d_mixed, d_query, d_kv, u_s, grads, sums, d_ctx, small, sem,
):
    rows, width = d_state.shape
    images = rows // vis
    start = pl.multiple_of(tp[0] * rows, 16)
    copy = pltpu.make_async_copy(cot_hbm.at[pl.ds(start, rows), :], cot_s, sem)
    copy.start()
    sums[...] = jnp.zeros_like(sums)

    def first(at):
        grad = d_state[at, :]
        sums[0:8, :] += fold(grad * (branch[at, :].astype(F32) + shifts[3:4, :]))
        sums[8:16, :] += fold(grad)
        d_low[at, :] = (grad * gains[3:4, :]).astype(BF16)

    rows_loop(rows, first)
    half = own_proj.shape[0]
    low_grad = d_low[...]
    own_out[width + half : 2 * width, :] = dot(mixed[:, 0:half], low_grad, 0, 0).astype(BF16)
    oth_out[width + half : 2 * width, :] = dot(mixed[:, half:], low_grad, 0, 0).astype(BF16)
    joined = jnp.concatenate([own_proj[...], oth_proj[...]], axis=0)
    d_mixed[...] = dot(low_grad, joined, 1, 1).astype(BF16)
    d_query[0:16, :] = jnp.zeros((16, width), BF16)
    d_kv[0:16, :] = jnp.zeros((16, 2 * width), BF16)
    d_kv[rows : rows + 16, :] = jnp.zeros((16, 2 * width), BF16)
    low = head_masks()
    low_q = low[:QUERY]
    pairs = width // LANES

    def image(i, carry):
        at = window(i)
        below = pl.multiple_of(rows + at, 16)
        for p in range(pairs):
            lanes = slice(p * LANES, (p + 1) * LANES)
            more = slice(width + p * LANES, width + (p + 1) * LANES)
            chosen = chance[i * pairs + p]
            grad_out = d_mixed[pl.ds(at, QUERY), lanes]
            vs0, vs1 = split_pair(kv[pl.ds(at, KEYS), more], low)
            vm0, vm1 = split_pair(kv[pl.ds(below, KEYS), more], low)
            d_score = attend_back(
                chosen, grad_out, jnp.concatenate([vs0, vm0, vs1, vm1], axis=0), 2
            )
            ks0, ks1 = split_pair(kv[pl.ds(at, KEYS), lanes], low)
            km0, km1 = split_pair(kv[pl.ds(below, KEYS), lanes], low)
            d_q = dot(d_score, jnp.concatenate([ks0, km0, ks1, km1], axis=0)) * HEAD_DIM**-0.5
            put_window(d_query, at, lanes, d_q.astype(BF16))
            d_k = dot(d_score, query[pl.ds(at, QUERY), lanes], 0, 0)
            d_v = dot(chosen, grad_out, 0, 0)
            for d, to in ((d_k, lanes), (d_v, more)):
                put_window(
                    d_kv, at, to, jnp.where(low_q, d[0:QUERY], d[2 * KEYS : 2 * KEYS + QUERY]).astype(BF16)
                )
                put_window(
                    d_kv, below, to,
                    jnp.where(low_q, d[KEYS : KEYS + QUERY], d[3 * KEYS : 3 * KEYS + QUERY]).astype(BF16),
                )
        return carry

    lax.fori_loop(0, images, image, 0)
    g = dot(act3_t[...], d_query[...])
    grads[:, 0:width] = g[:width]
    bias_q = g[width : width + 1]
    for c in range(2):
        g = dot(act4_t[...], d_kv[:, c * width : (c + 1) * width])
        grads[:, (c + 1) * width : (c + 2) * width] = g[:width]
        bias_v = g[width : width + 1]
    pack_heads(grads, own_out, oth_out, 0, width)
    u_s[0 : 2 * rows, :] = dot(d_kv[...], weight[:, width:], 1, 1)
    u_s[2 * rows :, :] = dot(d_query[...], weight[:, 0:width], 1, 1)
    copy.wait()

    def seen_rows(at):
        unit, scale = unit_rows(context[at, :])
        grad = u_s[at, :]
        sums[16:24, :] += fold(grad * unit)
        sums[24:32, :] += fold(grad)
        d_c = norm_back(grad, unit, scale, gains[1:2, :])
        high = d_c.astype(BF16)
        d_ctx[at, 0:width] = high
        d_ctx[at, width:] = (d_c - high.astype(F32)).astype(BF16)
        d_enc[at, :] = cot_s[at, :].astype(F32) + d_c

    rows_loop(rows, seen_rows)

    def masked_rows(c, carry):
        at = pl.ds(pl.multiple_of(c * CHUNK, 16), CHUNK)
        below = pl.ds(pl.multiple_of(rows + c * CHUNK, 16), CHUNK)
        last = pl.ds(pl.multiple_of(2 * rows + c * CHUNK, 16), CHUNK)
        unit, scale = unit_rows(context[below, :])
        grad4 = u_s[below, :]
        grad3 = u_s[last, :]
        sums[16:24, :] += fold(grad4 * unit)
        sums[24:32, :] += fold(grad4)
        sums[32:40, :] += fold(grad3 * unit)
        sums[40:48, :] += fold(grad3)
        d_z = d_state[at, :] + norm_back(
            grad3 * gains[0:1, :] + grad4 * gains[1:2, :], unit, scale, 1.0
        )
        sums[48:56, :] += fold(d_z)
        high = d_z.astype(BF16)
        d_ctx[below, 0:width] = high
        d_ctx[below, width:] = (d_z - high.astype(F32)).astype(BF16)
        return carry

    lax.fori_loop(0, rows // CHUNK, masked_rows, 0)
    pick = one_hot(seen, patches)
    both = dot(pick, d_ctx[0:rows, :], 0, 0)
    both = both + dot(one_hot(masked, patches), d_ctx[rows:, :], 0, 0)
    small[...] = jnp.zeros_like(small)
    small[0:1, :] = total(sums[32:40, :])
    small[1:2, :] = total(sums[16:24, :])
    small[2:3, :] = ffn_small[2:3, :]
    small[3:4, :] = total(sums[0:8, :])
    small[4:5, :] = ffn_small[0:1, :]
    small[5:6, :] = total(sums[40:48, :])
    small[6:7, :] = total(sums[24:32, :])
    small[7:8, :] = ffn_small[3:4, :]
    small[8:9, :] = total(sums[8:16, :]) * gains[3:4, :]
    small[9:10, :] = ffn_small[1:2, :]
    small[10:11, :] = total(sums[48:56, :])
    pack_small(small, own_out, oth_out, bias_q, bias_v, ffn_small, 11)
    after = 2 * width + 32
    d_pos = (both[:, 0:width] + both[:, width:]).astype(BF16)
    pad = jnp.zeros((own_out.shape[0] - after - patches, width), BF16)
    for out in (own_out, oth_out):
        out[after:, :] = jnp.concatenate([d_pos, pad], axis=0)


def enc_ffn_back_kernel(
    d_enc, x1, branch, act_t, hid, slope, own_fc1, oth_fc1, own_fc2, oth_fc2, gains, shifts,
    d_state, own_out, oth_out, small,
    d_low, d_before, u_s, sums,
):
    rows, width = d_enc.shape
    sums[...] = jnp.zeros_like(sums)

    def first(at):
        grad = d_enc[at, :]
        sums[0:8, :] += fold(grad * (branch[at, :].astype(F32) + shifts[3:4, :]))
        sums[8:16, :] += fold(grad)
        d_low[at, :] = (grad * gains[3:4, :]).astype(BF16)

    rows_loop(rows, first)
    small[...] = jnp.zeros_like(small)

    def bias(k, row):
        small[8 + k : 9 + k, :] = row

    u_s[...] = feed_forward_back(
        d_low, act_t, own_fc1, oth_fc1, own_fc2, oth_fc2, hid, slope, d_before, own_out, oth_out, bias
    )

    def back(at):
        unit, scale = unit_rows(x1[at, :])
        grad = u_s[at, :]
        sums[16:24, :] += fold(grad * unit)
        sums[24:32, :] += fold(grad)
        d_state[at, :] = d_enc[at, :] + norm_back(grad, unit, scale, gains[1:2, :])

    rows_loop(rows, back)
    small[0:1, :] = total(sums[0:8, :])
    small[1:2, :] = total(sums[8:16, :]) * gains[3:4, :]
    small[2:3, :] = total(sums[16:24, :])
    small[3:4, :] = total(sums[24:32, :])


def enc_attn_back_kernel(
    vis, tp, x_hbm, d_state, branch, mixed, qkv, chance, weight, own_proj, oth_proj, act_t, gains,
    shifts, ffn_small,
    own_out, oth_out, d_input,
    x_s, u_s, d_qkv, d_low, d_mixed, grads, sums, small, sem,
):
    rows, width = d_state.shape
    images = rows // vis
    start = pl.multiple_of(tp[0] * rows, 16)
    copy = pltpu.make_async_copy(x_hbm.at[pl.ds(start, rows), :], x_s, sem)
    copy.start()
    sums[...] = jnp.zeros_like(sums)

    def first(at):
        grad = d_state[at, :]
        sums[0:8, :] += fold(grad * (branch[at, :].astype(F32) + shifts[2:3, :]))
        sums[8:16, :] += fold(grad)
        d_low[at, :] = (grad * gains[2:3, :]).astype(BF16)

    rows_loop(rows, first)
    half = own_proj.shape[0]
    low_grad = d_low[...]
    own_out[width + half : 2 * width, :] = dot(mixed[:, 0:half], low_grad, 0, 0).astype(BF16)
    oth_out[width + half : 2 * width, :] = dot(mixed[:, half:], low_grad, 0, 0).astype(BF16)
    joined = jnp.concatenate([own_proj[...], oth_proj[...]], axis=0)
    d_mixed[...] = dot(low_grad, joined, 1, 1).astype(BF16)
    d_qkv[0:16, :] = jnp.zeros((16, 3 * width), BF16)
    low = head_masks()
    low_q = low[:QUERY]
    pairs = width // LANES

    def image(i, carry):
        at = window(i)
        for p in range(pairs):
            lanes = slice(p * LANES, (p + 1) * LANES)
            key = slice(width + p * LANES, width + (p + 1) * LANES)
            value = slice(2 * width + p * LANES, 2 * width + (p + 1) * LANES)
            chosen = chance[i * pairs + p]
            grad_out = d_mixed[pl.ds(at, QUERY), lanes]
            v_stack = jnp.concatenate(split_pair(qkv[pl.ds(at, KEYS), value], low), axis=0)
            d_score = attend_back(chosen, grad_out, v_stack, 1)
            k_stack = jnp.concatenate(split_pair(qkv[pl.ds(at, KEYS), key], low), axis=0)
            put_window(d_qkv, at, lanes, (dot(d_score, k_stack) * HEAD_DIM**-0.5).astype(BF16))
            d_k = dot(d_score, qkv[pl.ds(at, QUERY), lanes], 0, 0)
            d_v = dot(chosen, grad_out, 0, 0)
            for d, to in ((d_k, key), (d_v, value)):
                put_window(
                    d_qkv, at, to, jnp.where(low_q, d[0:QUERY], d[KEYS : KEYS + QUERY]).astype(BF16)
                )
        return carry

    lax.fori_loop(0, images, image, 0)
    biases = []
    for c in range(3):
        g = dot(act_t[...], d_qkv[:, c * width : (c + 1) * width])
        grads[:, c * width : (c + 1) * width] = g[:width]
        biases.append(g[width : width + 1])
    pack_heads(grads, own_out, oth_out, 0, width)
    u_s[...] = dot(d_qkv[...], weight[...], 1, 1)
    copy.wait()

    def back(at):
        unit, scale = unit_rows(x_s[at, :].astype(F32))
        grad = u_s[at, :]
        sums[16:24, :] += fold(grad * unit)
        sums[24:32, :] += fold(grad)
        d_input[at, :] = d_state[at, :] + norm_back(grad, unit, scale, gains[0:1, :])

    rows_loop(rows, back)
    small[...] = jnp.zeros_like(small)
    small[0:1, :] = total(sums[16:24, :])
    small[1:2, :] = ffn_small[2:3, :]
    small[2:3, :] = total(sums[0:8, :])
    small[3:4, :] = ffn_small[0:1, :]
    small[4:5, :] = total(sums[24:32, :])
    small[5:6, :] = ffn_small[3:4, :]
    small[6:7, :] = total(sums[8:16, :]) * gains[2:3, :]
    small[7:8, :] = ffn_small[1:2, :]
    pack_small(small, own_out, oth_out, biases[0], biases[2], ffn_small, 8)
    pad = jnp.zeros((own_out.shape[0] - 2 * width - small.shape[0], width), BF16)
    own_out[2 * width + small.shape[0] :, :] = pad
    oth_out[2 * width + small.shape[0] :, :] = pad


def halve_kernel(step, place, mine, got, keep, send):
    half = keep.shape[0]
    bit = place[step]
    at = pl.ds(pl.multiple_of(bit * half, 16), half)
    to = pl.ds(pl.multiple_of((1 - bit) * half, 16), half)
    keep[...] = (mine[at, :].astype(F32) + got[at, :].astype(F32)).astype(BF16)
    send[...] = (mine[to, :].astype(F32) + got[to, :].astype(F32)).astype(BF16)


def add_kernel(mine, got, out):
    out[...] = (mine[...].astype(F32) + got[...].astype(F32)).astype(BF16)


def join_kernel(step, place, mine, got, out):
    half = mine.shape[0]
    bit = place[step]
    out[pl.ds(pl.multiple_of(bit * half, 16), half), :] = mine[...]
    out[pl.ds(pl.multiple_of((1 - bit) * half, 16), half), :] = got[...]


def ffn_out_kernel(place, mine, got, grad1, grad2):
    width = grad1.shape[0]

    def write(first, second):
        for c in range(grad1.shape[1] // width):
            grad1[:, c * width : (c + 1) * width] = first[c * width : (c + 1) * width, :].astype(F32)
        grad2[...] = second[...].astype(F32)

    @pl.when(place[1] == 0)
    def _():
        write(mine, got)

    @pl.when(place[1] == 1)
    def _():
        write(got, mine)


def heads_out_kernel(place, mine, got, grad_qkv, grad_proj, rest, whole):
    join_kernel(1, place, mine, got, whole)
    width = grad_qkv.shape[1]
    half = width // 2
    first = whole[0:width, :].astype(F32)
    grad_qkv[0] = first[:, :half]
    grad_qkv[1] = first[:, half:]
    value = whole[width : width + half, :].astype(F32)
    grad_qkv[2, 0:half, :] = value[:, :half]
    grad_qkv[2, half:, :] = value[:, half:]
    grad_proj[...] = whole[width + half : 2 * width, :].astype(F32)
    rest[...] = whole[2 * width :, :].astype(F32)


def run(kernel, name, ins, outs, scratch, flops, hbm=(), smem=()):
    specs = []
    for k in range(len(ins)):
        if k in smem:
            specs.append(pl.BlockSpec(memory_space=pltpu.SMEM))
        elif k in hbm:
            specs.append(pl.BlockSpec(memory_space=pl.ANY))
        else:
            specs.append(pl.BlockSpec(memory_space=pltpu.VMEM))
    shapes = [jax.ShapeDtypeStruct(s, d) for s, d in outs]
    moved = sum(a.size * a.dtype.itemsize for a in (*ins, *shapes))
    return pl.pallas_call(
        kernel,
        name=name,
        out_shape=shapes,
        in_specs=specs,
        out_specs=[pl.BlockSpec(memory_space=pltpu.VMEM)] * len(outs),
        scratch_shapes=scratch,
        compiler_params=pltpu.CompilerParams(vmem_limit_bytes=VMEM_LIMIT),
        cost_estimate=pl.CostEstimate(flops=flops, bytes_accessed=moved, transcendentals=0),
    )(*ins)


def vmem(shape, dtype):
    return pltpu.VMEM(shape, dtype)


def swap(a):
    return lax.ppermute(a, "tp", [(0, 1), (1, 0)])


AXES = ("dp", "tp")
ORDERS = ((0, 1, 2, 3), (1, 0, 3, 2))


def flip(a, step):
    n = lax.axis_size("dp")
    pairs = [
        (2 * d + t, 2 * (d ^ (1 << ORDERS[t][step])) + t) for d in range(n) for t in range(2)
    ]
    return lax.ppermute(a, AXES, pairs)


def halve(place, step, mine, got):
    shape = ((mine.shape[0] // 2, mine.shape[1]), BF16)
    return run(functools.partial(halve_kernel, step), "halve", (place, mine, got), [shape, shape], [], 0, smem=(0,))


def add(mine, got):
    return run(add_kernel, "add", (mine, got), [(mine.shape, BF16)], [], 0)[0]


def join(place, step, mine, got):
    shape = ((2 * mine.shape[0], mine.shape[1]), BF16)
    return run(functools.partial(join_kernel, step), "join", (place, mine, got), [shape], [], 0, smem=(0,))[0]


def reduce_over_dp(place, own, oth):
    if lax.axis_size("dp") != 16:
        whole = lax.psum(own.astype(F32) + swap(oth).astype(F32), "dp").astype(BF16)
        half = whole.shape[0] // 2
        first = place[1] == 0
        return (
            jnp.where(first, whole[:half], whole[half:]),
            jnp.where(first, whole[half:], whole[:half]),
        )
    keep, send = halve(place, 1, own, swap(oth))
    keep, send = halve(place, 2, keep, flip(send, 0))
    part = add(keep, flip(send, 1))
    part = add(part, flip(part, 2))
    part = add(part, flip(part, 3))
    part = join(place, 2, part, flip(part, 1))
    return part, flip(part, 0)


def body(
    x_visible,
    patch_order,
    enc_qkv,
    enc_head_bias,
    enc_proj,
    enc_fc1,
    enc_fc1_bias,
    enc_fc2,
    enc_gains,
    enc_shifts,
    reg_qkv,
    reg_head_bias,
    reg_proj,
    reg_fc1,
    reg_fc1_bias,
    reg_fc2,
    reg_gains,
    reg_shifts,
    pos_embed,
    mask_token,
    enc_cot,
    reg_cot,
):
    all_images, patches = patch_order.shape
    width = x_visible.shape[1]
    vis = x_visible.shape[0] // all_images
    images = all_images // 2
    rows = images * vis
    hidden = 2 * enc_fc1.shape[1]
    half = width // 2
    pairs = width // LANES
    tp_index = lax.axis_index("tp")
    tp = tp_index.astype(jnp.int32).reshape(1)
    dp_index = lax.axis_index("dp")
    bits = [(dp_index >> jnp.where(tp_index == 0, *(o[k] for o in ORDERS))) & 1 for k in range(2)]
    place = jnp.stack([tp_index, *bits]).astype(jnp.int32)

    enc_b1 = enc_fc1_bias.reshape(1, -1)
    reg_b1 = reg_fc1_bias.reshape(1, -1)
    oth_enc_qkv, oth_enc_proj, oth_enc_bias = swap(enc_qkv), swap(enc_proj), swap(enc_head_bias)
    oth_enc_fc1, oth_enc_fc2, oth_enc_b1 = swap(enc_fc1), swap(enc_fc2), swap(enc_b1)
    oth_reg_qkv, oth_reg_proj, oth_reg_bias = swap(reg_qkv), swap(reg_proj), swap(reg_head_bias)
    oth_reg_fc1, oth_reg_fc2, oth_reg_b1 = swap(reg_fc1), swap(reg_fc2), swap(reg_b1)
    order = lax.dynamic_slice_in_dim(patch_order, tp_index * images, images, 0)
    seen = order[:, :vis].reshape(rows, 1)
    masked = order[:, vis:].reshape(rows, 1)

    state_f = ((rows, width), F32)
    state_b = ((rows, width), BF16)
    act_t = ((width + 16, rows), BF16)
    wide = ((rows, hidden), BF16)
    layer = 2 * rows * width

    x1, act1_t, qkv1, chance1, mixed1, branch1, weight1 = run(
        functools.partial(enc_attn_kernel, vis),
        "enc_attn",
        (tp, x_visible, enc_qkv, oth_enc_qkv, enc_proj, oth_enc_proj, enc_head_bias, oth_enc_bias,
         enc_gains, enc_shifts),
        [state_f, act_t, ((rows + 16, 3 * width), BF16), ((images * pairs, QUERY, 2 * KEYS), BF16),
         state_b, state_b, ((width, 3 * width), BF16)],
        [vmem(*state_b), vmem(*state_b), vmem(*state_f), pltpu.SemaphoreType.DMA],
        layer * width * 5, hbm=(1,), smem=(0,),
    )
    enc_state, encoded, act2_t, hid2, slope2, branch2 = run(
        enc_ffn_kernel,
        "enc_ffn",
        (x1, enc_fc1, oth_enc_fc1, enc_b1, oth_enc_b1, enc_fc2, oth_enc_fc2, enc_gains, enc_shifts),
        [state_f, state_b, act_t, wide, wide, state_b],
        [vmem(*state_b), vmem(*state_f)],
        layer * hidden * 2,
    )
    context, y1, act3_t, act4_t, query3, kv3, chance3, mixed3, branch3, weight3 = run(
        functools.partial(reg_attn_kernel, vis),
        "reg_attn",
        (enc_state, seen, masked, pos_embed, mask_token.reshape(1, width), reg_qkv, oth_reg_qkv,
         reg_proj, oth_reg_proj, reg_head_bias, oth_reg_bias, reg_gains, reg_shifts),
        [((2 * rows, width), F32), state_f, act_t, ((width + 16, 2 * rows), BF16), state_b,
         ((2 * rows + 16, 2 * width), BF16), ((images * pairs, QUERY, 4 * KEYS), BF16), state_b,
         state_b, ((width, 3 * width), BF16)],
        [vmem(*state_b), vmem((2 * rows, width), BF16), vmem(*state_f),
         vmem((2 * rows, 2 * width), F32)],
        layer * width * 8,
    )
    stage = ((2 * hidden // 2, width), BF16)
    predicted, d_state3, own_a, oth_a, small_a = run(
        reg_ffn_kernel,
        "reg_ffn_both",
        (tp, reg_cot, y1, reg_fc1, oth_reg_fc1, reg_b1, oth_reg_b1, reg_fc2, oth_reg_fc2, reg_gains,
         reg_shifts),
        [state_b, state_f, stage, stage, ((16, width), F32)],
        [vmem(*state_b), vmem(*act_t), vmem(*wide), vmem(*wide), vmem(*wide), vmem(*state_f),
         vmem(*state_b), vmem(*state_b), vmem((32, width), F32), pltpu.SemaphoreType.DMA],
        layer * hidden * 6, hbm=(1,), smem=(0,),
    )
    heads_b = ((2 * width + 256, width), BF16)
    d_enc, own_b, oth_b = run(
        functools.partial(reg_attn_back_kernel, vis, patches),
        "reg_attn_back",
        (tp, enc_cot, d_state3, branch3, mixed3, query3, kv3, chance3, weight3, reg_proj,
         oth_reg_proj, context, act3_t, act4_t, seen, masked, reg_gains, reg_shifts, small_a),
        [state_f, heads_b, heads_b],
        [vmem(*state_b), vmem(*state_b), vmem(*state_b), vmem(*state_b),
         vmem((2 * rows, 2 * width), BF16), vmem((3 * rows, width), F32),
         vmem((width, 3 * width), F32), vmem((56, width), F32), vmem((2 * rows, 2 * width), BF16),
         vmem((32, width), F32), pltpu.SemaphoreType.DMA],
        layer * width * 16, hbm=(1,), smem=(0,),
    )
    d_state1, own_c, oth_c, small_c = run(
        enc_ffn_back_kernel,
        "enc_ffn_back",
        (d_enc, x1, branch2, act2_t, hid2, slope2, enc_fc1, oth_enc_fc1, enc_fc2, oth_enc_fc2,
         enc_gains, enc_shifts),
        [state_f, stage, stage, ((16, width), F32)],
        [vmem(*state_b), vmem(*wide), vmem(*state_f), vmem((32, width), F32)],
        layer * hidden * 4,
    )
    heads_d = ((2 * width + 64, width), BF16)
    own_d, oth_d, d_input = run(
        functools.partial(enc_attn_back_kernel, vis),
        "enc_attn_back",
        (tp, x_visible, d_state1, branch1, mixed1, qkv1, chance1, weight1, enc_proj, oth_enc_proj,
         act1_t, enc_gains, enc_shifts, small_c),
        [heads_d, heads_d, state_f],
        [vmem(*state_b), vmem(*state_f), vmem((rows, 3 * width), BF16), vmem(*state_b),
         vmem(*state_b), vmem((width, 3 * width), F32), vmem((32, width), F32),
         vmem((32, width), F32), pltpu.SemaphoreType.DMA],
        layer * width * 12, hbm=(1,), smem=(0,),
    )

    def both_halves(mine):
        theirs = swap(mine)
        return jnp.where(
            tp_index == 0,
            jnp.concatenate([mine, theirs], axis=0),
            jnp.concatenate([theirs, mine], axis=0),
        )

    encoded, predicted, d_input = both_halves(encoded), both_halves(predicted), both_halves(d_input)

    fc_shapes = [((width, hidden // 2), F32), ((hidden // 2, width), F32)]
    reg_g1, reg_g2 = run(
        ffn_out_kernel, "ffn_out", (place, *reduce_over_dp(place, own_a, oth_a)), fc_shapes, [], 0, smem=(0,)
    )
    enc_g1, enc_g2 = run(
        ffn_out_kernel, "ffn_out", (place, *reduce_over_dp(place, own_c, oth_c)), fc_shapes, [], 0, smem=(0,)
    )

    def heads_out(own, oth):
        shapes = [((3, width, half), F32), ((half, width), F32), ((own.shape[0] - 2 * width, width), F32)]
        grad_qkv, grad_proj, rest = run(
            heads_out_kernel, "heads_out", (place, *reduce_over_dp(place, own, oth)), shapes,
            [vmem(own.shape, BF16)], 0, smem=(0,),
        )
        return grad_qkv, grad_proj, rest, (rest + swap(rest)) * 0.5

    reg_gq, reg_gp, rest, mean = heads_out(own_b, oth_b)
    n_b1 = hidden // (2 * width)
    grad_reg_gains, grad_reg_shifts, grad_mask_token = mean[0:5], mean[5:10], mean[10]
    hb_reg = rest[11].reshape(2, half)
    b1_reg = rest[12 : 12 + n_b1].reshape(-1)
    grad_pos = mean[32 : 32 + patches]
    enc_gq, enc_gp, rest, mean = heads_out(own_d, oth_d)
    grad_enc_gains, grad_enc_shifts = mean[0:4], mean[4:8]
    hb_enc = rest[8].reshape(2, half)
    b1_enc = rest[9 : 9 + n_b1].reshape(-1)
    return (
        encoded, predicted, d_input, enc_gq, hb_enc, enc_gp, enc_g1, b1_enc, enc_g2, grad_enc_gains,
        grad_enc_shifts, reg_gq, hb_reg, reg_gp, reg_g1, b1_reg, reg_g2, grad_reg_gains,
        grad_reg_shifts, grad_pos, grad_mask_token,
    )


def solution(mesh):
    placed = (
        P("dp", None),
        P("dp", None),
        P(None, None, "tp"),
        P(None, "tp"),
        P("tp", None),
        P(None, "tp"),
        P("tp"),
        P("tp", None),
        P(),
        P(),
        P(None, None, "tp"),
        P(None, "tp"),
        P("tp", None),
        P(None, "tp"),
        P("tp"),
        P("tp", None),
        P(),
        P(),
        P(),
        P(),
        P("dp", None),
        P("dp", None),
    )
    return jax.shard_map(
        body,
        mesh=mesh,
        in_specs=placed,
        out_specs=(
            P("dp", None),
            P("dp", None),
            P("dp", None),
            P(None, None, "tp"),
            P(None, "tp"),
            P("tp", None),
            P(None, "tp"),
            P("tp"),
            P("tp", None),
            P(),
            P(),
            P(None, None, "tp"),
            P(None, "tp"),
            P("tp", None),
            P(None, "tp"),
            P("tp"),
            P("tp", None),
            P(),
            P(),
            P(),
            P(),
        ),
        check_vma=False,
    )
```

```python
import functools

import jax
import jax.numpy as jnp
from jax import lax
from jax.experimental import pallas as pl
from jax.experimental.pallas import tpu as pltpu
from jax.sharding import PartitionSpec as P

HEAD_DIM = 64
EPSILON = 1e-06
F32 = jnp.float32
BF16 = jnp.bfloat16
LANES = 128
STEP = 96
QUERY = 112
KEYS = 128
GROUP = 8
VMEM_LIMIT = 60 << 20


def dot(a, b, ca=1, cb=0):
    return lax.dot_general(a, b, (((ca,), (cb,)), ((), ())), preferred_element_type=F32)


def mean_row(v):
    return jnp.mean(v, axis=-1, keepdims=True)


def unit_rows(v):
    centred = v - mean_row(v)
    scale = lax.rsqrt(mean_row(centred * centred) + EPSILON)
    return centred * scale, scale


def norm_back(grad_unit, unit, scale):
    return scale * (grad_unit - mean_row(grad_unit) - unit * mean_row(grad_unit * unit))


def total(v):
    return jnp.sum(jnp.sum(v.reshape(v.shape[0] // 8, 8, v.shape[1]), axis=0), axis=0, keepdims=True)


def gelu_pair(f):
    cdf = 0.5 + 0.5 * lax.erf(f * 0.7071067811865476)
    bell = jnp.exp(f * f * -0.5) * 0.3989422804014327
    return f * cdf, cdf + f * bell


def window(i):
    return i * STEP if isinstance(i, int) else pl.multiple_of(i * STEP, 32)


def aligned(at):
    return at if isinstance(at, int) else pl.multiple_of(at, 16)


def low_lanes():
    return lax.broadcasted_iota(jnp.int32, (KEYS, LANES), 1) < HEAD_DIM


def split_pair(v, low):
    zero = jnp.zeros_like(v)
    return jnp.where(low, v, zero), jnp.where(low, zero, v)


def stack_heads(blocks, low):
    pairs = [split_pair(b, low) for b in blocks]
    return jnp.concatenate([p[0] for p in pairs] + [p[1] for p in pairs], axis=0)


def same_head():
    shape = (2 * LANES, 2 * LANES)
    row = lax.broadcasted_iota(jnp.int32, shape, 0) < LANES
    lane = lax.broadcasted_iota(jnp.int32, shape, 1) < LANES
    return jnp.where(row == lane, 1.0, 0.0).astype(BF16)


def blocks_of(v):
    return [v[:, b : b + LANES] for b in range(0, v.shape[1], LANES)]


def head_sums(blocks, ones):
    n = len(blocks) // 2
    sides = [functools.reduce(jnp.add, blocks[h * n : (h + 1) * n]) for h in range(2)]
    s = dot(jnp.concatenate(sides, axis=1).astype(BF16), ones)
    return [s[:, :LANES]] * n + [s[:, LANES:]] * n


def softmax(scores, keys, queries, ones):
    blocks = [jnp.where(keys, b, -1e30) for b in blocks_of(scores)]
    n = len(blocks) // 2
    tops = []
    for h in range(2):
        top = functools.reduce(jnp.maximum, blocks[h * n : (h + 1) * n])
        tops += [jnp.max(top, axis=-1, keepdims=True)] * n
    blocks = [jnp.exp(b - t) for b, t in zip(blocks, tops)]
    sums = head_sums(blocks, ones)
    weights = [1.0 / sums[0]] * n + [1.0 / sums[n]] * n
    out = [jnp.where(queries, b * w, 0.0).astype(BF16) for b, w in zip(blocks, weights)]
    return jnp.concatenate(out, axis=1)


def put_window(ref, start, lanes, value):
    head = pl.ds(start, 16)
    ref[head, lanes] = ref[head, lanes] + value[:16]
    ref[pl.ds(start + 16, QUERY - 16), lanes] = value[16:QUERY]


def pair_lanes(part, p, width):
    return slice(part * width + p * LANES, part * width + (p + 1) * LANES)


def loop_groups(count, group):
    if count == 1:
        group(0, 0)
    else:
        lax.fori_loop(0, count, group, 0)


def attend(images, vis, query, key, value, chance, mixed):
    width = mixed.shape[1]
    pairs = width // LANES
    low = low_lanes()
    ones = same_head()
    lane = lax.broadcasted_iota(jnp.int32, (QUERY, LANES), 1)
    row = lax.broadcasted_iota(jnp.int32, (QUERY, LANES), 0)
    mixed[0:16, :] = jnp.zeros((16, width), BF16)

    def group(g, carry):
        units = [(g * GROUP + n, p) for n in range(GROUP) for p in range(pairs)]
        scores = [dot(query(window(i), p), stack_heads(key(window(i), p), low), 1, 1) for i, p in units]
        chosen = []
        for (i, p), s in zip(units, scores):
            keys = (lane >= 2 * i) & (lane < 2 * i + vis)
            queries = (row >= 2 * i) & (row < 2 * i + vis)
            chosen.append(softmax(s, keys, queries, ones))
        outs = [dot(c, stack_heads(value(window(i), p), low)).astype(BF16) for (i, p), c in zip(units, chosen)]
        for (i, p), c, o in zip(units, chosen, outs):
            chance[i * pairs + p] = c
            put_window(mixed, window(i), pair_lanes(0, p, width), o)
        return carry

    loop_groups(images // GROUP, group)


def attend_back(images, query, key, value, chance, d_mixed, put_query, put_key, put_value, group_size):
    width = d_mixed.shape[1]
    pairs = width // LANES
    low = low_lanes()
    low_q = low[:QUERY]
    ones = same_head()

    def merge(stack):
        n = stack.shape[0] // (2 * KEYS)
        return [
            jnp.where(
                low_q, stack[b * KEYS : b * KEYS + QUERY], stack[(n + b) * KEYS : (n + b) * KEYS + QUERY]
            ).astype(BF16)
            for b in range(n)
        ]

    def group(g, carry):
        units = [(g * group_size + n, p) for n in range(group_size) for p in range(pairs)]
        d_chance, d_value = [], []
        for i, p in units:
            grad = d_mixed[pl.ds(window(i), QUERY), pair_lanes(0, p, width)]
            d_chance.append(dot(grad, stack_heads(value(window(i), p), low), 1, 1))
            d_value.append(dot(chance[i * pairs + p], grad, 0, 0))
        d_score = []
        for (i, p), d in zip(units, d_chance):
            c = blocks_of(chance[i * pairs + p].astype(F32))
            t = [x * y for x, y in zip(c, blocks_of(d))]
            sums = head_sums(t, ones)
            d_score.append(jnp.concatenate([a - b * s for a, b, s in zip(t, c, sums)], axis=1).astype(BF16))
        d_query, d_key = [], []
        for (i, p), d in zip(units, d_score):
            at = window(i)
            d_query.append((dot(d, stack_heads(key(at, p), low)) * HEAD_DIM**-0.5).astype(BF16))
            d_key.append(dot(d, query(at, p), 0, 0))
        for (i, p), q, k, v in zip(units, d_query, d_key, d_value):
            at = window(i)
            put_query(at, p, q)
            put_key(at, p, merge(k))
            put_value(at, p, merge(v))
        return carry

    loop_groups(images // group_size, group)


def feed_forward(act, first, bias, second, hid, slope):
    out = None
    for side in range(2):
        half = first[side].shape[1]
        to = slice(side * half, (side + 1) * half)
        h, g = gelu_pair(dot(act[...], first[side][...]) + bias[side][...].reshape(1, half))
        h = h.astype(BF16)
        hid[:, to] = h
        slope[:, to] = g.astype(BF16)
        part = dot(h, second[side][...])
        out = part if out is None else out + part
    return out


def feed_forward_slopes(d_low, second, slope, d_before):
    half = second[0].shape[0]
    for side in range(2):
        to = slice(side * half, (side + 1) * half)
        grad = dot(d_low[...], second[side][...], 1, 1)
        d_before[:, to] = (grad * slope[:, to].astype(F32)).astype(BF16)


def feed_forward_back(d_low, act_t, first, hid, d_before, outs, bias):
    width, half = first[0].shape
    grad = dot(d_before[:, 0:half], first[0][...], 1, 1) + dot(d_before[:, half:], first[1][...], 1, 1)
    for side in range(2):
        to = slice(side * half, (side + 1) * half)
        outs[side][half:, :] = dot(hid[:, to], d_low[...], 0, 0).astype(BF16)
        g = dot(act_t[...], d_before[:, to])
        for c in range(half // width):
            cols = slice(c * width, (c + 1) * width)
            outs[side][cols, :] = g[:width, cols].astype(BF16)
            bias(side * (half // width) + c, g[width : width + 1, cols])
    return grad


def transposed(act):
    return jnp.concatenate([act.T, jnp.ones((16, act.shape[0]), BF16)], axis=0)


class Load:
    def __init__(self, src, ref, sem):
        self.copy, self.ref, self.pending = pltpu.make_async_copy(src, ref, sem), ref, True
        self.copy.start()

    def __call__(self):
        if self.pending:
            self.pending = False
            self.copy.wait()
        return self.ref


class Store:
    def __init__(self, dst, ref, sems):
        self.ref, self.sent = ref, False
        rows = ref.shape[0] // len(dst)
        self.copies = [
            pltpu.make_async_copy(ref if len(dst) == 1 else ref.at[pl.ds(k * rows, rows), :], to, sem)
            for k, (to, sem) in enumerate(zip(dst, sems))
        ]

    def send(self):
        self.sent = True
        for copy in self.copies:
            copy.start()

    def wait(self):
        for copy in self.copies:
            copy.wait()


def run(kernel, name, ins, outs, scratch, flops=0, after=(), limit=VMEM_LIMIT):
    arrays, specs, extra, copies = [], [], [], 0
    near = pl.BlockSpec(memory_space=pl.ANY)
    far = pl.BlockSpec(memory_space=pltpu.HBM)
    if limit == VMEM_LIMIT:
        near = far
    for kind, *given in ins:
        if kind == "heads":
            arrays += given
            specs += [near] * 2
            own = given[0]
            lead = own.shape[0] if own.ndim == 3 else 1
            extra.append(pltpu.VMEM((2 * lead * own.shape[-2], own.shape[-1]), own.dtype))
            copies += 2 * lead
        elif kind == "parts":
            arrays += given
            specs += [near] * len(given)
            count = sum(a.shape[0] for a in given)
            extra.append(pltpu.VMEM((count, given[0].shape[1]), given[0].dtype))
            copies += len(given)
        elif kind == "rows":
            arrays.append(given[0])
            specs.append(far)
            extra.append(pltpu.VMEM((given[0].shape[0] // 2, given[0].shape[1]), given[0].dtype))
            copies += 1
        elif kind in ("load", "far"):
            arrays.append(given[0])
            specs.append(near if kind == "load" else far)
            extra.append(pltpu.VMEM(given[0].shape, given[0].dtype))
            copies += 1
        else:
            arrays.append(given[0])
            specs.append(far if kind == "hbm" else pl.BlockSpec(memory_space=pltpu.VMEM))
    arrays += after
    specs += [pl.BlockSpec(memory_space=pltpu.VMEM)] * len(after)
    shapes, splits = [], []
    for shape, dtype, *more in outs:
        split = (more or [1])[0]
        splits.append(split)
        if split == "hbm":
            shapes.append(jax.ShapeDtypeStruct(shape, dtype))
            continue
        shapes += [jax.ShapeDtypeStruct((shape[0] // split, *shape[1:]), dtype)] * split
        extra.append(pltpu.VMEM(shape, dtype))
        copies += split
    out_specs = [pl.BlockSpec(memory_space=pl.ANY)] * len(shapes) + [pl.BlockSpec(memory_space=pltpu.VMEM)]
    shapes.append(jax.ShapeDtypeStruct((8, LANES), F32))

    def whole(*refs):
        refs = list(refs)
        n_in, n_out = len(arrays), len(shapes)
        in_refs, out_refs, rest = refs[:n_in], refs[n_in : n_in + n_out], refs[n_in + n_out :]
        scratch_refs, rest, sems = rest[: len(scratch)], rest[len(scratch) : -1], rest[-1]
        counter = iter(range(copies))
        handles, loads = [], []

        def load(src, ref):
            loads.append(Load(src, ref, sems.at[next(counter)]))
            return loads[-1]

        for kind, *given in ins:
            if kind == "heads":
                own, oth = in_refs.pop(0), in_refs.pop(0)
                ref = rest.pop(0)
                size = given[0].shape[-2]
                parts = []
                lead = given[0].shape[0] if given[0].ndim == 3 else None
                for k in range(lead or 1):
                    for side, src in enumerate((own, oth)):
                        to = ref.at[pl.ds((2 * k + side) * size, size), :]
                        parts.append(load(src if lead is None else src.at[k], to))

                def joined(parts=parts, ref=ref):
                    for p in parts:
                        p()
                    return ref

                handles.append(joined)
            elif kind == "parts":
                ref = rest.pop(0)
                parts, at = [], 0
                for a in given:
                    parts.append(load(in_refs.pop(0), ref.at[pl.ds(at, a.shape[0]), :]))
                    at += a.shape[0]

                def joined(parts=parts, ref=ref):
                    for p in parts:
                        p()
                    return ref

                handles.append(joined)
            elif kind == "rows":
                ref = rest.pop(0)
                count = ref.shape[0]
                start = pl.multiple_of(lax.axis_index("tp") * count, 8)
                handles.append(load(in_refs.pop(0).at[pl.ds(start, count), :], ref))
            elif kind in ("load", "far"):
                handles.append(load(in_refs.pop(0), rest.pop(0)))
            else:
                handles.append(in_refs.pop(0))
        results, stores = [], []
        for split in splits:
            if split == "hbm":
                results.append(out_refs.pop(0))
                continue
            dst = [out_refs.pop(0) for _ in range(split)]
            stores.append(Store(dst, rest.pop(0), [sems.at[next(counter)] for _ in dst]))
            results.append(stores[-1])
        out_refs[0][...] = jnp.zeros((8, LANES), F32)
        kernel(handles, results, scratch_refs)
        for item in loads:
            item()
        for store in stores:
            if not store.sent:
                store.send()
        for store in stores:
            store.wait()

    moved = sum(a.size * a.dtype.itemsize for a in (*arrays, *shapes)) if flops else 0
    return pl.pallas_call(
        whole,
        name=name,
        out_shape=shapes,
        in_specs=specs,
        out_specs=out_specs,
        scratch_shapes=[*scratch, *extra, pltpu.SemaphoreType.DMA((copies,))],
        compiler_params=pltpu.CompilerParams(vmem_limit_bytes=limit),
        cost_estimate=pl.CostEstimate(flops=flops, bytes_accessed=moved, transcendentals=0),
    )(*arrays)


def pair_bias(own, other, k):
    return jnp.concatenate([own[k : k + 1, :], other[k : k + 1, :]], axis=-1)


def enc_attn_kernel(vis, ins, outs, scratch):
    x, weight, proj, own_bias, oth_bias, gains, shifts = ins
    x1, act, qkv, chance, mixed, branch = outs
    rows, width = x1.ref.shape
    x_rows, w = x(), weight()
    unit, _ = unit_rows(x_rows[...].astype(F32))
    act.ref[...] = (unit * gains[0:1, :] + shifts[0:1, :]).astype(BF16)
    none = jnp.zeros((1, width), F32)
    bias = jnp.concatenate([pair_bias(own_bias, oth_bias, 0), none, pair_bias(own_bias, oth_bias, 1)], axis=1)
    qkv.ref[rows:, :] = jnp.zeros((16, 3 * width), BF16)
    for k in range(3):
        cols = slice(k * width, (k + 1) * width)
        out = dot(act.ref[...], w[cols, :], 1, 1) + bias[:, cols]
        qkv.ref[0:rows, cols] = (out * HEAD_DIM**-0.5 if k == 0 else out).astype(BF16)
    act.send()
    qkv.send()
    attend(
        rows // vis, vis,
        lambda at, p: qkv.ref[pl.ds(at, QUERY), pair_lanes(0, p, width)],
        lambda at, p: [qkv.ref[pl.ds(at, KEYS), pair_lanes(1, p, width)]],
        lambda at, p: [qkv.ref[pl.ds(at, KEYS), pair_lanes(2, p, width)]],
        chance.ref, mixed.ref,
    )
    proj_rows = proj()
    chance.send()
    mixed.send()
    u = dot(mixed.ref[...], proj_rows[...])
    branch.ref[...] = u.astype(BF16)
    x1.ref[...] = x_rows[...].astype(F32) + gains[2:3, :] * (u + shifts[2:3, :])


def one_hots(order, rows, vis):
    images, patches = order.shape
    shape = (rows, patches)
    row = lax.broadcasted_iota(jnp.int32, shape, 0)
    lane = lax.broadcasted_iota(jnp.int32, shape, 1)
    start = lax.broadcasted_iota(jnp.int32, (rows, images), 1) * vis
    own = lax.broadcasted_iota(jnp.int32, (rows, images), 0) - start
    image = jnp.where((own >= 0) & (own < vis), 1.0, 0.0).astype(BF16)
    picked = dot(image, order[...].astype(F32).astype(BF16))
    first = jnp.zeros(shape, jnp.int32)
    for i in range(1, images):
        first = jnp.where(row >= i * vis, i * vis, first)
    place = row - first
    out = []
    for at in (place, place + vis):
        index = jnp.sum(jnp.where(lane == at, picked, 0.0), axis=-1, keepdims=True)
        out.append(jnp.where(lane.astype(F32) == index, 1.0, 0.0).astype(BF16))
    return out


def middle_kernel(vis, ins, outs, scratch):
    (x1, own_fc1, oth_fc1, own_b1, oth_b1, own_fc2, oth_fc2, gains, shifts,
     order, pos, token, weight, proj, own_bias, oth_bias,
     reg_own_fc1, reg_oth_fc1, reg_own_b1, reg_oth_b1, reg_own_fc2, reg_oth_fc2, cot,
     reg_gains, reg_shifts) = ins
    (encoded, act2_t, hid2, slope2, branch2, context, act3, act4, query, kv, chance, mixed, branch3,
     predicted, d_state, own_out, oth_out, small) = outs
    act_s, act5_t, hid, slope, d_before, y1, d_low = scratch
    rows, width = d_state.ref.shape

    state = x1()[...]
    first, second = (own_fc1(), oth_fc1()), (own_fc2(), oth_fc2())
    order, w = order(), weight()
    unit, _ = unit_rows(state)
    act = (unit * gains[1:2, :] + shifts[1:2, :]).astype(BF16)
    act_s[...] = act
    act2_t.ref[...] = transposed(act)
    u = feed_forward(act_s, first, (own_b1, oth_b1), second, hid2.ref, slope2.ref)
    branch2.ref[...] = u.astype(BF16)
    state = state + gains[3:4, :] * (u + shifts[3:4, :])
    encoded.ref[...] = state.astype(BF16)

    high = pos[...].astype(BF16)
    rest = (pos[...] - high.astype(F32)).astype(BF16)
    table = jnp.concatenate([high, rest], axis=1)
    seen, masked = one_hots(order, rows, vis)
    picked = dot(seen, table)
    c = state + (picked[:, :width] + picked[:, width:])
    context.ref[0:rows, :] = c
    unit, _ = unit_rows(c)
    act4.ref[0:rows, :] = (unit * reg_gains[1:2, :] + reg_shifts[1:2, :]).astype(BF16)
    picked = dot(masked, table)
    z = token[...].reshape(1, width) + (picked[:, :width] + picked[:, width:])
    context.ref[rows:, :] = z
    unit, _ = unit_rows(z)
    act3.ref[...] = (unit * reg_gains[0:1, :] + reg_shifts[0:1, :]).astype(BF16)
    act4.ref[rows:, :] = (unit * reg_gains[1:2, :] + reg_shifts[1:2, :]).astype(BF16)

    q = dot(act3.ref[...], w[0:width, :], 1, 1) + pair_bias(own_bias, oth_bias, 0)
    query.ref[...] = (q * HEAD_DIM**-0.5).astype(BF16)
    kv.ref[2 * rows :, :] = jnp.zeros((16, 2 * width), BF16)
    bias_v = jnp.concatenate([jnp.zeros((1, width), F32), pair_bias(own_bias, oth_bias, 1)], axis=1)
    kv.ref[0 : 2 * rows, :] = (dot(act4.ref[...], w[width:, :], 1, 1) + bias_v).astype(BF16)
    for out in (hid2, slope2, act2_t, branch2, encoded, context, act3, act4, query, kv):
        out.send()
    attend(
        rows // vis, vis,
        lambda at, p: query.ref[pl.ds(at, QUERY), pair_lanes(0, p, width)],
        functools.partial(context_windows, kv.ref, rows, width, 0),
        functools.partial(context_windows, kv.ref, rows, width, 1),
        chance.ref, mixed.ref,
    )
    first, second = (reg_own_fc1(), reg_oth_fc1()), (reg_own_fc2(), reg_oth_fc2())
    proj_rows, cot_rows = proj(), cot()
    chance.send()
    mixed.send()
    u = dot(mixed.ref[...], proj_rows[...])
    branch3.ref[...] = u.astype(BF16)
    state = context.ref[rows:, :] + reg_gains[3:4, :] * (u + reg_shifts[3:4, :])
    y1[...] = state

    unit, _ = unit_rows(state)
    act = (unit * reg_gains[2:3, :] + reg_shifts[2:3, :]).astype(BF16)
    act_s[...] = act
    act5_t[...] = transposed(act)
    u = feed_forward(act_s, first, (reg_own_b1, reg_oth_b1), second, hid, slope)
    branch = u + reg_shifts[4:5, :]
    predicted.ref[...] = (y1[...] + reg_gains[4:5, :] * branch).astype(BF16)
    grad = cot_rows[...].astype(F32)
    d_low[...] = (grad * reg_gains[4:5, :]).astype(BF16)
    small.ref[...] = jnp.zeros(small.ref.shape, F32)
    small.ref[0:1, :] = total(grad * branch)
    small.ref[1:2, :] = total(grad) * reg_gains[4:5, :]

    def bias(k, row):
        small.ref[8 + k : 9 + k, :] = row

    feed_forward_slopes(d_low, second, slope, d_before)
    grad = feed_forward_back(d_low, act5_t, first, hid, d_before, (own_out.ref, oth_out.ref), bias)
    unit, scale = unit_rows(y1[...])
    small.ref[2:3, :] = total(grad * unit)
    small.ref[3:4, :] = total(grad)
    d_state.ref[...] = cot_rows[...].astype(F32) + norm_back(grad * reg_gains[2:3, :], unit, scale)


def context_windows(kv, rows, width, part, at, p):
    lanes = pair_lanes(part, p, width)
    return [kv[pl.ds(at, KEYS), lanes], kv[pl.ds(aligned(rows + at), KEYS), lanes]]


def pack_small(small, outs, bias_q, bias_v, ffn_small, at):
    width = small.shape[1]
    half = width // 2
    for side, out in enumerate(outs):
        lanes = slice(side * half, (side + 1) * half)
        small[at : at + 1, 0:half] = bias_q[:, lanes]
        small[at + 1 : at + 2, 0:half] = bias_v[:, lanes]
        small[at + 2 : at + 4, :] = ffn_small[8 + 2 * side : 10 + 2 * side, :]
        out[2 * width : 2 * width + small.shape[0], :] = small[...].astype(BF16)


def split_heads(grad, outs, first):
    width = grad.shape[1]
    half = width // 2
    for k in range(grad.shape[0] // width):
        for side, out in enumerate(outs):
            at = k * width + side * half
            out[(first + k) * half : (first + k + 1) * half, :] = grad[at : at + half].astype(BF16)


def reg_attn_back_kernel(vis, patches, ins, outs, scratch):
    (d_state, branch, proj, mixed, chance, kv, query, weight, act3, act4, context, order, cot, gains, shifts, ffn_small) = ins
    d_enc, own, oth = outs
    d_low, d_mixed, d_query, d_kv, d_ctx, small = scratch
    rows, width = d_enc.ref.shape
    half = width // 2
    packs = (own.ref, oth.ref)
    grad = d_state()[...]
    small[...] = jnp.zeros_like(small)
    small[3:4, :] = total(grad * (branch()[...].astype(F32) + shifts[3:4, :]))
    small[8:9, :] = total(grad) * gains[3:4, :]
    d_low[...] = (grad * gains[3:4, :]).astype(BF16)
    d_mixed[...] = dot(d_low[...], proj()[...], 1, 1).astype(BF16)
    g = dot(mixed()[...], d_low[...], 0, 0)
    for side, out in enumerate(packs):
        out[3 * half : 2 * width, :] = g[side * half : (side + 1) * half].astype(BF16)
    d_query[0:16, :] = jnp.zeros((16, width), BF16)
    d_kv[0:16, :] = jnp.zeros((16, 2 * width), BF16)
    d_kv[rows : rows + 16, :] = jnp.zeros((16, 2 * width), BF16)

    def put_context(part, at, p, blocks):
        lanes = pair_lanes(part, p, width)
        put_window(d_kv, at, lanes, blocks[0])
        put_window(d_kv, aligned(rows + at), lanes, blocks[1])

    q, keys, chances = query(), kv(), chance()
    attend_back(
        rows // vis,
        lambda at, p: q[pl.ds(at, QUERY), pair_lanes(0, p, width)],
        functools.partial(context_windows, keys, rows, width, 0),
        functools.partial(context_windows, keys, rows, width, 1),
        chances, d_mixed,
        lambda at, p, v: put_window(d_query, at, pair_lanes(0, p, width), v),
        functools.partial(put_context, 0),
        functools.partial(put_context, 1),
        GROUP,
    )
    w, a3, a4, ctx, cot_rows, order = weight(), act3(), act4(), context(), cot(), order()
    split_heads(dot(d_query[...], a3[...], 0, 0), packs, 0)
    split_heads(dot(d_kv[...], a4[...], 0, 0), packs, 1)
    bias_q = total(d_query[...].astype(F32))
    bias_v = total(d_kv[:, width:].astype(F32))
    grad4 = dot(d_kv[...], w[width:, :])
    grad3 = dot(d_query[...], w[0:width, :])
    unit, scale = unit_rows(ctx[0:rows, :])
    gain_sum = total(grad4[:rows] * unit)
    d_c = norm_back(grad4[:rows] * gains[1:2, :], unit, scale)
    high = d_c.astype(BF16)
    d_ctx[0:rows, 0:width] = high
    d_ctx[0:rows, width:] = (d_c - high.astype(F32)).astype(BF16)
    d_enc.ref[...] = cot_rows[...].astype(F32) + d_c
    unit, scale = unit_rows(ctx[rows:, :])
    small[0:1, :] = total(grad3 * unit)
    small[1:2, :] = gain_sum + total(grad4[rows:] * unit)
    small[5:6, :] = total(grad3)
    small[6:7, :] = total(grad4)
    d_z = d_state()[...] + norm_back(grad3 * gains[0:1, :] + grad4[rows:] * gains[1:2, :], unit, scale)
    small[10:11, :] = total(d_z)
    high = d_z.astype(BF16)
    d_ctx[rows:, 0:width] = high
    d_ctx[rows:, width:] = (d_z - high.astype(F32)).astype(BF16)
    seen, masked = one_hots(order, rows, vis)
    both = dot(seen, d_ctx[0:rows, :], 0, 0) + dot(masked, d_ctx[rows:, :], 0, 0)
    small[2:3, :] = ffn_small[2:3, :]
    small[4:5, :] = ffn_small[0:1, :]
    small[7:8, :] = ffn_small[3:4, :]
    small[9:10, :] = ffn_small[1:2, :]
    pack_small(small, packs, bias_q, bias_v, ffn_small, 11)
    after = 2 * width + small.shape[0]
    d_pos = (both[:, 0:width] + both[:, width:]).astype(BF16)
    pad = jnp.zeros((own.ref.shape[0] - after - patches, width), BF16)
    for out in packs:
        out[after:, :] = jnp.concatenate([d_pos, pad], axis=0)


def enc_ffn_back_kernel(ins, outs, scratch):
    (d_enc, branch, own_fc2, oth_fc2, slope, hid, act_t, own_fc1, oth_fc1, x1, gains, shifts) = ins
    d_state, small, own_out, oth_out = outs
    d_low, d_before = scratch
    grad = d_enc()[...]
    small.ref[...] = jnp.zeros(small.ref.shape, F32)
    small.ref[0:1, :] = total(grad * (branch()[...].astype(F32) + shifts[3:4, :]))
    small.ref[1:2, :] = total(grad) * gains[3:4, :]
    d_low[...] = (grad * gains[3:4, :]).astype(BF16)

    def bias(k, row):
        small.ref[8 + k : 9 + k, :] = row

    feed_forward_slopes(d_low, (own_fc2(), oth_fc2()), slope(), d_before)
    hid, act_t, first, x1_rows = hid(), act_t(), (own_fc1(), oth_fc1()), x1()
    grad = feed_forward_back(d_low, act_t, first, hid, d_before, (own_out.ref, oth_out.ref), bias)
    unit, scale = unit_rows(x1_rows[...])
    small.ref[2:3, :] = total(grad * unit)
    small.ref[3:4, :] = total(grad)
    d_state.ref[...] = d_enc()[...] + norm_back(grad * gains[1:2, :], unit, scale)


def enc_attn_back_kernel(vis, ins, outs, scratch):
    (d_state, branch, proj, mixed, chance, qkv, weight, act, x, gains, shifts, ffn_small) = ins
    d_input, own, oth = outs
    d_low, d_mixed, d_qkv, small = scratch
    rows, width = d_input.ref.shape
    half = width // 2
    packs = (own.ref, oth.ref)
    grad = d_state()[...]
    small[...] = jnp.zeros_like(small)
    small[2:3, :] = total(grad * (branch()[...].astype(F32) + shifts[2:3, :]))
    small[6:7, :] = total(grad) * gains[2:3, :]
    d_low[...] = (grad * gains[2:3, :]).astype(BF16)
    d_mixed[...] = dot(d_low[...], proj()[...], 1, 1).astype(BF16)
    g = dot(mixed()[...], d_low[...], 0, 0)
    for side, out in enumerate(packs):
        out[3 * half : 2 * width, :] = g[side * half : (side + 1) * half].astype(BF16)
    d_qkv[0:16, :] = jnp.zeros((16, 3 * width), BF16)
    s = qkv()
    attend_back(
        rows // vis,
        lambda at, p: s[pl.ds(at, QUERY), pair_lanes(0, p, width)],
        lambda at, p: [s[pl.ds(at, KEYS), pair_lanes(1, p, width)]],
        lambda at, p: [s[pl.ds(at, KEYS), pair_lanes(2, p, width)]],
        chance(), d_mixed,
        lambda at, p, v: put_window(d_qkv, at, pair_lanes(0, p, width), v),
        lambda at, p, v: put_window(d_qkv, at, pair_lanes(1, p, width), v[0]),
        lambda at, p, v: put_window(d_qkv, at, pair_lanes(2, p, width), v[0]),
        GROUP,
    )
    act, w, x_rows = act(), weight(), x()
    split_heads(dot(d_qkv[...], act[...], 0, 0), packs, 0)
    bias_q = total(d_qkv[:, 0:width].astype(F32))
    bias_v = total(d_qkv[:, 2 * width :].astype(F32))
    grad = dot(d_qkv[...], w[...])
    unit, scale = unit_rows(x_rows[...].astype(F32))
    small[0:1, :] = total(grad * unit)
    small[4:5, :] = total(grad)
    small[1:2, :] = ffn_small[2:3, :]
    small[3:4, :] = ffn_small[0:1, :]
    small[5:6, :] = ffn_small[3:4, :]
    small[7:8, :] = ffn_small[1:2, :]
    pack_small(small, packs, bias_q, bias_v, ffn_small, 8)
    pad = jnp.zeros((own.ref.shape[0] - 2 * width - small.shape[0], width), BF16)
    for out in packs:
        out[2 * width + small.shape[0] :, :] = pad
    d_input.ref[...] = d_state()[...] + norm_back(grad * gains[0:1, :], unit, scale)


def step_bits():
    if plain():
        return [jnp.int32(0), jnp.int32(0)]
    x, y, core = lax.axis_index("x"), lax.axis_index("y"), lax.axis_index("tp")
    return [jnp.where(core == 0, x, y), jnp.where(core == 0, y, x)]


def place_quarters(parts, whole):
    size = whole.shape[0] // 4
    first, second = step_bits()
    for part, (a, b) in zip(parts, ((0, 0), (0, 1), (1, 0), (1, 1))):
        at = ((first ^ a) * 2 + (second ^ b)) * size
        whole[pl.ds(pl.multiple_of(at, 16), size), :] = part()[...]


def halve_kernel(step, ins, outs, scratch):
    bit = step_bits()[step]
    keep, send = outs
    to = 0
    for mine, got in zip(ins[::2], ins[1::2]):
        mine, got = mine(), got()
        half = mine.shape[0] // 2
        for out, b in ((send, 1 - bit), (keep, bit)):
            at = pl.ds(pl.multiple_of(b * half, 16), half)
            out.ref[to : to + half, :] = (mine[at, :].astype(F32) + got[at, :].astype(F32)).astype(BF16)
        to += half
    send.send()


def add_kernel(ins, outs, scratch):
    outs[0].ref[...] = (ins[0]()[...].astype(F32) + ins[1]()[...].astype(F32)).astype(BF16)


def fc_out(first, second, grad1, grad2):
    width, half = grad1.ref.shape
    grad2.ref[...] = second.astype(F32)
    grad2.send()
    for c in range(half // width):
        grad1.ref[:, c * width : (c + 1) * width] = first[c * width : (c + 1) * width].astype(F32)
    grad1.send()


def heads_out(first, second, grad_qkv, grad_proj, rest):
    half = grad_proj.ref.shape[0]
    count = first.shape[0]
    grad_qkv.ref[0:count, :] = first.astype(F32)
    grad_qkv.ref[count:, :] = second[: 3 * half - count].astype(F32)
    grad_qkv.send()
    grad_proj.ref[...] = second[3 * half - count : 4 * half - count].astype(F32)
    grad_proj.send()
    rest.ref[...] = second[4 * half - count :].astype(F32)
    rest.send()


def both_cores(mine, got, out, sems):
    rows = mine.shape[0]
    core = lax.axis_index("tp")
    copies = []
    for src, at, sem in ((mine, core, 0), (got, 1 - core, 1)):
        to = out.at[pl.ds(pl.multiple_of(at * rows, 16), rows), :]
        copies.append(pltpu.make_async_copy(src, to, sems.at[sem]))
        copies[-1].start()
    return copies


def out_ab_kernel(ins, outs, scratch):
    *parts, encoded, got_encoded, predicted, got_predicted = ins
    encoded_out, predicted_out, *grads = outs
    whole, sems, more = scratch
    copies = both_cores(encoded, got_encoded, encoded_out, sems)
    copies += both_cores(predicted, got_predicted, predicted_out, more)
    place_quarters(parts, whole)
    side = whole.shape[0] // 2
    of_a = grads[1].ref.shape[0]
    fc_out(whole[0:of_a, :], whole[side : side + of_a, :], *grads[:2])
    heads_out(whole[of_a:side, :], whole[side + of_a :, :], *grads[2:])
    for copy in copies:
        copy.wait()


def out_c_kernel(ins, outs, scratch):
    *parts, d_input, got_input = ins
    input_out, *grads = outs
    whole, sems = scratch
    copies = both_cores(d_input, got_input, input_out, sems)
    place_quarters(parts, whole)
    side = whole.shape[0] // 2
    fc_out(whole[0:side, :], whole[side:, :], *grads)
    for copy in copies:
        copy.wait()


def out_d_kernel(ins, outs, scratch):
    place_quarters(ins, scratch[0])
    side = scratch[0].shape[0] // 2
    heads_out(scratch[0][0:side, :], scratch[0][side:, :], *outs)


def small_kernel(ins, outs, scratch):
    own_b, got_b, own_d, got_d = ins
    gains_b, shifts_b, token, pos, bias_b, fc_b, gains_d, shifts_d, bias_d, fc_d = outs
    mean = (own_b[...] + got_b[...]) * 0.5
    half = bias_b.ref.shape[1]
    width = 2 * half
    gains_b.ref[...] = mean[0:5]
    shifts_b.ref[...] = mean[5:10]
    token.ref[...] = mean[10, :]
    bias_b.ref[...] = own_b[11:13, 0:half]
    for k in range(2):
        fc_b.ref[k * width : (k + 1) * width] = own_b[13 + k, :]
    pos.ref[...] = mean[32 : 32 + pos.ref.shape[0]]
    mean = (own_d[...] + got_d[...]) * 0.5
    gains_d.ref[...] = mean[0:4]
    shifts_d.ref[...] = mean[4:8]
    bias_d.ref[...] = own_d[8:10, 0:half]
    for k in range(2):
        fc_d.ref[k * width : (k + 1) * width] = own_d[10 + k, :]


CHIPS = ("z", "y", "x")
ORDERS = ((0, 1, 2, 3), (1, 0, 3, 2))


def plain():
    return "dp" in jax.sharding.get_abstract_mesh().axis_names


def swap(a):
    return lax.ppermute(a, "tp", [(0, 1), (1, 0)])


def flip(a, step):
    pairs = [
        (2 * d + t, 2 * (d ^ (1 << ORDERS[t][step])) + t) for d in range(16) for t in range(2)
    ]
    return lax.ppermute(a, (*CHIPS, "tp"), pairs)


def gathered(part):
    other = flip(part, 1)
    return [part, other, flip(part, 0), flip(other, 0)]


def quarters_of(whole):
    size = whole.shape[0] // 4
    return [whole[k * size : (k + 1) * size] for k in range(4)]


def add_up(own, oth):
    return lax.psum(own.astype(F32) + swap(oth).astype(F32), "dp").astype(BF16)


def body(
    x_visible,
    patch_order,
    enc_qkv,
    enc_head_bias,
    enc_proj,
    enc_fc1,
    enc_fc1_bias,
    enc_fc2,
    enc_gains,
    enc_shifts,
    reg_qkv,
    reg_head_bias,
    reg_proj,
    reg_fc1,
    reg_fc1_bias,
    reg_fc2,
    reg_gains,
    reg_shifts,
    pos_embed,
    mask_token,
    enc_cot,
    reg_cot,
):
    all_images, patches = patch_order.shape
    width = x_visible.shape[1]
    vis = x_visible.shape[0] // all_images
    images = all_images // 2
    rows = images * vis
    hidden = 2 * enc_fc1.shape[1]
    half = width // 2
    pairs = width // LANES
    enc_qkv, reg_qkv = jnp.swapaxes(enc_qkv, 1, 2), jnp.swapaxes(reg_qkv, 1, 2)
    enc_heads = ("heads", enc_qkv, swap(enc_qkv))
    enc_out = ("heads", enc_proj, swap(enc_proj))
    enc_bias = ("vmem", enc_head_bias), ("vmem", swap(enc_head_bias))
    oth_enc_fc1, oth_enc_fc2, oth_enc_b1 = swap(enc_fc1), swap(enc_fc2), swap(enc_fc1_bias)
    reg_heads = ("heads", reg_qkv, swap(reg_qkv))
    reg_out = ("heads", reg_proj, swap(reg_proj))
    reg_bias = ("vmem", reg_head_bias), ("vmem", swap(reg_head_bias))
    oth_reg_fc1, oth_reg_fc2, oth_reg_b1 = swap(reg_fc1), swap(reg_fc2), swap(reg_fc1_bias)
    order = ("rows", patch_order)
    enc_vectors = ("vmem", enc_gains), ("vmem", enc_shifts)
    reg_vectors = ("vmem", reg_gains), ("vmem", reg_shifts)

    last = []

    def step(*given, **more):
        *outs, token = run(*given, after=tuple(last), **more)
        last[:] = [token]
        return outs

    def load(*arrays):
        return [("load", a) for a in arrays]

    def vmem(shape, dtype):
        return pltpu.VMEM(shape, dtype)

    def hbm(*arrays):
        return [("hbm", a) for a in arrays]

    def halve(which, *arrays):
        shape = ((sum(a.shape[0] for a in arrays[::2]) // 2, width), BF16)
        ins = [("parts", *a) if isinstance(a, list) else ("load" if which else "far", a) for a in arrays]
        return step(
            functools.partial(halve_kernel, which), "halve", ins, [shape, shape], [],
            limit=12 << 20,
        )

    def add(mine, got):
        return step(add_kernel, "add", load(mine, got), [(mine.shape, BF16)], [], limit=8 << 20)[0]

    state_f = ((rows, width), F32)
    state_b = ((rows, width), BF16)
    act_t = ((width + 16, rows), BF16)
    wide = ((rows, hidden), BF16)
    layer = 2 * rows * width
    x1, act1, qkv1, chance1, mixed1, branch1 = step(
        functools.partial(enc_attn_kernel, vis),
        "enc_attn",
        [("rows", x_visible), enc_heads, enc_out, *enc_bias, *enc_vectors],
        [state_f, state_b, ((rows + 16, 3 * width), BF16),
         ((images * pairs, QUERY, 2 * KEYS), BF16), state_b, state_b],
        [],
        layer * width * 5,
    )
    stage = ((hidden, width), BF16)
    small = ((16, width), F32)
    (encoded, act2_t, hid2, slope2, branch2, context, act3, act4, query3, kv3, chance3, mixed3, branch3,
     predicted, d_state3, own_a, oth_a, small_a) = step(
        functools.partial(middle_kernel, vis),
        "middle",
        [*load(x1, enc_fc1, oth_enc_fc1), ("vmem", enc_fc1_bias), ("vmem", oth_enc_b1),
         *load(enc_fc2, oth_enc_fc2), *enc_vectors, order, ("vmem", pos_embed),
         ("vmem", mask_token), reg_heads, reg_out, *reg_bias,
         *load(reg_fc1, oth_reg_fc1), ("vmem", reg_fc1_bias), ("vmem", oth_reg_b1),
         *load(reg_fc2, oth_reg_fc2), ("rows", reg_cot), *reg_vectors],
        [state_b, act_t, wide, wide, state_b, ((2 * rows, width), F32), state_b,
         ((2 * rows, width), BF16), state_b, ((2 * rows + 16, 2 * width), BF16),
         ((images * pairs, QUERY, 4 * KEYS), BF16), state_b, state_b,
         state_b, state_f, stage, stage, small],
        [vmem(*state_b), vmem(*act_t), vmem(*wide), vmem(*wide), vmem(*wide), vmem(*state_f),
         vmem(*state_b)],
        layer * (hidden * 8 + width * 8),
    )
    got_a = swap(oth_a)
    got_encoded, got_predicted = swap(encoded), swap(predicted)
    heads_b = ((2 * width + 256, width), BF16)
    d_enc, own_b, *oth_b = step(
        functools.partial(reg_attn_back_kernel, vis, patches),
        "reg_attn_back",
        [*load(d_state3, branch3), reg_out, *load(mixed3, chance3, kv3, query3), reg_heads,
         *load(act3, act4, context), order, ("rows", enc_cot), *reg_vectors, ("vmem", small_a)],
        [state_f, heads_b, (*heads_b, 2)],
        [vmem(*state_b), vmem(*state_b), vmem(*state_b), vmem((2 * rows, 2 * width), BF16),
         vmem((2 * rows, 2 * width), BF16), vmem((32, width), F32)],
        layer * width * 16,
    )
    if not plain():
        keep_ab, send_ab = halve(0, own_a, got_a, own_b, [swap(p) for p in oth_b])
        got_ab = flip(send_ab, 0)
    d_state1, small_c, own_c, *oth_c = step(
        enc_ffn_back_kernel,
        "enc_ffn_back",
        [*load(d_enc, branch2, enc_fc2, oth_enc_fc2, slope2, hid2, act2_t, enc_fc1, oth_enc_fc1, x1),
         *enc_vectors],
        [state_f, small, stage, (*stage, 4)],
        [vmem(*state_b), vmem(*wide)],
        layer * hidden * 4,
    )
    if not plain():
        keep_ab, send_ab = halve(1, keep_ab, got_ab)
        got_ab = flip(send_ab, 1)
        keep_c, send_c = halve(0, own_c, [swap(p) for p in oth_c])
        got_c = flip(send_c, 0)
    heads_d = ((2 * width + 64, width), BF16)
    d_input, own_d, *oth_d = step(
        functools.partial(enc_attn_back_kernel, vis),
        "enc_attn_back",
        [*load(d_state1, branch1), enc_out, *load(mixed1, chance1, qkv1), enc_heads, *load(act1),
         ("rows", x_visible), *enc_vectors, ("vmem", small_c)],
        [state_f, heads_d, (*heads_d, 4)],
        [vmem(*state_b), vmem(*state_b), vmem((rows, 3 * width), BF16), vmem((32, width), F32)],
        layer * width * 12,
    )
    got_input = swap(d_input)
    if not plain():
        got_oth_d = [swap(p) for p in oth_d]
        part_ab = add(keep_ab, got_ab)
        got_ab = flip(part_ab, 2)
        keep_c, send_c = halve(1, keep_c, got_c)
        got_c = flip(send_c, 1)
        keep_d, send_d = halve(0, own_d, got_oth_d)
        got_d = flip(send_d, 0)
        part_c = add(keep_c, got_c)
        got_c = flip(part_c, 2)
        part_ab = add(part_ab, got_ab)
        got_ab = flip(part_ab, 3)
        keep_d, send_d = halve(1, keep_d, got_d)
        got_d = flip(send_d, 1)
        part_c = add(part_c, got_c)
        got_c = flip(part_c, 3)
        part_d = add(keep_d, got_d)
        got_d = flip(part_d, 2)
        part_ab = add(part_ab, got_ab)
        quarters_ab = gathered(part_ab)
        part_d = add(part_d, got_d)
        got_d = flip(part_d, 3)
        part_c = add(part_c, got_c)
        quarters_c = gathered(part_c)
        part_d = add(part_d, got_d)
        quarters_d = gathered(part_d)
    else:
        sum_a, sum_b = add_up(own_a, oth_a), add_up(own_b, jnp.concatenate(oth_b))
        at_a, at_b = sum_a.shape[0] // 2, sum_b.shape[0] // 2
        whole = jnp.concatenate([sum_a[:at_a], sum_b[:at_b], sum_a[at_a:], sum_b[at_b:]], axis=0)
        quarters_ab = quarters_of(whole)
        quarters_c, quarters_d = quarters_of(add_up(own_c, jnp.concatenate(oth_c))), quarters_of(add_up(own_d, jnp.concatenate(oth_d)))

    def out_shapes(pack):
        if pack is None:
            return [((width, hidden // 2), F32), ((hidden // 2, width), F32)]
        return [((3 * half, width), F32), ((half, width), F32), ((pack[0][0] - 2 * width, width), F32)]

    def pack_scratch(quarters):
        return vmem((4 * quarters[0].shape[0], width), BF16)

    two = pltpu.SemaphoreType.DMA((2,))
    encoded_out, predicted_out, reg_g1, reg_g2, reg_gq, reg_gp, rest_b = step(
        out_ab_kernel,
        "out_ab",
        [*load(*quarters_ab), *hbm(encoded, got_encoded, predicted, got_predicted)],
        [((2 * rows, width), BF16, "hbm")] * 2 + out_shapes(None) + out_shapes(heads_b),
        [pack_scratch(quarters_ab), two, two],
        limit=20 << 20,
    )
    got_rest_b = swap(rest_b)
    input_out, enc_g1, enc_g2 = step(
        out_c_kernel,
        "out_c",
        [*load(*quarters_c), *hbm(d_input, got_input)],
        [((2 * rows, width), F32, "hbm")] + out_shapes(None),
        [pack_scratch(quarters_c), two],
        limit=12 << 20,
    )
    enc_gq, enc_gp, rest_d = step(
        out_d_kernel, "out_d", load(*quarters_d), out_shapes(heads_d), [pack_scratch(quarters_d)],
        limit=8 << 20,
    )
    biases = [((2, half), F32), ((hidden // 2,), F32)]
    (grad_reg_gains, grad_reg_shifts, token, grad_pos, hb_reg, b1_reg, grad_enc_gains, grad_enc_shifts,
     hb_enc, b1_enc) = step(
        small_kernel,
        "small",
        [("vmem", a) for a in (rest_b, got_rest_b, rest_d, swap(rest_d))],
        [((5, width), F32)] * 2 + [((width,), F32), ((patches, width), F32)] + biases
        + [((4, width), F32)] * 2 + biases,
        [],
        limit=8 << 20,
    )

    def heads(g):
        return jnp.swapaxes(g.reshape(3, half, width), 1, 2)

    return (
        encoded_out, predicted_out, input_out, heads(enc_gq), hb_enc, enc_gp, enc_g1, b1_enc,
        enc_g2, grad_enc_gains, grad_enc_shifts, heads(reg_gq), hb_reg, reg_gp, reg_g1, b1_reg,
        reg_g2, grad_reg_gains, grad_reg_shifts, grad_pos, token,
    )


def solution(mesh):
    if mesh.shape["dp"] == 16:
        mesh = jax.sharding.Mesh(mesh.devices.reshape(4, 2, 2, 2), (*CHIPS, "tp"))
        dp = CHIPS
    else:
        dp = "dp"
    whole, rows = P(), P(dp, None)
    columns, heads = P(None, "tp"), P(None, None, "tp")
    down = P("tp", None)
    weights = (heads, columns, down, columns, P("tp"), down, whole, whole)
    return jax.shard_map(
        body,
        mesh=mesh,
        in_specs=(rows, rows, *weights, *weights, whole, whole, rows, rows),
        out_specs=(rows, rows, rows, *weights, *weights, whole, whole),
        check_vma=False,
    )
```

```python
import functools

import jax
import jax.numpy as jnp
from jax import lax
from jax.experimental import pallas as pl
from jax.experimental.pallas import tpu as pltpu
from jax.sharding import PartitionSpec as P

HEAD_DIM = 64
EPSILON = 1e-06
F32 = jnp.float32
BF16 = jnp.bfloat16
LANES = 128
STEP = 96
QUERY = 112
KEYS = 128
GROUP = 8
VMEM_LIMIT = 60 << 20


def dot(a, b, ca=1, cb=0):
    return lax.dot_general(a, b, (((ca,), (cb,)), ((), ())), preferred_element_type=F32)


def mean_row(v):
    return jnp.mean(v, axis=-1, keepdims=True)


def unit_rows(v):
    centred = v - mean_row(v)
    scale = lax.rsqrt(mean_row(centred * centred) + EPSILON)
    return centred * scale, scale


def norm_back(grad_unit, unit, scale):
    return scale * (grad_unit - mean_row(grad_unit) - unit * mean_row(grad_unit * unit))


def total(v):
    return jnp.sum(jnp.sum(v.reshape(v.shape[0] // 8, 8, v.shape[1]), axis=0), axis=0, keepdims=True)


def gelu_pair(f):
    cdf = 0.5 + 0.5 * lax.erf(f * 0.7071067811865476)
    bell = jnp.exp(f * f * -0.5) * 0.3989422804014327
    return f * cdf, cdf + f * bell


def window(i):
    return i * STEP if isinstance(i, int) else pl.multiple_of(i * STEP, 32)


def aligned(at):
    return at if isinstance(at, int) else pl.multiple_of(at, 16)


def low_lanes():
    return lax.broadcasted_iota(jnp.int32, (KEYS, LANES), 1) < HEAD_DIM


def split_pair(v, low):
    zero = jnp.zeros_like(v)
    return jnp.where(low, v, zero), jnp.where(low, zero, v)


def stack_heads(blocks, low):
    pairs = [split_pair(b, low) for b in blocks]
    return jnp.concatenate([p[0] for p in pairs] + [p[1] for p in pairs], axis=0)


def same_head():
    shape = (2 * LANES, 2 * LANES)
    row = lax.broadcasted_iota(jnp.int32, shape, 0) < LANES
    lane = lax.broadcasted_iota(jnp.int32, shape, 1) < LANES
    return jnp.where(row == lane, 1.0, 0.0).astype(BF16)


def blocks_of(v):
    return [v[:, b : b + LANES] for b in range(0, v.shape[1], LANES)]


def head_sums(blocks, ones):
    n = len(blocks) // 2
    sides = [functools.reduce(jnp.add, blocks[h * n : (h + 1) * n]) for h in range(2)]
    s = dot(jnp.concatenate(sides, axis=1).astype(BF16), ones)
    return [s[:, :LANES]] * n + [s[:, LANES:]] * n


def softmax(scores, keys, queries, ones):
    blocks = [jnp.where(keys, b, -1e30) for b in blocks_of(scores)]
    n = len(blocks) // 2
    tops = []
    for h in range(2):
        top = functools.reduce(jnp.maximum, blocks[h * n : (h + 1) * n])
        tops += [jnp.max(top, axis=-1, keepdims=True)] * n
    blocks = [jnp.exp(b - t) for b, t in zip(blocks, tops)]
    sums = head_sums(blocks, ones)
    weights = [1.0 / sums[0]] * n + [1.0 / sums[n]] * n
    out = [jnp.where(queries, b * w, 0.0).astype(BF16) for b, w in zip(blocks, weights)]
    return jnp.concatenate(out, axis=1)


def put_window(ref, start, lanes, value):
    head = pl.ds(start, 16)
    ref[head, lanes] = ref[head, lanes] + value[:16]
    ref[pl.ds(start + 16, QUERY - 16), lanes] = value[16:QUERY]


def pair_lanes(part, p, width):
    return slice(part * width + p * LANES, part * width + (p + 1) * LANES)


def loop_groups(count, group):
    if count == 1:
        group(0, 0)
    else:
        lax.fori_loop(0, count, group, 0)


def attend(images, vis, query, key, value, chance, mixed):
    width = mixed.shape[1]
    pairs = width // LANES
    low = low_lanes()
    ones = same_head()
    lane = lax.broadcasted_iota(jnp.int32, (QUERY, LANES), 1)
    row = lax.broadcasted_iota(jnp.int32, (QUERY, LANES), 0)
    mixed[0:16, :] = jnp.zeros((16, width), BF16)

    def group(g, carry):
        units = [(g * GROUP + n, p) for n in range(GROUP) for p in range(pairs)]
        scores = [dot(query(window(i), p), stack_heads(key(window(i), p), low), 1, 1) for i, p in units]
        chosen = []
        for (i, p), s in zip(units, scores):
            keys = (lane >= 2 * i) & (lane < 2 * i + vis)
            queries = (row >= 2 * i) & (row < 2 * i + vis)
            chosen.append(softmax(s, keys, queries, ones))
        outs = [dot(c, stack_heads(value(window(i), p), low)).astype(BF16) for (i, p), c in zip(units, chosen)]
        for (i, p), c, o in zip(units, chosen, outs):
            chance[i * pairs + p] = c
            put_window(mixed, window(i), pair_lanes(0, p, width), o)
        return carry

    loop_groups(images // GROUP, group)


def attend_back(images, query, key, value, chance, d_mixed, put_query, put_key, put_value, group_size):
    width = d_mixed.shape[1]
    pairs = width // LANES
    low = low_lanes()
    low_q = low[:QUERY]
    ones = same_head()

    def merge(stack):
        n = stack.shape[0] // (2 * KEYS)
        return [
            jnp.where(
                low_q, stack[b * KEYS : b * KEYS + QUERY], stack[(n + b) * KEYS : (n + b) * KEYS + QUERY]
            ).astype(BF16)
            for b in range(n)
        ]

    def group(g, carry):
        units = [(g * group_size + n, p) for n in range(group_size) for p in range(pairs)]
        d_chance, d_value = [], []
        for i, p in units:
            grad = d_mixed[pl.ds(window(i), QUERY), pair_lanes(0, p, width)]
            d_chance.append(dot(grad, stack_heads(value(window(i), p), low), 1, 1))
            d_value.append(dot(chance[i * pairs + p], grad, 0, 0))
        d_score = []
        for (i, p), d in zip(units, d_chance):
            c = blocks_of(chance[i * pairs + p].astype(F32))
            t = [x * y for x, y in zip(c, blocks_of(d))]
            sums = head_sums(t, ones)
            d_score.append(jnp.concatenate([a - b * s for a, b, s in zip(t, c, sums)], axis=1).astype(BF16))
        d_query, d_key = [], []
        for (i, p), d in zip(units, d_score):
            at = window(i)
            d_query.append((dot(d, stack_heads(key(at, p), low)) * HEAD_DIM**-0.5).astype(BF16))
            d_key.append(dot(d, query(at, p), 0, 0))
        for (i, p), q, k, v in zip(units, d_query, d_key, d_value):
            at = window(i)
            put_query(at, p, q)
            put_key(at, p, merge(k))
            put_value(at, p, merge(v))
        return carry

    loop_groups(images // group_size, group)


def feed_forward(act, first, bias, second, hid, slope):
    out = None
    for side in range(2):
        half = first[side].shape[1]
        to = slice(side * half, (side + 1) * half)
        h, g = gelu_pair(dot(act[...], first[side][...]) + bias[side][...].reshape(1, half))
        h = h.astype(BF16)
        hid[:, to] = h
        slope[:, to] = g.astype(BF16)
        part = dot(h, second[side][...])
        out = part if out is None else out + part
    return out


def feed_forward_slopes(d_low, second, slope, d_before):
    half = second[0].shape[0]
    for side in range(2):
        to = slice(side * half, (side + 1) * half)
        grad = dot(d_low[...], second[side][...], 1, 1)
        d_before[:, to] = (grad * slope[:, to].astype(F32)).astype(BF16)


def feed_forward_back(d_low, act_t, first, hid, d_before, outs, bias, rest):
    width, half = first[0].shape
    grad = dot(d_before[:, 0:half], first[0][...], 1, 1) + dot(d_before[:, half:], first[1][...], 1, 1)
    sends = rest(grad)
    for side in range(2):
        to = slice(side * half, (side + 1) * half)
        out = outs[side].ref
        out[half:, :] = dot(hid[:, to], d_low[...], 0, 0).astype(BF16)
        g = dot(act_t[...], d_before[:, to])
        for c in range(half // width):
            cols = slice(c * width, (c + 1) * width)
            out[cols, :] = g[:width, cols].astype(BF16)
            bias(side * (half // width) + c, g[width : width + 1, cols])
        for send in (*sends, outs[side]):
            send.send()
        sends = ()


def transposed(act):
    return jnp.concatenate([act.T, jnp.ones((16, act.shape[0]), BF16)], axis=0)


class Load:
    def __init__(self, src, ref, sem):
        self.copy, self.ref, self.pending = pltpu.make_async_copy(src, ref, sem), ref, True
        self.copy.start()

    def __call__(self):
        if self.pending:
            self.pending = False
            self.copy.wait()
        return self.ref


class Store:
    def __init__(self, dst, ref, sems):
        self.ref, self.sent = ref, False
        rows = ref.shape[0] // len(dst)
        self.copies = [
            pltpu.make_async_copy(ref if len(dst) == 1 else ref.at[pl.ds(k * rows, rows), :], to, sem)
            for k, (to, sem) in enumerate(zip(dst, sems))
        ]

    def send(self):
        self.sent = True
        for copy in self.copies:
            copy.start()

    def wait(self):
        for copy in self.copies:
            copy.wait()


def run(kernel, name, ins, outs, scratch, flops=0, after=(), limit=VMEM_LIMIT):
    arrays, specs, extra, copies = [], [], [], 0
    near = pl.BlockSpec(memory_space=pl.ANY)
    far = pl.BlockSpec(memory_space=pltpu.HBM)
    if limit == VMEM_LIMIT:
        near = far
    for kind, *given in ins:
        if kind == "heads":
            arrays += given
            specs += [near] * 2
            own = given[0]
            lead = own.shape[0] if own.ndim == 3 else 1
            extra.append(pltpu.VMEM((2 * lead * own.shape[-2], own.shape[-1]), own.dtype))
            copies += 2 * lead
        elif kind == "parts":
            arrays += given
            specs += [near] * len(given)
            count = sum(a.shape[0] for a in given)
            extra.append(pltpu.VMEM((count, given[0].shape[1]), given[0].dtype))
            copies += len(given)
        elif kind == "rows":
            arrays.append(given[0])
            specs.append(far)
            extra.append(pltpu.VMEM((given[0].shape[0] // 2, given[0].shape[1]), given[0].dtype))
            copies += 1
        elif kind == "near":
            arrays.append(given[0])
            specs.append(pl.BlockSpec(memory_space=pltpu.VMEM))
        elif kind in ("load", "far"):
            arrays.append(given[0])
            specs.append(near if kind == "load" else far)
            extra.append(pltpu.VMEM(given[0].shape, given[0].dtype))
            copies += 1
        else:
            arrays.append(given[0])
            specs.append(far if kind == "hbm" else pl.BlockSpec(memory_space=pltpu.VMEM))
    arrays += after
    specs += [pl.BlockSpec(memory_space=pltpu.VMEM)] * len(after)
    shapes, splits = [], []
    for shape, dtype, *more in outs:
        split = (more or [1])[0]
        splits.append(split)
        if split == "hbm":
            shapes.append(jax.ShapeDtypeStruct(shape, dtype))
            continue
        shapes += [jax.ShapeDtypeStruct((shape[0] // split, *shape[1:]), dtype)] * split
        extra.append(pltpu.VMEM(shape, dtype))
        copies += split
    out_specs = [pl.BlockSpec(memory_space=pl.ANY)] * len(shapes) + [pl.BlockSpec(memory_space=pltpu.VMEM)]
    shapes.append(jax.ShapeDtypeStruct((8, LANES), F32))

    def whole(*refs):
        refs = list(refs)
        n_in, n_out = len(arrays), len(shapes)
        in_refs, out_refs, rest = refs[:n_in], refs[n_in : n_in + n_out], refs[n_in + n_out :]
        scratch_refs, rest, sems = rest[: len(scratch)], rest[len(scratch) : -1], rest[-1]
        counter = iter(range(copies))
        handles, loads = [], []

        def load(src, ref):
            loads.append(Load(src, ref, sems.at[next(counter)]))
            return loads[-1]

        for kind, *given in ins:
            if kind == "heads":
                own, oth = in_refs.pop(0), in_refs.pop(0)
                ref = rest.pop(0)
                size = given[0].shape[-2]
                parts = []
                lead = given[0].shape[0] if given[0].ndim == 3 else None
                for k in range(lead or 1):
                    for side, src in enumerate((own, oth)):
                        to = ref.at[pl.ds((2 * k + side) * size, size), :]
                        parts.append(load(src if lead is None else src.at[k], to))

                def joined(parts=parts, ref=ref):
                    for p in parts:
                        p()
                    return ref

                handles.append(joined)
            elif kind == "parts":
                ref = rest.pop(0)
                parts, at = [], 0
                for a in given:
                    parts.append(load(in_refs.pop(0), ref.at[pl.ds(at, a.shape[0]), :]))
                    at += a.shape[0]

                def joined(parts=parts, ref=ref):
                    for p in parts:
                        p()
                    return ref

                handles.append(joined)
            elif kind == "rows":
                ref = rest.pop(0)
                count = ref.shape[0]
                start = pl.multiple_of(lax.axis_index("tp") * count, 8)
                handles.append(load(in_refs.pop(0).at[pl.ds(start, count), :], ref))
            elif kind == "near":
                handles.append(functools.partial(lambda ref: ref, in_refs.pop(0)))
            elif kind in ("load", "far"):
                handles.append(load(in_refs.pop(0), rest.pop(0)))
            else:
                handles.append(in_refs.pop(0))
        results, stores = [], []
        for split in splits:
            if split == "hbm":
                results.append(out_refs.pop(0))
                continue
            dst = [out_refs.pop(0) for _ in range(split)]
            stores.append(Store(dst, rest.pop(0), [sems.at[next(counter)] for _ in dst]))
            results.append(stores[-1])
        out_refs[0][...] = jnp.zeros((8, LANES), F32)
        kernel(handles, results, scratch_refs)
        for item in loads:
            item()
        for store in stores:
            if not store.sent:
                store.send()
        for store in stores:
            store.wait()

    moved = sum(a.size * a.dtype.itemsize for a in (*arrays, *shapes)) if flops else 0
    return pl.pallas_call(
        whole,
        name=name,
        out_shape=shapes,
        in_specs=specs,
        out_specs=out_specs,
        scratch_shapes=[*scratch, *extra, pltpu.SemaphoreType.DMA((copies,))],
        compiler_params=pltpu.CompilerParams(vmem_limit_bytes=limit),
        cost_estimate=pl.CostEstimate(flops=flops, bytes_accessed=moved, transcendentals=0),
    )(*arrays)


def pair_bias(own, other, k):
    return jnp.concatenate([own[k : k + 1, :], other[k : k + 1, :]], axis=-1)


def enc_attn_kernel(vis, ins, outs, scratch):
    x, weight, proj, own_bias, oth_bias, gains, shifts = ins
    x1, act, qkv, chance, mixed, branch = outs
    rows, width = x1.ref.shape
    x_rows = x()
    unit, _ = unit_rows(x_rows[...].astype(F32))
    act.ref[...] = (unit * gains[0:1, :] + shifts[0:1, :]).astype(BF16)
    w = weight()
    none = jnp.zeros((1, width), F32)
    bias = jnp.concatenate([pair_bias(own_bias, oth_bias, 0), none, pair_bias(own_bias, oth_bias, 1)], axis=1)
    qkv.ref[rows:, :] = jnp.zeros((16, 3 * width), BF16)
    for k in range(3):
        cols = slice(k * width, (k + 1) * width)
        out = dot(act.ref[...], w[cols, :], 1, 1) + bias[:, cols]
        qkv.ref[0:rows, cols] = (out * HEAD_DIM**-0.5 if k == 0 else out).astype(BF16)
    act.send()
    qkv.send()
    attend(
        rows // vis, vis,
        lambda at, p: qkv.ref[pl.ds(at, QUERY), pair_lanes(0, p, width)],
        lambda at, p: [qkv.ref[pl.ds(at, KEYS), pair_lanes(1, p, width)]],
        lambda at, p: [qkv.ref[pl.ds(at, KEYS), pair_lanes(2, p, width)]],
        chance.ref, mixed.ref,
    )
    proj_rows = proj()
    chance.send()
    mixed.send()
    u = dot(mixed.ref[...], proj_rows[...])
    branch.ref[...] = u.astype(BF16)
    x1.ref[...] = x_rows[...].astype(F32) + gains[2:3, :] * (u + shifts[2:3, :])


def one_hots(order, rows, vis):
    images, patches = order.shape
    shape = (rows, patches)
    row = lax.broadcasted_iota(jnp.int32, shape, 0)
    lane = lax.broadcasted_iota(jnp.int32, shape, 1)
    start = lax.broadcasted_iota(jnp.int32, (rows, images), 1) * vis
    own = lax.broadcasted_iota(jnp.int32, (rows, images), 0) - start
    image = jnp.where((own >= 0) & (own < vis), 1.0, 0.0).astype(BF16)
    picked = dot(image, order[...].astype(F32).astype(BF16))
    first = jnp.zeros(shape, jnp.int32)
    for i in range(1, images):
        first = jnp.where(row >= i * vis, i * vis, first)
    place = row - first
    out = []
    for at in (place, place + vis):
        index = jnp.sum(jnp.where(lane == at, picked, 0.0), axis=-1, keepdims=True)
        out.append(jnp.where(lane.astype(F32) == index, 1.0, 0.0).astype(BF16))
    return out


def middle_kernel(vis, ins, outs, scratch):
    (x1, own_fc1, oth_fc1, own_b1, oth_b1, own_fc2, oth_fc2, gains, shifts,
     order, pos, token, weight, proj, own_bias, oth_bias,
     reg_own_fc1, reg_oth_fc1, reg_own_b1, reg_oth_b1, reg_own_fc2, reg_oth_fc2, cot,
     reg_gains, reg_shifts) = ins
    (encoded, act2_t, hid2, slope2, branch2, context, act3, act4, query, kv, chance, mixed, branch3,
     predicted, d_state, own_out, oth_out, small) = outs
    act_s, act5_t, hid, slope, d_before, y1, d_low = scratch
    rows, width = d_state.ref.shape

    state = x1()[...]
    unit, _ = unit_rows(state)
    act = (unit * gains[1:2, :] + shifts[1:2, :]).astype(BF16)
    act_s[...] = act
    act2_t.ref[...] = transposed(act)
    first, second = (own_fc1(), oth_fc1()), (own_fc2(), oth_fc2())
    order, w = order(), weight()
    u = feed_forward(act_s, first, (own_b1, oth_b1), second, hid2.ref, slope2.ref)
    branch2.ref[...] = u.astype(BF16)
    state = state + gains[3:4, :] * (u + shifts[3:4, :])
    encoded.ref[...] = state.astype(BF16)

    high = pos[...].astype(BF16)
    rest = (pos[...] - high.astype(F32)).astype(BF16)
    table = jnp.concatenate([high, rest], axis=1)
    seen, masked = one_hots(order, rows, vis)
    picked = dot(seen, table)
    c = state + (picked[:, :width] + picked[:, width:])
    context.ref[0:rows, :] = c
    unit, _ = unit_rows(c)
    act4.ref[0:rows, :] = (unit * reg_gains[1:2, :] + reg_shifts[1:2, :]).astype(BF16)
    picked = dot(masked, table)
    z = token[...].reshape(1, width) + (picked[:, :width] + picked[:, width:])
    context.ref[rows:, :] = z
    unit, _ = unit_rows(z)
    act3.ref[...] = (unit * reg_gains[0:1, :] + reg_shifts[0:1, :]).astype(BF16)
    act4.ref[rows:, :] = (unit * reg_gains[1:2, :] + reg_shifts[1:2, :]).astype(BF16)

    q = dot(act3.ref[...], w[0:width, :], 1, 1) + pair_bias(own_bias, oth_bias, 0)
    query.ref[...] = (q * HEAD_DIM**-0.5).astype(BF16)
    kv.ref[2 * rows :, :] = jnp.zeros((16, 2 * width), BF16)
    bias_v = jnp.concatenate([jnp.zeros((1, width), F32), pair_bias(own_bias, oth_bias, 1)], axis=1)
    kv.ref[0 : 2 * rows, :] = (dot(act4.ref[...], w[width:, :], 1, 1) + bias_v).astype(BF16)
    for out in (hid2, slope2, act2_t, branch2, encoded, context, act3, act4, query, kv):
        out.send()
    attend(
        rows // vis, vis,
        lambda at, p: query.ref[pl.ds(at, QUERY), pair_lanes(0, p, width)],
        functools.partial(context_windows, kv.ref, rows, width, 0),
        functools.partial(context_windows, kv.ref, rows, width, 1),
        chance.ref, mixed.ref,
    )
    first, second = (reg_own_fc1(), reg_oth_fc1()), (reg_own_fc2(), reg_oth_fc2())
    proj_rows, cot_rows = proj(), cot()
    chance.send()
    mixed.send()
    u = dot(mixed.ref[...], proj_rows[...])
    branch3.ref[...] = u.astype(BF16)
    state = context.ref[rows:, :] + reg_gains[3:4, :] * (u + reg_shifts[3:4, :])
    y1[...] = state

    unit, _ = unit_rows(state)
    act = (unit * reg_gains[2:3, :] + reg_shifts[2:3, :]).astype(BF16)
    act_s[...] = act
    act5_t[...] = transposed(act)
    u = feed_forward(act_s, first, (reg_own_b1, reg_oth_b1), second, hid, slope)
    branch = u + reg_shifts[4:5, :]
    predicted.ref[...] = (y1[...] + reg_gains[4:5, :] * branch).astype(BF16)
    grad = cot_rows[...].astype(F32)
    d_low[...] = (grad * reg_gains[4:5, :]).astype(BF16)
    small.ref[...] = jnp.zeros(small.ref.shape, F32)
    small.ref[0:1, :] = total(grad * branch)
    small.ref[1:2, :] = total(grad) * reg_gains[4:5, :]

    def bias(k, row):
        small.ref[8 + k : 9 + k, :] = row

    feed_forward_slopes(d_low, second, slope, d_before)
    def rest(grad):
        unit, scale = unit_rows(y1[...])
        small.ref[2:3, :] = total(grad * unit)
        small.ref[3:4, :] = total(grad)
        d_state.ref[...] = cot_rows[...].astype(F32) + norm_back(grad * reg_gains[2:3, :], unit, scale)
        return predicted, branch3, d_state

    feed_forward_back(d_low, act5_t, first, hid, d_before, (own_out, oth_out), bias, rest)


def context_windows(kv, rows, width, part, at, p):
    lanes = pair_lanes(part, p, width)
    return [kv[pl.ds(at, KEYS), lanes], kv[pl.ds(aligned(rows + at), KEYS), lanes]]


def pack_small(small, outs, bias_q, bias_v, ffn_small, at):
    width = small.shape[1]
    half = width // 2
    for side, out in enumerate(outs):
        lanes = slice(side * half, (side + 1) * half)
        small[at : at + 1, 0:half] = bias_q[:, lanes]
        small[at + 1 : at + 2, 0:half] = bias_v[:, lanes]
        small[at + 2 : at + 4, :] = ffn_small[8 + 2 * side : 10 + 2 * side, :]
        out[2 * width : 2 * width + small.shape[0], :] = small[...].astype(BF16)


def split_heads(grad, outs, first):
    width = grad.shape[1]
    half = width // 2
    for k in range(grad.shape[0] // width):
        for side, out in enumerate(outs):
            at = k * width + side * half
            out[(first + k) * half : (first + k + 1) * half, :] = grad[at : at + half].astype(BF16)


def reg_attn_back_kernel(vis, patches, ins, outs, scratch):
    (d_state, branch, proj, mixed, chance, kv, query, weight, act3, act4, context, order, cot, gains, shifts, ffn_small) = ins
    d_enc, own, oth = outs
    d_low, d_mixed, d_query, d_kv, d_ctx, small = scratch
    rows, width = d_enc.ref.shape
    half = width // 2
    packs = (own.ref, oth.ref)
    grad = d_state()[...]
    small[...] = jnp.zeros_like(small)
    small[3:4, :] = total(grad * (branch()[...].astype(F32) + shifts[3:4, :]))
    small[8:9, :] = total(grad) * gains[3:4, :]
    d_low[...] = (grad * gains[3:4, :]).astype(BF16)
    d_mixed[...] = dot(d_low[...], proj()[...], 1, 1).astype(BF16)
    g = dot(mixed()[...], d_low[...], 0, 0)
    for side, out in enumerate(packs):
        out[3 * half : 2 * width, :] = g[side * half : (side + 1) * half].astype(BF16)
    d_query[0:16, :] = jnp.zeros((16, width), BF16)
    d_kv[0:16, :] = jnp.zeros((16, 2 * width), BF16)
    d_kv[rows : rows + 16, :] = jnp.zeros((16, 2 * width), BF16)

    def put_context(part, at, p, blocks):
        lanes = pair_lanes(part, p, width)
        put_window(d_kv, at, lanes, blocks[0])
        put_window(d_kv, aligned(rows + at), lanes, blocks[1])

    q, keys, chances = query(), kv(), chance()
    attend_back(
        rows // vis,
        lambda at, p: q[pl.ds(at, QUERY), pair_lanes(0, p, width)],
        functools.partial(context_windows, keys, rows, width, 0),
        functools.partial(context_windows, keys, rows, width, 1),
        chances, d_mixed,
        lambda at, p, v: put_window(d_query, at, pair_lanes(0, p, width), v),
        functools.partial(put_context, 0),
        functools.partial(put_context, 1),
        GROUP,
    )
    w, a3, a4, ctx, cot_rows, order = weight(), act3(), act4(), context(), cot(), order()
    split_heads(dot(d_query[...], a3[...], 0, 0), packs, 0)
    split_heads(dot(d_kv[...], a4[...], 0, 0), packs, 1)
    bias_q = total(d_query[...].astype(F32))
    bias_v = total(d_kv[:, width:].astype(F32))
    grad4 = dot(d_kv[...], w[width:, :])
    grad3 = dot(d_query[...], w[0:width, :])
    unit, scale = unit_rows(ctx[0:rows, :])
    gain_sum = total(grad4[:rows] * unit)
    d_c = norm_back(grad4[:rows] * gains[1:2, :], unit, scale)
    high = d_c.astype(BF16)
    d_ctx[0:rows, 0:width] = high
    d_ctx[0:rows, width:] = (d_c - high.astype(F32)).astype(BF16)
    d_enc.ref[...] = cot_rows[...].astype(F32) + d_c
    unit, scale = unit_rows(ctx[rows:, :])
    small[0:1, :] = total(grad3 * unit)
    small[1:2, :] = gain_sum + total(grad4[rows:] * unit)
    small[5:6, :] = total(grad3)
    small[6:7, :] = total(grad4)
    d_z = d_state()[...] + norm_back(grad3 * gains[0:1, :] + grad4[rows:] * gains[1:2, :], unit, scale)
    small[10:11, :] = total(d_z)
    high = d_z.astype(BF16)
    d_ctx[rows:, 0:width] = high
    d_ctx[rows:, width:] = (d_z - high.astype(F32)).astype(BF16)
    seen, masked = one_hots(order, rows, vis)
    both = dot(seen, d_ctx[0:rows, :], 0, 0) + dot(masked, d_ctx[rows:, :], 0, 0)
    small[2:3, :] = ffn_small[2:3, :]
    small[4:5, :] = ffn_small[0:1, :]
    small[7:8, :] = ffn_small[3:4, :]
    small[9:10, :] = ffn_small[1:2, :]
    pack_small(small, packs, bias_q, bias_v, ffn_small, 11)
    after = 2 * width + small.shape[0]
    d_pos = (both[:, 0:width] + both[:, width:]).astype(BF16)
    pad = jnp.zeros((own.ref.shape[0] - after - patches, width), BF16)
    for out in packs:
        out[after:, :] = jnp.concatenate([d_pos, pad], axis=0)


def enc_ffn_back_kernel(ins, outs, scratch):
    (d_enc, branch, own_fc2, oth_fc2, slope, hid, act_t, own_fc1, oth_fc1, x1, gains, shifts) = ins
    d_state, small, own_out, oth_out = outs
    d_low, d_before = scratch
    grad = d_enc()[...]
    small.ref[...] = jnp.zeros(small.ref.shape, F32)
    small.ref[0:1, :] = total(grad * (branch()[...].astype(F32) + shifts[3:4, :]))
    small.ref[1:2, :] = total(grad) * gains[3:4, :]
    d_low[...] = (grad * gains[3:4, :]).astype(BF16)

    def bias(k, row):
        small.ref[8 + k : 9 + k, :] = row

    feed_forward_slopes(d_low, (own_fc2(), oth_fc2()), slope(), d_before)
    hid, act_t, first, x1_rows = hid(), act_t(), (own_fc1(), oth_fc1()), x1()

    def rest(grad):
        unit, scale = unit_rows(x1_rows[...])
        small.ref[2:3, :] = total(grad * unit)
        small.ref[3:4, :] = total(grad)
        d_state.ref[...] = d_enc()[...] + norm_back(grad * gains[1:2, :], unit, scale)
        return (d_state,)

    feed_forward_back(d_low, act_t, first, hid, d_before, (own_out, oth_out), bias, rest)


def enc_attn_back_kernel(vis, ins, outs, scratch):
    (d_state, branch, proj, mixed, chance, qkv, weight, act, x, gains, shifts, ffn_small) = ins
    d_input, own, oth = outs
    d_low, d_mixed, d_qkv, small = scratch
    rows, width = d_input.ref.shape
    half = width // 2
    packs = (own.ref, oth.ref)
    grad = d_state()[...]
    small[...] = jnp.zeros_like(small)
    small[2:3, :] = total(grad * (branch()[...].astype(F32) + shifts[2:3, :]))
    small[6:7, :] = total(grad) * gains[2:3, :]
    d_low[...] = (grad * gains[2:3, :]).astype(BF16)
    d_mixed[...] = dot(d_low[...], proj()[...], 1, 1).astype(BF16)
    g = dot(mixed()[...], d_low[...], 0, 0)
    for side, out in enumerate(packs):
        out[3 * half : 2 * width, :] = g[side * half : (side + 1) * half].astype(BF16)
    d_qkv[0:16, :] = jnp.zeros((16, 3 * width), BF16)
    s = qkv()
    attend_back(
        rows // vis,
        lambda at, p: s[pl.ds(at, QUERY), pair_lanes(0, p, width)],
        lambda at, p: [s[pl.ds(at, KEYS), pair_lanes(1, p, width)]],
        lambda at, p: [s[pl.ds(at, KEYS), pair_lanes(2, p, width)]],
        chance(), d_mixed,
        lambda at, p, v: put_window(d_qkv, at, pair_lanes(0, p, width), v),
        lambda at, p, v: put_window(d_qkv, at, pair_lanes(1, p, width), v[0]),
        lambda at, p, v: put_window(d_qkv, at, pair_lanes(2, p, width), v[0]),
        GROUP,
    )
    act, w, x_rows = act(), weight(), x()
    grad = dot(d_qkv[...], w[...])
    split_heads(dot(d_qkv[...], act[...], 0, 0), packs, 0)
    bias_q = total(d_qkv[:, 0:width].astype(F32))
    bias_v = total(d_qkv[:, 2 * width :].astype(F32))
    unit, scale = unit_rows(x_rows[...].astype(F32))
    small[0:1, :] = total(grad * unit)
    small[4:5, :] = total(grad)
    small[1:2, :] = ffn_small[2:3, :]
    small[3:4, :] = ffn_small[0:1, :]
    small[5:6, :] = ffn_small[3:4, :]
    small[7:8, :] = ffn_small[1:2, :]
    pack_small(small, packs, bias_q, bias_v, ffn_small, 8)
    pad = jnp.zeros((own.ref.shape[0] - 2 * width - small.shape[0], width), BF16)
    for out in packs:
        out[2 * width + small.shape[0] :, :] = pad
    d_input.ref[...] = d_state()[...] + norm_back(grad * gains[0:1, :], unit, scale)


def step_bits():
    if plain():
        return [jnp.int32(0), jnp.int32(0)]
    x, y, core = lax.axis_index("x"), lax.axis_index("y"), lax.axis_index("tp")
    return [jnp.where(core == 0, x, y), jnp.where(core == 0, y, x)]


def place_quarters(parts, whole):
    size = whole.shape[0] // 4
    first, second = step_bits()
    pieces = len(parts) // 4
    size = size // pieces
    for k, (a, b) in enumerate(((0, 0), (0, 1), (1, 0), (1, 1))):
        at = ((first ^ a) * 2 + (second ^ b)) * pieces * size
        for j, part in enumerate(parts[k * pieces : (k + 1) * pieces]):
            whole[pl.ds(pl.multiple_of(at + j * size, 16), size), :] = part()[...]


def sum_rows(a, b):
    return (a.astype(F32) + b.astype(F32)).astype(BF16)


def halve_kernel(step, counts, *refs):
    *ins, _, keep, send, token = refs
    token[...] = jnp.zeros((8, LANES), F32)
    bit = step_bits()[step]

    def write(keep_half):
        rest, to = list(ins), 0
        for count in counts:
            mine, got, rest = rest[0], rest[1 : 1 + count], rest[1 + count :]
            half = mine.shape[0] // 2
            size = min(half, got[0].shape[0])
            for out, b in ((send, 1 - keep_half), (keep, keep_half)):
                for at in range(b * half, (b + 1) * half, size):
                    piece, first = divmod(at, got[0].shape[0])
                    where = slice(to + at - b * half, to + at - b * half + size)
                    out[where, :] = sum_rows(mine[at : at + size, :], got[piece][first : first + size, :])
            to += half

    for b in range(2):
        pl.when(bit == b)(functools.partial(write, b))


def piece_rows(refs, at, size):
    for ref in refs:
        if at < ref.shape[0]:
            return ref[at : at + size, :]
        at -= ref.shape[0]


def add_kernel(n_mine, n_got, *refs):
    mine, got, outs = refs[:n_mine], refs[n_mine : n_mine + n_got], refs[n_mine + n_got + 1 : -1]
    refs[-1][...] = jnp.zeros((8, LANES), F32)
    at = 0
    for out in outs:
        size = min(r.shape[0] for r in (out, *mine, *got))
        for to in range(0, out.shape[0], size):
            out[to : to + size, :] = sum_rows(piece_rows(mine, at, size), piece_rows(got, at, size))
            at += size


def fc_out(first, second, grad1, grad2):
    width, half = grad1.ref.shape
    grad2.ref[...] = second.astype(F32)
    grad2.send()
    for c in range(half // width):
        grad1.ref[:, c * width : (c + 1) * width] = first[c * width : (c + 1) * width].astype(F32)
    grad1.send()


def heads_out(first, second, grad_qkv, grad_proj, rest):
    half = grad_proj.ref.shape[0]
    count = first.shape[0]
    grad_qkv.ref[0:count, :] = first.astype(F32)
    grad_qkv.ref[count:, :] = second[: 3 * half - count].astype(F32)
    grad_qkv.send()
    grad_proj.ref[...] = second[3 * half - count : 4 * half - count].astype(F32)
    grad_proj.send()
    rest.ref[...] = second[4 * half - count :].astype(F32)
    rest.send()


def both_cores(mine, got, out, sems):
    rows = mine.shape[0]
    core = lax.axis_index("tp")
    copies = []
    for src, at, sem in ((mine, core, 0), (got, 1 - core, 1)):
        to = out.at[pl.ds(pl.multiple_of(at * rows, 16), rows), :]
        copies.append(pltpu.make_async_copy(src, to, sems.at[sem]))
        copies[-1].start()
    return copies


def out_ab_kernel(ins, outs, scratch):
    *parts, encoded, got_encoded, predicted, got_predicted = ins
    encoded_out, predicted_out, *grads = outs
    whole, sems, more = scratch
    copies = both_cores(encoded, got_encoded, encoded_out, sems)
    copies += both_cores(predicted, got_predicted, predicted_out, more)
    place_quarters(parts, whole)
    side = whole.shape[0] // 2
    of_a = grads[1].ref.shape[0]
    fc_out(whole[0:of_a, :], whole[side : side + of_a, :], *grads[:2])
    heads_out(whole[of_a:side, :], whole[side + of_a :, :], *grads[2:])
    for copy in copies:
        copy.wait()


def out_c_kernel(ins, outs, scratch):
    *parts, d_input, got_input = ins
    input_out, *grads = outs
    whole, sems = scratch
    copies = both_cores(d_input, got_input, input_out, sems)
    place_quarters(parts, whole)
    side = whole.shape[0] // 2
    fc_out(whole[0:side, :], whole[side:, :], *grads)
    for copy in copies:
        copy.wait()


def out_d_kernel(ins, outs, scratch):
    place_quarters(ins, scratch[0])
    side = scratch[0].shape[0] // 2
    heads_out(scratch[0][0:side, :], scratch[0][side:, :], *outs)


def small_kernel(ins, outs, scratch):
    own_b, got_b, own_d, got_d = ins
    gains_b, shifts_b, token, pos, bias_b, fc_b, gains_d, shifts_d, bias_d, fc_d = outs
    mean = (own_b[...] + got_b[...]) * 0.5
    half = bias_b.ref.shape[1]
    width = 2 * half
    gains_b.ref[...] = mean[0:5]
    shifts_b.ref[...] = mean[5:10]
    token.ref[...] = mean[10, :]
    bias_b.ref[...] = own_b[11:13, 0:half]
    for k in range(2):
        fc_b.ref[k * width : (k + 1) * width] = own_b[13 + k, :]
    pos.ref[...] = mean[32 : 32 + pos.ref.shape[0]]
    mean = (own_d[...] + got_d[...]) * 0.5
    gains_d.ref[...] = mean[0:4]
    shifts_d.ref[...] = mean[4:8]
    bias_d.ref[...] = own_d[8:10, 0:half]
    for k in range(2):
        fc_d.ref[k * width : (k + 1) * width] = own_d[10 + k, :]


CHIPS = ("z", "y", "x")
ORDERS = ((0, 1, 2, 3), (1, 0, 3, 2))


def plain():
    return "dp" in jax.sharding.get_abstract_mesh().axis_names


def swap(a):
    return lax.ppermute(a, "tp", [(0, 1), (1, 0)])


def flip(a, step):
    pairs = [
        (2 * d + t, 2 * (d ^ (1 << ORDERS[t][step])) + t) for d in range(16) for t in range(2)
    ]
    return lax.ppermute(a, (*CHIPS, "tp"), pairs)


def flips(pieces, step):
    return [flip(p, step) for p in pieces]


def gathered(part):
    other = flips(part, 1)
    return [*part, *other, *flips(part, 0), *flips(other, 0)]


def quarters_of(whole):
    size = whole.shape[0] // 4
    return [whole[k * size : (k + 1) * size] for k in range(4)]


def add_up(own, oth):
    return lax.psum(own.astype(F32) + swap(oth).astype(F32), "dp").astype(BF16)


def body(
    x_visible,
    patch_order,
    enc_qkv,
    enc_head_bias,
    enc_proj,
    enc_fc1,
    enc_fc1_bias,
    enc_fc2,
    enc_gains,
    enc_shifts,
    reg_qkv,
    reg_head_bias,
    reg_proj,
    reg_fc1,
    reg_fc1_bias,
    reg_fc2,
    reg_gains,
    reg_shifts,
    pos_embed,
    mask_token,
    enc_cot,
    reg_cot,
):
    all_images, patches = patch_order.shape
    width = x_visible.shape[1]
    vis = x_visible.shape[0] // all_images
    images = all_images // 2
    rows = images * vis
    hidden = 2 * enc_fc1.shape[1]
    half = width // 2
    pairs = width // LANES
    enc_qkv, reg_qkv = jnp.swapaxes(enc_qkv, 1, 2), jnp.swapaxes(reg_qkv, 1, 2)
    enc_heads = ("heads", enc_qkv, swap(enc_qkv))
    enc_out = ("heads", enc_proj, swap(enc_proj))
    enc_bias = ("vmem", enc_head_bias), ("vmem", swap(enc_head_bias))
    oth_enc_fc1, oth_enc_fc2, oth_enc_b1 = swap(enc_fc1), swap(enc_fc2), swap(enc_fc1_bias)
    reg_heads = ("heads", reg_qkv, swap(reg_qkv))
    reg_out = ("heads", reg_proj, swap(reg_proj))
    reg_bias = ("vmem", reg_head_bias), ("vmem", swap(reg_head_bias))
    oth_reg_fc1, oth_reg_fc2, oth_reg_b1 = swap(reg_fc1), swap(reg_fc2), swap(reg_fc1_bias)
    order = ("rows", patch_order)
    enc_vectors = ("vmem", enc_gains), ("vmem", enc_shifts)
    reg_vectors = ("vmem", reg_gains), ("vmem", reg_shifts)

    last = []

    def step(*given, **more):
        *outs, token = run(*given, after=tuple(last), **more)
        last[:] = [token]
        return outs

    def load(*arrays):
        return [("load", a) for a in arrays]

    def vmem(shape, dtype):
        return pltpu.VMEM(shape, dtype)

    def hbm(*arrays):
        return [("hbm", a) for a in arrays]

    def light(kernel, name, ins, shapes, chain=True):
        whole = pl.BlockSpec(memory_space=pltpu.VMEM)
        ins = [*ins, last[0] if chain else jnp.zeros((8, LANES), F32)]
        outs = [jax.ShapeDtypeStruct(shape, BF16) for shape in shapes]
        *outs, token = pl.pallas_call(
            kernel,
            name=name,
            out_shape=[*outs, jax.ShapeDtypeStruct((8, LANES), F32)],
            in_specs=[whole] * len(ins),
            out_specs=[whole] * (len(outs) + 1),
            compiler_params=pltpu.CompilerParams(vmem_limit_bytes=8 << 20),
            cost_estimate=pl.CostEstimate(flops=0, bytes_accessed=0, transcendentals=0),
        )(*ins)
        last[:] = [token]
        return outs

    def halve(which, *arrays, chain=True):
        pieces = [a if isinstance(a, list) else [a] for a in arrays]
        shape = (sum(a.shape[0] for a in arrays[::2]) // 2, width)
        kernel = functools.partial(halve_kernel, which, [len(p) for p in pieces[1::2]])
        return light(kernel, "halve", [a for p in pieces for a in p], [shape, shape], chain)

    def add(mine, got, pieces):
        rows_in = sum(a.shape[0] for a in mine) // pieces
        kernel = functools.partial(add_kernel, len(mine), len(got))
        return light(kernel, "add", [*mine, *got], [(rows_in, width)] * pieces)

    def near(*arrays):
        return [("near", a) for a in arrays]

    state_f = ((rows, width), F32)
    state_b = ((rows, width), BF16)
    act_t = ((width + 16, rows), BF16)
    wide = ((rows, hidden), BF16)
    layer = 2 * rows * width
    x1, act1, qkv1, chance1, mixed1, branch1 = step(
        functools.partial(enc_attn_kernel, vis),
        "enc_attn",
        [("rows", x_visible), enc_heads, enc_out, *enc_bias, *enc_vectors],
        [state_f, state_b, ((rows + 16, 3 * width), BF16),
         ((images * pairs, QUERY, 2 * KEYS), BF16), state_b, state_b],
        [],
        layer * width * 5,
    )
    stage = ((hidden, width), BF16)
    small = ((16, width), F32)
    (encoded, act2_t, hid2, slope2, branch2, context, act3, act4, query3, kv3, chance3, mixed3, branch3,
     predicted, d_state3, own_a, oth_a, small_a) = step(
        functools.partial(middle_kernel, vis),
        "middle",
        [*load(x1, enc_fc1, oth_enc_fc1), ("vmem", enc_fc1_bias), ("vmem", oth_enc_b1),
         *load(enc_fc2, oth_enc_fc2), *enc_vectors, order, ("vmem", pos_embed),
         ("vmem", mask_token), reg_heads, reg_out, *reg_bias,
         *load(reg_fc1, oth_reg_fc1), ("vmem", reg_fc1_bias), ("vmem", oth_reg_b1),
         *load(reg_fc2, oth_reg_fc2), ("rows", reg_cot), *reg_vectors],
        [state_b, act_t, wide, wide, state_b, ((2 * rows, width), F32), state_b,
         ((2 * rows, width), BF16), state_b, ((2 * rows + 16, 2 * width), BF16),
         ((images * pairs, QUERY, 4 * KEYS), BF16), state_b, state_b,
         state_b, state_f, stage, stage, small],
        [vmem(*state_b), vmem(*act_t), vmem(*wide), vmem(*wide), vmem(*wide), vmem(*state_f),
         vmem(*state_b)],
        layer * (hidden * 8 + width * 8),
    )
    got_a = swap(oth_a)
    got_encoded, got_predicted = swap(encoded), swap(predicted)
    heads_b = ((2 * width + 256, width), BF16)
    d_enc, own_b, *oth_b = step(
        functools.partial(reg_attn_back_kernel, vis, patches),
        "reg_attn_back",
        [*load(d_state3, branch3), reg_out, *load(mixed3, chance3, kv3, query3), reg_heads,
         *load(act3, act4, context), order, ("rows", enc_cot), *reg_vectors, ("vmem", small_a)],
        [state_f, heads_b, (*heads_b, 2)],
        [vmem(*state_b), vmem(*state_b), vmem(*state_b), vmem((2 * rows, 2 * width), BF16),
         vmem((2 * rows, 2 * width), BF16), vmem((32, width), F32)],
        layer * width * 16,
    )
    if not plain():
        keep_ab, send_ab = halve(0, own_a, got_a, own_b, [swap(p) for p in oth_b], chain=False)
        got_ab = flip(send_ab, 0)
    d_state1, small_c, own_c, *oth_c = step(
        enc_ffn_back_kernel,
        "enc_ffn_back",
        [*load(d_enc, branch2, enc_fc2, oth_enc_fc2, slope2, hid2, act2_t, enc_fc1, oth_enc_fc1, x1),
         *enc_vectors],
        [state_f, small, stage, (*stage, 4)],
        [vmem(*state_b), vmem(*wide)],
        layer * hidden * 4,
    )
    if not plain():
        keep_ab, send_ab = halve(1, keep_ab, got_ab)
        got_ab = flip(send_ab, 1)
        keep_c, send_c = halve(0, own_c, [swap(p) for p in oth_c])
        got_c = flip(send_c, 0)
    heads_d = ((2 * width + 64, width), BF16)
    d_input, own_d, *oth_d = step(
        functools.partial(enc_attn_back_kernel, vis),
        "enc_attn_back",
        [*load(d_state1, branch1), enc_out, *load(mixed1, chance1, qkv1), enc_heads, *load(act1),
         ("rows", x_visible), *enc_vectors, ("vmem", small_c)],
        [state_f, heads_d, (*heads_d, 4)],
        [vmem(*state_b), vmem(*state_b), vmem((rows, 3 * width), BF16), vmem((32, width), F32)],
        layer * width * 12,
    )
    got_input = swap(d_input)
    if not plain():
        got_oth_d = [swap(p) for p in oth_d]
        n_ab, n_c = 1, 1
        part_ab = add([keep_ab], [got_ab], n_ab)
        got_ab = flips(part_ab, 2)
        keep_c, send_c = halve(1, keep_c, got_c)
        got_c = flip(send_c, 1)
        keep_d, send_d = halve(0, own_d, got_oth_d)
        got_d = flip(send_d, 0)
        part_c = add([keep_c], [got_c], n_c)
        got_c = flips(part_c, 2)
        part_ab = add(part_ab, got_ab, 2)
        got_ab = flips(part_ab, 3)
        keep_d, send_d = halve(1, keep_d, got_d)
        got_d = flip(send_d, 1)
        part_c = add(part_c, got_c, n_c)
        got_c = flips(part_c, 3)
        part_d = add([keep_d], [got_d], 1)
        got_d = flips(part_d, 2)
        part_ab = add(part_ab, got_ab, n_ab)
        quarters_ab = gathered(part_ab)
        part_d = add(part_d, got_d, 1)
        got_d = flips(part_d, 3)
        part_c = add(part_c, got_c, n_c)
        quarters_c = gathered(part_c)
        part_d = add(part_d, got_d, 1)
        quarters_d = gathered(part_d)
    else:
        sum_a, sum_b = add_up(own_a, oth_a), add_up(own_b, jnp.concatenate(oth_b))
        at_a, at_b = sum_a.shape[0] // 2, sum_b.shape[0] // 2
        whole = jnp.concatenate([sum_a[:at_a], sum_b[:at_b], sum_a[at_a:], sum_b[at_b:]], axis=0)
        quarters_ab = quarters_of(whole)
        quarters_c, quarters_d = quarters_of(add_up(own_c, jnp.concatenate(oth_c))), quarters_of(add_up(own_d, jnp.concatenate(oth_d)))

    def out_shapes(pack):
        if pack is None:
            return [((width, hidden // 2), F32), ((hidden // 2, width), F32)]
        return [((3 * half, width), F32), ((half, width), F32), ((pack[0][0] - 2 * width, width), F32)]

    def pack_scratch(quarters):
        return vmem((sum(q.shape[0] for q in quarters), width), BF16)

    two = pltpu.SemaphoreType.DMA((2,))
    encoded_out, predicted_out, reg_g1, reg_g2, reg_gq, reg_gp, rest_b = step(
        out_ab_kernel,
        "out_ab",
        [*near(*quarters_ab), *hbm(encoded, got_encoded, predicted, got_predicted)],
        [((2 * rows, width), BF16, "hbm")] * 2 + out_shapes(None) + out_shapes(heads_b),
        [pack_scratch(quarters_ab), two, two],
        limit=20 << 20,
    )
    got_rest_b = swap(rest_b)
    input_out, enc_g1, enc_g2 = step(
        out_c_kernel,
        "out_c",
        [*near(*quarters_c), *hbm(d_input, got_input)],
        [((2 * rows, width), F32, "hbm")] + out_shapes(None),
        [pack_scratch(quarters_c), two],
        limit=12 << 20,
    )
    enc_gq, enc_gp, rest_d = step(
        out_d_kernel, "out_d", near(*quarters_d), out_shapes(heads_d), [pack_scratch(quarters_d)],
        limit=8 << 20,
    )
    biases = [((2, half), F32), ((hidden // 2,), F32)]
    (grad_reg_gains, grad_reg_shifts, token, grad_pos, hb_reg, b1_reg, grad_enc_gains, grad_enc_shifts,
     hb_enc, b1_enc) = step(
        small_kernel,
        "small",
        [("vmem", a) for a in (rest_b, got_rest_b, rest_d, swap(rest_d))],
        [((5, width), F32)] * 2 + [((width,), F32), ((patches, width), F32)] + biases
        + [((4, width), F32)] * 2 + biases,
        [],
        limit=8 << 20,
    )

    def heads(g):
        return jnp.swapaxes(g.reshape(3, half, width), 1, 2)

    return (
        encoded_out, predicted_out, input_out, heads(enc_gq), hb_enc, enc_gp, enc_g1, b1_enc,
        enc_g2, grad_enc_gains, grad_enc_shifts, heads(reg_gq), hb_reg, reg_gp, reg_g1, b1_reg,
        reg_g2, grad_reg_gains, grad_reg_shifts, grad_pos, token,
    )


def solution(mesh):
    if mesh.shape["dp"] == 16:
        mesh = jax.sharding.Mesh(mesh.devices.reshape(4, 2, 2, 2), (*CHIPS, "tp"))
        dp = CHIPS
    else:
        dp = "dp"
    whole, rows = P(), P(dp, None)
    columns, heads = P(None, "tp"), P(None, None, "tp")
    down = P("tp", None)
    weights = (heads, columns, down, columns, P("tp"), down, whole, whole)
    return jax.shard_map(
        body,
        mesh=mesh,
        in_specs=(rows, rows, *weights, *weights, whole, whole, rows, rows),
        out_specs=(rows, rows, rows, *weights, *weights, whole, whole),
        check_vma=False,
    )
```

```python
import functools

import jax
import jax.numpy as jnp
from jax import lax
from jax.experimental import pallas as pl
from jax.experimental.pallas import tpu as pltpu
from jax.sharding import PartitionSpec as P

HEAD_DIM = 64
EPSILON = 1e-06
F32 = jnp.float32
BF16 = jnp.bfloat16
LANES = 128
STEP = 96
QUERY = 112
KEYS = 128
GROUP = 8
VMEM_LIMIT = 60 << 20


def dot(a, b, ca=1, cb=0):
    return lax.dot_general(a, b, (((ca,), (cb,)), ((), ())), preferred_element_type=F32)


def mean_row(v):
    return jnp.mean(v, axis=-1, keepdims=True)


def unit_rows(v):
    centred = v - mean_row(v)
    scale = lax.rsqrt(mean_row(centred * centred) + EPSILON)
    return centred * scale, scale


def norm_back(grad_unit, unit, scale):
    return scale * (grad_unit - mean_row(grad_unit) - unit * mean_row(grad_unit * unit))


def total(v):
    return jnp.sum(jnp.sum(v.reshape(v.shape[0] // 8, 8, v.shape[1]), axis=0), axis=0, keepdims=True)


def gelu_pair(f):
    cdf = 0.5 + 0.5 * lax.erf(f * 0.7071067811865476)
    bell = jnp.exp(f * f * -0.5) * 0.3989422804014327
    return f * cdf, cdf + f * bell


def window(i):
    return i * STEP if isinstance(i, int) else pl.multiple_of(i * STEP, 32)


def aligned(at):
    return at if isinstance(at, int) else pl.multiple_of(at, 16)


def low_lanes():
    return lax.broadcasted_iota(jnp.int32, (KEYS, LANES), 1) < HEAD_DIM


def split_pair(v, low):
    zero = jnp.zeros_like(v)
    return jnp.where(low, v, zero), jnp.where(low, zero, v)


def stack_heads(blocks, low):
    pairs = [split_pair(b, low) for b in blocks]
    return jnp.concatenate([p[0] for p in pairs] + [p[1] for p in pairs], axis=0)


def same_head():
    shape = (2 * LANES, 2 * LANES)
    row = lax.broadcasted_iota(jnp.int32, shape, 0) < LANES
    lane = lax.broadcasted_iota(jnp.int32, shape, 1) < LANES
    return jnp.where(row == lane, 1.0, 0.0).astype(BF16)


def blocks_of(v):
    return [v[:, b : b + LANES] for b in range(0, v.shape[1], LANES)]


def head_sums(blocks, ones):
    n = len(blocks) // 2
    sides = [functools.reduce(jnp.add, blocks[h * n : (h + 1) * n]) for h in range(2)]
    s = dot(jnp.concatenate(sides, axis=1).astype(BF16), ones)
    return [s[:, :LANES]] * n + [s[:, LANES:]] * n


def softmax(scores, keys, queries, ones):
    blocks = [jnp.where(keys, b, -1e30) for b in blocks_of(scores)]
    n = len(blocks) // 2
    tops = []
    for h in range(2):
        top = functools.reduce(jnp.maximum, blocks[h * n : (h + 1) * n])
        tops += [jnp.max(top, axis=-1, keepdims=True)] * n
    blocks = [jnp.exp(b - t) for b, t in zip(blocks, tops)]
    sums = head_sums(blocks, ones)
    weights = [1.0 / sums[0]] * n + [1.0 / sums[n]] * n
    out = [jnp.where(queries, b * w, 0.0).astype(BF16) for b, w in zip(blocks, weights)]
    return jnp.concatenate(out, axis=1)


def put_window(ref, start, lanes, value):
    head = pl.ds(start, 16)
    ref[head, lanes] = ref[head, lanes] + value[:16]
    ref[pl.ds(start + 16, QUERY - 16), lanes] = value[16:QUERY]


def pair_lanes(part, p, width):
    return slice(part * width + p * LANES, part * width + (p + 1) * LANES)


def loop_groups(count, group):
    if count == 1:
        group(0, 0)
    else:
        lax.fori_loop(0, count, group, 0)


def attend(images, vis, query, key, value, chance, mixed):
    width = mixed.shape[1]
    pairs = width // LANES
    low = low_lanes()
    ones = same_head()
    lane = lax.broadcasted_iota(jnp.int32, (QUERY, LANES), 1)
    row = lax.broadcasted_iota(jnp.int32, (QUERY, LANES), 0)
    mixed[0:16, :] = jnp.zeros((16, width), BF16)

    def group(g, carry):
        units = [(g * GROUP + n, p) for n in range(GROUP) for p in range(pairs)]
        scores = [dot(query(window(i), p), stack_heads(key(window(i), p), low), 1, 1) for i, p in units]
        chosen = []
        for (i, p), s in zip(units, scores):
            keys = (lane >= 2 * i) & (lane < 2 * i + vis)
            queries = (row >= 2 * i) & (row < 2 * i + vis)
            chosen.append(softmax(s, keys, queries, ones))
        outs = [dot(c, stack_heads(value(window(i), p), low)).astype(BF16) for (i, p), c in zip(units, chosen)]
        for (i, p), c, o in zip(units, chosen, outs):
            chance[i * pairs + p] = c
            put_window(mixed, window(i), pair_lanes(0, p, width), o)
        return carry

    loop_groups(images // GROUP, group)


def attend_back(images, query, key, value, chance, d_mixed, put_query, put_key, put_value, group_size):
    width = d_mixed.shape[1]
    pairs = width // LANES
    low = low_lanes()
    low_q = low[:QUERY]
    ones = same_head()

    def merge(stack):
        n = stack.shape[0] // (2 * KEYS)
        return [
            jnp.where(
                low_q, stack[b * KEYS : b * KEYS + QUERY], stack[(n + b) * KEYS : (n + b) * KEYS + QUERY]
            ).astype(BF16)
            for b in range(n)
        ]

    def group(g, carry):
        units = [(g * group_size + n, p) for n in range(group_size) for p in range(pairs)]
        d_chance, d_value = [], []
        for i, p in units:
            grad = d_mixed[pl.ds(window(i), QUERY), pair_lanes(0, p, width)]
            d_chance.append(dot(grad, stack_heads(value(window(i), p), low), 1, 1))
            d_value.append(dot(chance[i * pairs + p], grad, 0, 0))
        d_score = []
        for (i, p), d in zip(units, d_chance):
            c = blocks_of(chance[i * pairs + p].astype(F32))
            t = [x * y for x, y in zip(c, blocks_of(d))]
            sums = head_sums(t, ones)
            d_score.append(jnp.concatenate([a - b * s for a, b, s in zip(t, c, sums)], axis=1).astype(BF16))
        d_query, d_key = [], []
        for (i, p), d in zip(units, d_score):
            at = window(i)
            d_query.append((dot(d, stack_heads(key(at, p), low)) * HEAD_DIM**-0.5).astype(BF16))
            d_key.append(dot(d, query(at, p), 0, 0))
        for (i, p), q, k, v in zip(units, d_query, d_key, d_value):
            at = window(i)
            put_query(at, p, q)
            put_key(at, p, merge(k))
            put_value(at, p, merge(v))
        return carry

    loop_groups(images // group_size, group)


def feed_forward(act, first, bias, second, hid, slope):
    out = None
    for side in range(2):
        half = first[side].shape[1]
        to = slice(side * half, (side + 1) * half)
        h, g = gelu_pair(dot(act[...], first[side][...]) + bias[side][...].reshape(1, half))
        h = h.astype(BF16)
        hid[:, to] = h
        slope[:, to] = g.astype(BF16)
        part = dot(h, second[side][...])
        out = part if out is None else out + part
    return out


def feed_forward_slopes(d_low, second, slope, d_before):
    half = second[0].shape[0]
    for side in range(2):
        to = slice(side * half, (side + 1) * half)
        grad = dot(d_low[...], second[side][...], 1, 1)
        d_before[:, to] = (grad * slope[:, to].astype(F32)).astype(BF16)


def feed_forward_back(d_low, act_t, first, hid, d_before, outs, bias, rest):
    width, half = first[0].shape
    grad = dot(d_before[:, 0:half], first[0][...], 1, 1) + dot(d_before[:, half:], first[1][...], 1, 1)
    sends = rest(grad)
    for side in range(2):
        to = slice(side * half, (side + 1) * half)
        out = outs[side].ref
        out[half:, :] = dot(hid[:, to], d_low[...], 0, 0).astype(BF16)
        g = dot(act_t[...], d_before[:, to])
        for c in range(half // width):
            cols = slice(c * width, (c + 1) * width)
            out[cols, :] = g[:width, cols].astype(BF16)
            bias(side * (half // width) + c, g[width : width + 1, cols])
        for send in (*sends, outs[side]):
            send.send()
        sends = ()


def transposed(act):
    return jnp.concatenate([act.T, jnp.ones((16, act.shape[0]), BF16)], axis=0)


class Load:
    def __init__(self, src, ref, sem):
        self.copy, self.ref, self.pending = pltpu.make_async_copy(src, ref, sem), ref, True
        self.copy.start()

    def __call__(self):
        if self.pending:
            self.pending = False
            self.copy.wait()
        return self.ref


class Store:
    def __init__(self, dst, ref, sems):
        self.ref, self.sent = ref, False
        rows = ref.shape[0] // len(dst)
        self.copies = [
            pltpu.make_async_copy(ref if len(dst) == 1 else ref.at[pl.ds(k * rows, rows), :], to, sem)
            for k, (to, sem) in enumerate(zip(dst, sems))
        ]

    def send(self):
        self.sent = True
        for copy in self.copies:
            copy.start()

    def wait(self):
        for copy in self.copies:
            copy.wait()


def run(kernel, name, ins, outs, scratch, flops=0, after=(), limit=VMEM_LIMIT):
    arrays, specs, extra, copies = [], [], [], 0
    near = pl.BlockSpec(memory_space=pl.ANY)
    far = pl.BlockSpec(memory_space=pltpu.HBM)
    if limit == VMEM_LIMIT:
        near = far
    for kind, *given in ins:
        if kind == "heads":
            arrays += given
            specs += [near] * 2
            own = given[0]
            lead = own.shape[0] if own.ndim == 3 else 1
            extra.append(pltpu.VMEM((2 * lead * own.shape[-2], own.shape[-1]), own.dtype))
            copies += 2 * lead
        elif kind == "parts":
            arrays += given
            specs += [near] * len(given)
            count = sum(a.shape[0] for a in given)
            extra.append(pltpu.VMEM((count, given[0].shape[1]), given[0].dtype))
            copies += len(given)
        elif kind == "rows":
            arrays.append(given[0])
            specs.append(far)
            extra.append(pltpu.VMEM((given[0].shape[0] // 2, given[0].shape[1]), given[0].dtype))
            copies += 1
        elif kind == "near":
            arrays.append(given[0])
            specs.append(pl.BlockSpec(memory_space=pltpu.VMEM))
        elif kind in ("load", "far"):
            arrays.append(given[0])
            specs.append(near if kind == "load" else far)
            extra.append(pltpu.VMEM(given[0].shape, given[0].dtype))
            copies += 1
        else:
            arrays.append(given[0])
            specs.append(far if kind == "hbm" else pl.BlockSpec(memory_space=pltpu.VMEM))
    arrays += after
    specs += [pl.BlockSpec(memory_space=pltpu.VMEM)] * len(after)
    shapes, splits = [], []
    for shape, dtype, *more in outs:
        split = (more or [1])[0]
        splits.append(split)
        if split == "hbm":
            shapes.append(jax.ShapeDtypeStruct(shape, dtype))
            continue
        shapes += [jax.ShapeDtypeStruct((shape[0] // split, *shape[1:]), dtype)] * split
        extra.append(pltpu.VMEM(shape, dtype))
        copies += split
    out_specs = [pl.BlockSpec(memory_space=pl.ANY)] * len(shapes) + [pl.BlockSpec(memory_space=pltpu.VMEM)]
    shapes.append(jax.ShapeDtypeStruct((8, LANES), F32))

    def whole(*refs):
        refs = list(refs)
        n_in, n_out = len(arrays), len(shapes)
        in_refs, out_refs, rest = refs[:n_in], refs[n_in : n_in + n_out], refs[n_in + n_out :]
        scratch_refs, rest, sems = rest[: len(scratch)], rest[len(scratch) : -1], rest[-1]
        counter = iter(range(copies))
        handles, loads = [], []

        def load(src, ref):
            loads.append(Load(src, ref, sems.at[next(counter)]))
            return loads[-1]

        for kind, *given in ins:
            if kind == "heads":
                own, oth = in_refs.pop(0), in_refs.pop(0)
                ref = rest.pop(0)
                size = given[0].shape[-2]
                parts = []
                lead = given[0].shape[0] if given[0].ndim == 3 else None
                for k in range(lead or 1):
                    for side, src in enumerate((own, oth)):
                        to = ref.at[pl.ds((2 * k + side) * size, size), :]
                        parts.append(load(src if lead is None else src.at[k], to))

                def joined(parts=parts, ref=ref):
                    for p in parts:
                        p()
                    return ref

                handles.append(joined)
            elif kind == "parts":
                ref = rest.pop(0)
                parts, at = [], 0
                for a in given:
                    parts.append(load(in_refs.pop(0), ref.at[pl.ds(at, a.shape[0]), :]))
                    at += a.shape[0]

                def joined(parts=parts, ref=ref):
                    for p in parts:
                        p()
                    return ref

                handles.append(joined)
            elif kind == "rows":
                ref = rest.pop(0)
                count = ref.shape[0]
                start = pl.multiple_of(lax.axis_index("tp") * count, 8)
                handles.append(load(in_refs.pop(0).at[pl.ds(start, count), :], ref))
            elif kind == "near":
                handles.append(functools.partial(lambda ref: ref, in_refs.pop(0)))
            elif kind in ("load", "far"):
                handles.append(load(in_refs.pop(0), rest.pop(0)))
            else:
                handles.append(in_refs.pop(0))
        results, stores = [], []
        for split in splits:
            if split == "hbm":
                results.append(out_refs.pop(0))
                continue
            dst = [out_refs.pop(0) for _ in range(split)]
            stores.append(Store(dst, rest.pop(0), [sems.at[next(counter)] for _ in dst]))
            results.append(stores[-1])
        out_refs[0][...] = jnp.zeros((8, LANES), F32)
        kernel(handles, results, scratch_refs)
        for item in loads:
            item()
        for store in stores:
            if not store.sent:
                store.send()
        for store in stores:
            store.wait()

    moved = sum(a.size * a.dtype.itemsize for a in (*arrays, *shapes)) if flops else 0
    return pl.pallas_call(
        whole,
        name=name,
        out_shape=shapes,
        in_specs=specs,
        out_specs=out_specs,
        scratch_shapes=[*scratch, *extra, pltpu.SemaphoreType.DMA((copies,))],
        compiler_params=pltpu.CompilerParams(vmem_limit_bytes=limit),
        cost_estimate=pl.CostEstimate(flops=flops, bytes_accessed=moved, transcendentals=0),
    )(*arrays)


def pair_bias(own, other, k, first=0):
    at = first + k
    return jnp.concatenate([own[k : k + 1, :], other[at : at + 1, :]], axis=-1)


def enc_attn_kernel(vis, ins, outs, scratch):
    x, weight, proj, own_bias, oth_bias, gains, shifts = ins
    x1, act, qkv, chance, mixed, branch = outs
    rows, width = x1.ref.shape
    x_rows = x()
    unit, _ = unit_rows(x_rows[...].astype(F32))
    act.ref[...] = (unit * gains[0:1, :] + shifts[0:1, :]).astype(BF16)
    w = weight()
    none = jnp.zeros((1, width), F32)
    bias = jnp.concatenate([pair_bias(own_bias, oth_bias, 0), none, pair_bias(own_bias, oth_bias, 1)], axis=1)
    qkv.ref[rows:, :] = jnp.zeros((16, 3 * width), BF16)
    for k in range(3):
        cols = slice(k * width, (k + 1) * width)
        out = dot(act.ref[...], w[cols, :], 1, 1) + bias[:, cols]
        qkv.ref[0:rows, cols] = (out * HEAD_DIM**-0.5 if k == 0 else out).astype(BF16)
    act.send()
    qkv.send()
    attend(
        rows // vis, vis,
        lambda at, p: qkv.ref[pl.ds(at, QUERY), pair_lanes(0, p, width)],
        lambda at, p: [qkv.ref[pl.ds(at, KEYS), pair_lanes(1, p, width)]],
        lambda at, p: [qkv.ref[pl.ds(at, KEYS), pair_lanes(2, p, width)]],
        chance.ref, mixed.ref,
    )
    proj_rows = proj()
    chance.send()
    mixed.send()
    u = dot(mixed.ref[...], proj_rows[...])
    branch.ref[...] = u.astype(BF16)
    x1.ref[...] = x_rows[...].astype(F32) + gains[2:3, :] * (u + shifts[2:3, :])


def one_hots(order, rows, vis):
    images, patches = order.shape
    shape = (rows, patches)
    row = lax.broadcasted_iota(jnp.int32, shape, 0)
    lane = lax.broadcasted_iota(jnp.int32, shape, 1)
    start = lax.broadcasted_iota(jnp.int32, (rows, images), 1) * vis
    own = lax.broadcasted_iota(jnp.int32, (rows, images), 0) - start
    image = jnp.where((own >= 0) & (own < vis), 1.0, 0.0).astype(BF16)
    picked = dot(image, order[...].astype(F32).astype(BF16))
    first = jnp.zeros(shape, jnp.int32)
    for i in range(1, images):
        first = jnp.where(row >= i * vis, i * vis, first)
    place = row - first
    out = []
    for at in (place, place + vis):
        index = jnp.sum(jnp.where(lane == at, picked, 0.0), axis=-1, keepdims=True)
        out.append(jnp.where(lane.astype(F32) == index, 1.0, 0.0).astype(BF16))
    return out


def middle_kernel(vis, ins, outs, scratch):
    (x1, own_fc1, oth_fc1, own_b1, oth_b1, own_fc2, oth_fc2, gains, shifts,
     order, pos, token, weight, proj, own_bias, oth_bias,
     reg_own_fc1, reg_oth_fc1, reg_own_b1, reg_oth_b1, reg_own_fc2, reg_oth_fc2, cot,
     reg_gains, reg_shifts) = ins
    (encoded, act2_t, hid2, slope2, branch2, context, act3, act4, query, kv, chance, mixed, branch3,
     predicted, d_state, own_out, oth_out, small) = outs
    act_s, act5_t, hid, slope, d_before, y1, d_low = scratch
    rows, width = d_state.ref.shape

    state = x1()[...]
    unit, _ = unit_rows(state)
    act = (unit * gains[1:2, :] + shifts[1:2, :]).astype(BF16)
    act_s[...] = act
    act2_t.ref[...] = transposed(act)
    first, second = (own_fc1(), oth_fc1()), (own_fc2(), oth_fc2())
    order, w = order(), weight()
    half = own_b1.shape[0]
    oth_b1, reg_oth_b1 = oth_b1.at[pl.ds(0, half)], reg_oth_b1.at[pl.ds(half, half)]
    u = feed_forward(act_s, first, (own_b1, oth_b1), second, hid2.ref, slope2.ref)
    branch2.ref[...] = u.astype(BF16)
    state = state + gains[3:4, :] * (u + shifts[3:4, :])
    encoded.ref[...] = state.astype(BF16)

    high = pos[...].astype(BF16)
    rest = (pos[...] - high.astype(F32)).astype(BF16)
    table = jnp.concatenate([high, rest], axis=1)
    seen, masked = one_hots(order, rows, vis)
    picked = dot(seen, table)
    c = state + (picked[:, :width] + picked[:, width:])
    context.ref[0:rows, :] = c
    unit, _ = unit_rows(c)
    act4.ref[0:rows, :] = (unit * reg_gains[1:2, :] + reg_shifts[1:2, :]).astype(BF16)
    picked = dot(masked, table)
    z = token[...].reshape(1, width) + (picked[:, :width] + picked[:, width:])
    context.ref[rows:, :] = z
    unit, _ = unit_rows(z)
    act3.ref[...] = (unit * reg_gains[0:1, :] + reg_shifts[0:1, :]).astype(BF16)
    act4.ref[rows:, :] = (unit * reg_gains[1:2, :] + reg_shifts[1:2, :]).astype(BF16)

    q = dot(act3.ref[...], w[0:width, :], 1, 1) + pair_bias(own_bias, oth_bias, 0, 2)
    query.ref[...] = (q * HEAD_DIM**-0.5).astype(BF16)
    kv.ref[2 * rows :, :] = jnp.zeros((16, 2 * width), BF16)
    bias_v = jnp.concatenate([jnp.zeros((1, width), F32), pair_bias(own_bias, oth_bias, 1, 2)], axis=1)
    kv.ref[0 : 2 * rows, :] = (dot(act4.ref[...], w[width:, :], 1, 1) + bias_v).astype(BF16)
    for out in (hid2, slope2, act2_t, branch2, encoded, context, act3, act4, query, kv):
        out.send()
    attend(
        rows // vis, vis,
        lambda at, p: query.ref[pl.ds(at, QUERY), pair_lanes(0, p, width)],
        functools.partial(context_windows, kv.ref, rows, width, 0),
        functools.partial(context_windows, kv.ref, rows, width, 1),
        chance.ref, mixed.ref,
    )
    first, second = (reg_own_fc1(), reg_oth_fc1()), (reg_own_fc2(), reg_oth_fc2())
    proj_rows, cot_rows = proj(), cot()
    chance.send()
    mixed.send()
    u = dot(mixed.ref[...], proj_rows[...])
    branch3.ref[...] = u.astype(BF16)
    state = context.ref[rows:, :] + reg_gains[3:4, :] * (u + reg_shifts[3:4, :])
    y1[...] = state

    unit, _ = unit_rows(state)
    act = (unit * reg_gains[2:3, :] + reg_shifts[2:3, :]).astype(BF16)
    act_s[...] = act
    act5_t[...] = transposed(act)
    u = feed_forward(act_s, first, (reg_own_b1, reg_oth_b1), second, hid, slope)
    branch = u + reg_shifts[4:5, :]
    predicted.ref[...] = (y1[...] + reg_gains[4:5, :] * branch).astype(BF16)
    grad = cot_rows[...].astype(F32)
    d_low[...] = (grad * reg_gains[4:5, :]).astype(BF16)
    small.ref[...] = jnp.zeros(small.ref.shape, F32)
    small.ref[0:1, :] = total(grad * branch)
    small.ref[1:2, :] = total(grad) * reg_gains[4:5, :]

    def bias(k, row):
        small.ref[8 + k : 9 + k, :] = row

    feed_forward_slopes(d_low, second, slope, d_before)
    def rest(grad):
        unit, scale = unit_rows(y1[...])
        small.ref[2:3, :] = total(grad * unit)
        small.ref[3:4, :] = total(grad)
        d_state.ref[...] = cot_rows[...].astype(F32) + norm_back(grad * reg_gains[2:3, :], unit, scale)
        return predicted, branch3, d_state

    feed_forward_back(d_low, act5_t, first, hid, d_before, (own_out, oth_out), bias, rest)


def context_windows(kv, rows, width, part, at, p):
    lanes = pair_lanes(part, p, width)
    return [kv[pl.ds(at, KEYS), lanes], kv[pl.ds(aligned(rows + at), KEYS), lanes]]


def pack_small(small, outs, bias_q, bias_v, ffn_small, at):
    width = small.shape[1]
    half = width // 2
    for side, out in enumerate(outs):
        lanes = slice(side * half, (side + 1) * half)
        small[at : at + 1, 0:half] = bias_q[:, lanes]
        small[at + 1 : at + 2, 0:half] = bias_v[:, lanes]
        small[at + 2 : at + 4, :] = ffn_small[8 + 2 * side : 10 + 2 * side, :]
        out[2 * width : 2 * width + small.shape[0], :] = small[...].astype(BF16)


def split_heads(grad, outs, first):
    width = grad.shape[1]
    half = width // 2
    for k in range(grad.shape[0] // width):
        for side, out in enumerate(outs):
            at = k * width + side * half
            out[(first + k) * half : (first + k + 1) * half, :] = grad[at : at + half].astype(BF16)


def reg_attn_back_kernel(vis, patches, ins, outs, scratch):
    (d_state, branch, proj, mixed, chance, kv, query, weight, act3, act4, context, order, cot, gains, shifts, ffn_small) = ins
    d_enc, own, oth = outs
    d_low, d_mixed, d_query, d_kv, d_ctx, small = scratch
    rows, width = d_enc.ref.shape
    half = width // 2
    packs = (own.ref, oth.ref)
    grad = d_state()[...]
    small[...] = jnp.zeros_like(small)
    small[3:4, :] = total(grad * (branch()[...].astype(F32) + shifts[3:4, :]))
    small[8:9, :] = total(grad) * gains[3:4, :]
    d_low[...] = (grad * gains[3:4, :]).astype(BF16)
    d_mixed[...] = dot(d_low[...], proj()[...], 1, 1).astype(BF16)
    g = dot(mixed()[...], d_low[...], 0, 0)
    for side, out in enumerate(packs):
        out[3 * half : 2 * width, :] = g[side * half : (side + 1) * half].astype(BF16)
    d_query[0:16, :] = jnp.zeros((16, width), BF16)
    d_kv[0:16, :] = jnp.zeros((16, 2 * width), BF16)
    d_kv[rows : rows + 16, :] = jnp.zeros((16, 2 * width), BF16)

    def put_context(part, at, p, blocks):
        lanes = pair_lanes(part, p, width)
        put_window(d_kv, at, lanes, blocks[0])
        put_window(d_kv, aligned(rows + at), lanes, blocks[1])

    q, keys, chances = query(), kv(), chance()
    attend_back(
        rows // vis,
        lambda at, p: q[pl.ds(at, QUERY), pair_lanes(0, p, width)],
        functools.partial(context_windows, keys, rows, width, 0),
        functools.partial(context_windows, keys, rows, width, 1),
        chances, d_mixed,
        lambda at, p, v: put_window(d_query, at, pair_lanes(0, p, width), v),
        functools.partial(put_context, 0),
        functools.partial(put_context, 1),
        GROUP,
    )
    w, a3, a4, ctx, cot_rows, order = weight(), act3(), act4(), context(), cot(), order()
    split_heads(dot(d_query[...], a3[...], 0, 0), packs, 0)
    split_heads(dot(d_kv[...], a4[...], 0, 0), packs, 1)
    bias_q = total(d_query[...].astype(F32))
    bias_v = total(d_kv[:, width:].astype(F32))
    grad4 = dot(d_kv[...], w[width:, :])
    grad3 = dot(d_query[...], w[0:width, :])
    unit, scale = unit_rows(ctx[0:rows, :])
    gain_sum = total(grad4[:rows] * unit)
    d_c = norm_back(grad4[:rows] * gains[1:2, :], unit, scale)
    high = d_c.astype(BF16)
    d_ctx[0:rows, 0:width] = high
    d_ctx[0:rows, width:] = (d_c - high.astype(F32)).astype(BF16)
    d_enc.ref[...] = cot_rows[...].astype(F32) + d_c
    unit, scale = unit_rows(ctx[rows:, :])
    small[0:1, :] = total(grad3 * unit)
    small[1:2, :] = gain_sum + total(grad4[rows:] * unit)
    small[5:6, :] = total(grad3)
    small[6:7, :] = total(grad4)
    d_z = d_state()[...] + norm_back(grad3 * gains[0:1, :] + grad4[rows:] * gains[1:2, :], unit, scale)
    small[10:11, :] = total(d_z)
    high = d_z.astype(BF16)
    d_ctx[rows:, 0:width] = high
    d_ctx[rows:, width:] = (d_z - high.astype(F32)).astype(BF16)
    seen, masked = one_hots(order, rows, vis)
    both = dot(seen, d_ctx[0:rows, :], 0, 0) + dot(masked, d_ctx[rows:, :], 0, 0)
    small[2:3, :] = ffn_small[2:3, :]
    small[4:5, :] = ffn_small[0:1, :]
    small[7:8, :] = ffn_small[3:4, :]
    small[9:10, :] = ffn_small[1:2, :]
    pack_small(small, packs, bias_q, bias_v, ffn_small, 11)
    after = 2 * width + small.shape[0]
    d_pos = (both[:, 0:width] + both[:, width:]).astype(BF16)
    pad = jnp.zeros((own.ref.shape[0] - after - patches, width), BF16)
    for out in packs:
        out[after:, :] = jnp.concatenate([d_pos, pad], axis=0)


def enc_ffn_back_kernel(ins, outs, scratch):
    (d_enc, branch, own_fc2, oth_fc2, slope, hid, act_t, own_fc1, oth_fc1, x1, gains, shifts) = ins
    d_state, small, own_out, oth_out = outs
    d_low, d_before = scratch
    grad = d_enc()[...]
    small.ref[...] = jnp.zeros(small.ref.shape, F32)
    small.ref[0:1, :] = total(grad * (branch()[...].astype(F32) + shifts[3:4, :]))
    small.ref[1:2, :] = total(grad) * gains[3:4, :]
    d_low[...] = (grad * gains[3:4, :]).astype(BF16)

    def bias(k, row):
        small.ref[8 + k : 9 + k, :] = row

    feed_forward_slopes(d_low, (own_fc2(), oth_fc2()), slope(), d_before)
    hid, act_t, first, x1_rows = hid(), act_t(), (own_fc1(), oth_fc1()), x1()

    def rest(grad):
        unit, scale = unit_rows(x1_rows[...])
        small.ref[2:3, :] = total(grad * unit)
        small.ref[3:4, :] = total(grad)
        d_state.ref[...] = d_enc()[...] + norm_back(grad * gains[1:2, :], unit, scale)
        return (d_state,)

    feed_forward_back(d_low, act_t, first, hid, d_before, (own_out, oth_out), bias, rest)


def enc_attn_back_kernel(vis, ins, outs, scratch):
    (d_state, branch, proj, mixed, chance, qkv, weight, act, x, gains, shifts, ffn_small) = ins
    d_input, own, oth = outs
    d_low, d_mixed, d_qkv, small = scratch
    rows, width = d_input.ref.shape
    half = width // 2
    packs = (own.ref, oth.ref)
    grad = d_state()[...]
    small[...] = jnp.zeros_like(small)
    small[2:3, :] = total(grad * (branch()[...].astype(F32) + shifts[2:3, :]))
    small[6:7, :] = total(grad) * gains[2:3, :]
    d_low[...] = (grad * gains[2:3, :]).astype(BF16)
    d_mixed[...] = dot(d_low[...], proj()[...], 1, 1).astype(BF16)
    g = dot(mixed()[...], d_low[...], 0, 0)
    for side, out in enumerate(packs):
        out[3 * half : 2 * width, :] = g[side * half : (side + 1) * half].astype(BF16)
    d_qkv[0:16, :] = jnp.zeros((16, 3 * width), BF16)
    s = qkv()
    attend_back(
        rows // vis,
        lambda at, p: s[pl.ds(at, QUERY), pair_lanes(0, p, width)],
        lambda at, p: [s[pl.ds(at, KEYS), pair_lanes(1, p, width)]],
        lambda at, p: [s[pl.ds(at, KEYS), pair_lanes(2, p, width)]],
        chance(), d_mixed,
        lambda at, p, v: put_window(d_qkv, at, pair_lanes(0, p, width), v),
        lambda at, p, v: put_window(d_qkv, at, pair_lanes(1, p, width), v[0]),
        lambda at, p, v: put_window(d_qkv, at, pair_lanes(2, p, width), v[0]),
        GROUP,
    )
    act, w, x_rows = act(), weight(), x()
    grad = dot(d_qkv[...], w[...])
    split_heads(dot(d_qkv[...], act[...], 0, 0), packs, 0)
    bias_q = total(d_qkv[:, 0:width].astype(F32))
    bias_v = total(d_qkv[:, 2 * width :].astype(F32))
    unit, scale = unit_rows(x_rows[...].astype(F32))
    small[0:1, :] = total(grad * unit)
    small[4:5, :] = total(grad)
    small[1:2, :] = ffn_small[2:3, :]
    small[3:4, :] = ffn_small[0:1, :]
    small[5:6, :] = ffn_small[3:4, :]
    small[7:8, :] = ffn_small[1:2, :]
    pack_small(small, packs, bias_q, bias_v, ffn_small, 8)
    pad = jnp.zeros((own.ref.shape[0] - 2 * width - small.shape[0], width), BF16)
    for out in packs:
        out[2 * width + small.shape[0] :, :] = pad
    d_input.ref[...] = d_state()[...] + norm_back(grad * gains[0:1, :], unit, scale)


def step_bits():
    if plain():
        return [jnp.int32(0), jnp.int32(0)]
    x, y, core = lax.axis_index("x"), lax.axis_index("y"), lax.axis_index("tp")
    return [jnp.where(core == 0, x, y), jnp.where(core == 0, y, x)]


def place_quarters(parts, whole):
    size = whole.shape[0] // 4
    first, second = step_bits()
    pieces = len(parts) // 4
    size = size // pieces
    for k, (a, b) in enumerate(((0, 0), (0, 1), (1, 0), (1, 1))):
        at = ((first ^ a) * 2 + (second ^ b)) * pieces * size
        for j, part in enumerate(parts[k * pieces : (k + 1) * pieces]):
            whole[pl.ds(pl.multiple_of(at + j * size, 16), size), :] = part()[...]


def sum_rows(a, b):
    return (a.astype(F32) + b.astype(F32)).astype(BF16)


def halve_kernel(step, counts, *refs):
    *ins, _, keep, send, token = refs
    token[...] = jnp.zeros((8, LANES), F32)
    bit = step_bits()[step]

    def write(keep_half):
        rest, to = list(ins), 0
        for count in counts:
            mine, got, rest = rest[0], rest[1 : 1 + count], rest[1 + count :]
            half = mine.shape[0] // 2
            size = min(half, got[0].shape[0])
            for out, b in ((send, 1 - keep_half), (keep, keep_half)):
                for at in range(b * half, (b + 1) * half, size):
                    piece, first = divmod(at, got[0].shape[0])
                    where = slice(to + at - b * half, to + at - b * half + size)
                    out[where, :] = sum_rows(mine[at : at + size, :], got[piece][first : first + size, :])
            to += half

    for b in range(2):
        pl.when(bit == b)(functools.partial(write, b))


def piece_rows(refs, at, size):
    for ref in refs:
        if at < ref.shape[0]:
            return ref[at : at + size, :]
        at -= ref.shape[0]


def add_kernel(n_mine, n_got, *refs):
    mine, got, outs = refs[:n_mine], refs[n_mine : n_mine + n_got], refs[n_mine + n_got + 1 : -1]
    refs[-1][...] = jnp.zeros((8, LANES), F32)
    at = 0
    for out in outs:
        size = min(r.shape[0] for r in (out, *mine, *got))
        for to in range(0, out.shape[0], size):
            out[to : to + size, :] = sum_rows(piece_rows(mine, at, size), piece_rows(got, at, size))
            at += size


def fc_out(first, second, grad1, grad2):
    width, half = grad1.ref.shape
    grad2.ref[...] = second.astype(F32)
    grad2.send()
    for c in range(half // width):
        grad1.ref[:, c * width : (c + 1) * width] = first[c * width : (c + 1) * width].astype(F32)
    grad1.send()


def heads_out(first, second, grad_qkv, grad_proj, rest):
    half = grad_proj.ref.shape[0]
    count = first.shape[0]
    grad_qkv.ref[0:count, :] = first.astype(F32)
    grad_qkv.ref[count:, :] = second[: 3 * half - count].astype(F32)
    grad_qkv.send()
    grad_proj.ref[...] = second[3 * half - count : 4 * half - count].astype(F32)
    grad_proj.send()
    rest.ref[...] = second[4 * half - count :].astype(F32)
    rest.send()


def both_cores(mine, got, out, sems):
    rows = mine.shape[0]
    core = lax.axis_index("tp")
    copies = []
    for src, at, sem in ((mine, core, 0), (got, 1 - core, 1)):
        to = out.at[pl.ds(pl.multiple_of(at * rows, 16), rows), :]
        copies.append(pltpu.make_async_copy(src, to, sems.at[sem]))
        copies[-1].start()
    return copies


def out_ab_kernel(ins, outs, scratch):
    *parts, encoded, got_encoded, predicted, got_predicted = ins
    encoded_out, predicted_out, *grads = outs
    whole, sems, more = scratch
    copies = both_cores(encoded, got_encoded, encoded_out, sems)
    copies += both_cores(predicted, got_predicted, predicted_out, more)
    place_quarters(parts, whole)
    side = whole.shape[0] // 2
    of_a = grads[1].ref.shape[0]
    fc_out(whole[0:of_a, :], whole[side : side + of_a, :], *grads[:2])
    heads_out(whole[of_a:side, :], whole[side + of_a :, :], *grads[2:])
    for copy in copies:
        copy.wait()


def out_c_kernel(ins, outs, scratch):
    *parts, d_input, got_input = ins
    input_out, *grads = outs
    whole, sems = scratch
    copies = both_cores(d_input, got_input, input_out, sems)
    place_quarters(parts, whole)
    side = whole.shape[0] // 2
    fc_out(whole[0:side, :], whole[side:, :], *grads)
    for copy in copies:
        copy.wait()


def out_d_kernel(ins, outs, scratch):
    place_quarters(ins, scratch[0])
    side = scratch[0].shape[0] // 2
    heads_out(scratch[0][0:side, :], scratch[0][side:, :], *outs)


def small_kernel(ins, outs, scratch):
    own_b, got_b, own_d, got_d = ins
    gains_b, shifts_b, token, pos, bias_b, fc_b, gains_d, shifts_d, bias_d, fc_d = outs
    mean = (own_b[...] + got_b[...]) * 0.5
    half = bias_b.ref.shape[1]
    width = 2 * half
    gains_b.ref[...] = mean[0:5]
    shifts_b.ref[...] = mean[5:10]
    token.ref[...] = mean[10, :]
    bias_b.ref[...] = own_b[11:13, 0:half]
    for k in range(2):
        fc_b.ref[k * width : (k + 1) * width] = own_b[13 + k, :]
    pos.ref[...] = mean[32 : 32 + pos.ref.shape[0]]
    mean = (own_d[...] + got_d[...]) * 0.5
    gains_d.ref[...] = mean[0:4]
    shifts_d.ref[...] = mean[4:8]
    bias_d.ref[...] = own_d[8:10, 0:half]
    for k in range(2):
        fc_d.ref[k * width : (k + 1) * width] = own_d[10 + k, :]


CHIPS = ("z", "y", "x")
ORDERS = ((0, 1, 2, 3), (1, 0, 3, 2))


def plain():
    return "dp" in jax.sharding.get_abstract_mesh().axis_names


def swap(a):
    return lax.ppermute(a, "tp", [(0, 1), (1, 0)])


def flip(a, step):
    pairs = [
        (2 * d + t, 2 * (d ^ (1 << ORDERS[t][step])) + t) for d in range(16) for t in range(2)
    ]
    return lax.ppermute(a, (*CHIPS, "tp"), pairs)


def flips(pieces, step):
    return [flip(p, step) for p in pieces]


def gathered(part):
    other = flips(part, 1)
    return [*part, *other, *flips(part, 0), *flips(other, 0)]


def quarters_of(whole):
    size = whole.shape[0] // 4
    return [whole[k * size : (k + 1) * size] for k in range(4)]


def add_up(own, oth):
    return lax.psum(own.astype(F32) + swap(oth).astype(F32), "dp").astype(BF16)


def body(
    x_visible,
    patch_order,
    enc_qkv,
    enc_head_bias,
    enc_proj,
    enc_fc1,
    enc_fc1_bias,
    enc_fc2,
    enc_gains,
    enc_shifts,
    reg_qkv,
    reg_head_bias,
    reg_proj,
    reg_fc1,
    reg_fc1_bias,
    reg_fc2,
    reg_gains,
    reg_shifts,
    pos_embed,
    mask_token,
    enc_cot,
    reg_cot,
):
    all_images, patches = patch_order.shape
    width = x_visible.shape[1]
    vis = x_visible.shape[0] // all_images
    images = all_images // 2
    rows = images * vis
    hidden = 2 * enc_fc1.shape[1]
    half = width // 2
    pairs = width // LANES
    enc_qkv, reg_qkv = jnp.swapaxes(enc_qkv, 1, 2), jnp.swapaxes(reg_qkv, 1, 2)
    oth_bias = swap(jnp.concatenate([enc_head_bias, reg_head_bias], axis=0))
    oth_b1 = swap(jnp.concatenate([enc_fc1_bias, reg_fc1_bias]))
    enc_heads = ("heads", enc_qkv, swap(enc_qkv))
    enc_out = ("heads", enc_proj, swap(enc_proj))
    enc_bias = ("vmem", enc_head_bias), ("vmem", oth_bias)
    oth_enc_fc1, oth_enc_fc2 = swap(enc_fc1), swap(enc_fc2)
    reg_heads = ("heads", reg_qkv, swap(reg_qkv))
    reg_out = ("heads", reg_proj, swap(reg_proj))
    reg_bias = ("vmem", reg_head_bias), ("vmem", oth_bias)
    oth_reg_fc1, oth_reg_fc2 = swap(reg_fc1), swap(reg_fc2)
    order = ("rows", patch_order)
    enc_vectors = ("vmem", enc_gains), ("vmem", enc_shifts)
    reg_vectors = ("vmem", reg_gains), ("vmem", reg_shifts)

    last = []

    def step(*given, **more):
        *outs, token = run(*given, after=tuple(last), **more)
        last[:] = [token]
        return outs

    def load(*arrays):
        return [("load", a) for a in arrays]

    def vmem(shape, dtype):
        return pltpu.VMEM(shape, dtype)

    def hbm(*arrays):
        return [("hbm", a) for a in arrays]

    def light(kernel, name, ins, shapes, chain=True):
        whole = pl.BlockSpec(memory_space=pltpu.VMEM)
        ins = [*ins, last[0] if chain else jnp.zeros((8, LANES), F32)]
        outs = [jax.ShapeDtypeStruct(shape, BF16) for shape in shapes]
        *outs, token = pl.pallas_call(
            kernel,
            name=name,
            out_shape=[*outs, jax.ShapeDtypeStruct((8, LANES), F32)],
            in_specs=[whole] * len(ins),
            out_specs=[whole] * (len(outs) + 1),
            compiler_params=pltpu.CompilerParams(vmem_limit_bytes=8 << 20),
            cost_estimate=pl.CostEstimate(flops=0, bytes_accessed=0, transcendentals=0),
        )(*ins)
        last[:] = [token]
        return outs

    def halve(which, *arrays, chain=True):
        pieces = [a if isinstance(a, list) else [a] for a in arrays]
        shape = (sum(a.shape[0] for a in arrays[::2]) // 2, width)
        kernel = functools.partial(halve_kernel, which, [len(p) for p in pieces[1::2]])
        return light(kernel, "halve", [a for p in pieces for a in p], [shape, shape], chain)

    def add(mine, got, pieces):
        rows_in = sum(a.shape[0] for a in mine) // pieces
        kernel = functools.partial(add_kernel, len(mine), len(got))
        return light(kernel, "add", [*mine, *got], [(rows_in, width)] * pieces)

    def near(*arrays):
        return [("near", a) for a in arrays]

    state_f = ((rows, width), F32)
    state_b = ((rows, width), BF16)
    act_t = ((width + 16, rows), BF16)
    wide = ((rows, hidden), BF16)
    layer = 2 * rows * width
    x1, act1, qkv1, chance1, mixed1, branch1 = step(
        functools.partial(enc_attn_kernel, vis),
        "enc_attn",
        [("rows", x_visible), enc_heads, enc_out, *enc_bias, *enc_vectors],
        [state_f, state_b, ((rows + 16, 3 * width), BF16),
         ((images * pairs, QUERY, 2 * KEYS), BF16), state_b, state_b],
        [],
        layer * width * 5,
    )
    stage = ((hidden, width), BF16)
    small = ((16, width), F32)
    (encoded, act2_t, hid2, slope2, branch2, context, act3, act4, query3, kv3, chance3, mixed3, branch3,
     predicted, d_state3, own_a, oth_a, small_a) = step(
        functools.partial(middle_kernel, vis),
        "middle",
        [*load(x1, enc_fc1, oth_enc_fc1), ("vmem", enc_fc1_bias), ("vmem", oth_b1),
         *load(enc_fc2, oth_enc_fc2), *enc_vectors, order, ("vmem", pos_embed),
         ("vmem", mask_token), reg_heads, reg_out, *reg_bias,
         *load(reg_fc1, oth_reg_fc1), ("vmem", reg_fc1_bias), ("vmem", oth_b1),
         *load(reg_fc2, oth_reg_fc2), ("rows", reg_cot), *reg_vectors],
        [state_b, act_t, wide, wide, state_b, ((2 * rows, width), F32), state_b,
         ((2 * rows, width), BF16), state_b, ((2 * rows + 16, 2 * width), BF16),
         ((images * pairs, QUERY, 4 * KEYS), BF16), state_b, state_b,
         state_b, state_f, stage, stage, small],
        [vmem(*state_b), vmem(*act_t), vmem(*wide), vmem(*wide), vmem(*wide), vmem(*state_f),
         vmem(*state_b)],
        layer * (hidden * 8 + width * 8),
    )
    got_a = swap(oth_a)
    got_encoded, got_predicted = swap(encoded), swap(predicted)
    heads_b = ((2 * width + 256, width), BF16)
    d_enc, own_b, *oth_b = step(
        functools.partial(reg_attn_back_kernel, vis, patches),
        "reg_attn_back",
        [*load(d_state3, branch3), reg_out, *load(mixed3, chance3, kv3, query3), reg_heads,
         *load(act3, act4, context), order, ("rows", enc_cot), *reg_vectors, ("vmem", small_a)],
        [state_f, heads_b, (*heads_b, 2)],
        [vmem(*state_b), vmem(*state_b), vmem(*state_b), vmem((2 * rows, 2 * width), BF16),
         vmem((2 * rows, 2 * width), BF16), vmem((32, width), F32)],
        layer * width * 16,
    )
    if not plain():
        keep_ab, send_ab = halve(0, own_a, got_a, own_b, [swap(p) for p in oth_b], chain=False)
        got_ab = flip(send_ab, 0)
    d_state1, small_c, own_c, *oth_c = step(
        enc_ffn_back_kernel,
        "enc_ffn_back",
        [*load(d_enc, branch2, enc_fc2, oth_enc_fc2, slope2, hid2, act2_t, enc_fc1, oth_enc_fc1, x1),
         *enc_vectors],
        [state_f, small, stage, (*stage, 4)],
        [vmem(*state_b), vmem(*wide)],
        layer * hidden * 4,
    )
    if not plain():
        keep_ab, send_ab = halve(1, keep_ab, got_ab)
        got_ab = flip(send_ab, 1)
        keep_c, send_c = halve(0, own_c, [swap(p) for p in oth_c])
        got_c = flip(send_c, 0)
    heads_d = ((2 * width + 64, width), BF16)
    d_input, own_d, *oth_d = step(
        functools.partial(enc_attn_back_kernel, vis),
        "enc_attn_back",
        [*load(d_state1, branch1), enc_out, *load(mixed1, chance1, qkv1), enc_heads, *load(act1),
         ("rows", x_visible), *enc_vectors, ("vmem", small_c)],
        [state_f, heads_d, (*heads_d, 4)],
        [vmem(*state_b), vmem(*state_b), vmem((rows, 3 * width), BF16), vmem((32, width), F32)],
        layer * width * 12,
    )
    got_input = swap(d_input)
    if not plain():
        got_oth_d = [swap(p) for p in oth_d]
        n_ab, n_c = 1, 1
        part_ab = add([keep_ab], [got_ab], n_ab)
        got_ab = flips(part_ab, 2)
        keep_c, send_c = halve(1, keep_c, got_c)
        got_c = flip(send_c, 1)
        keep_d, send_d = halve(0, own_d, got_oth_d)
        got_d = flip(send_d, 0)
        part_c = add([keep_c], [got_c], n_c)
        got_c = flips(part_c, 2)
        part_ab = add(part_ab, got_ab, 2)
        got_ab = flips(part_ab, 3)
        keep_d, send_d = halve(1, keep_d, got_d)
        got_d = flip(send_d, 1)
        part_c = add(part_c, got_c, n_c)
        got_c = flips(part_c, 3)
        part_d = add([keep_d], [got_d], 1)
        got_d = flips(part_d, 2)
        part_ab = add(part_ab, got_ab, n_ab)
        quarters_ab = gathered(part_ab)
        part_d = add(part_d, got_d, 1)
        got_d = flips(part_d, 3)
        part_c = add(part_c, got_c, n_c)
        quarters_c = gathered(part_c)
        part_d = add(part_d, got_d, 1)
        quarters_d = gathered(part_d)
    else:
        sum_a, sum_b = add_up(own_a, oth_a), add_up(own_b, jnp.concatenate(oth_b))
        at_a, at_b = sum_a.shape[0] // 2, sum_b.shape[0] // 2
        whole = jnp.concatenate([sum_a[:at_a], sum_b[:at_b], sum_a[at_a:], sum_b[at_b:]], axis=0)
        quarters_ab = quarters_of(whole)
        quarters_c, quarters_d = quarters_of(add_up(own_c, jnp.concatenate(oth_c))), quarters_of(add_up(own_d, jnp.concatenate(oth_d)))

    def out_shapes(pack):
        if pack is None:
            return [((width, hidden // 2), F32), ((hidden // 2, width), F32)]
        return [((3 * half, width), F32), ((half, width), F32), ((pack[0][0] - 2 * width, width), F32)]

    def pack_scratch(quarters):
        return vmem((sum(q.shape[0] for q in quarters), width), BF16)

    two = pltpu.SemaphoreType.DMA((2,))
    encoded_out, predicted_out, reg_g1, reg_g2, reg_gq, reg_gp, rest_b = step(
        out_ab_kernel,
        "out_ab",
        [*near(*quarters_ab), *hbm(encoded, got_encoded, predicted, got_predicted)],
        [((2 * rows, width), BF16, "hbm")] * 2 + out_shapes(None) + out_shapes(heads_b),
        [pack_scratch(quarters_ab), two, two],
        limit=20 << 20,
    )
    got_rest_b = swap(rest_b)
    input_out, enc_g1, enc_g2 = step(
        out_c_kernel,
        "out_c",
        [*near(*quarters_c), *hbm(d_input, got_input)],
        [((2 * rows, width), F32, "hbm")] + out_shapes(None),
        [pack_scratch(quarters_c), two],
        limit=12 << 20,
    )
    enc_gq, enc_gp, rest_d = step(
        out_d_kernel, "out_d", near(*quarters_d), out_shapes(heads_d), [pack_scratch(quarters_d)],
        limit=8 << 20,
    )
    biases = [((2, half), F32), ((hidden // 2,), F32)]
    (grad_reg_gains, grad_reg_shifts, token, grad_pos, hb_reg, b1_reg, grad_enc_gains, grad_enc_shifts,
     hb_enc, b1_enc) = step(
        small_kernel,
        "small",
        [("vmem", a) for a in (rest_b, got_rest_b, rest_d, swap(rest_d))],
        [((5, width), F32)] * 2 + [((width,), F32), ((patches, width), F32)] + biases
        + [((4, width), F32)] * 2 + biases,
        [],
        limit=8 << 20,
    )

    def heads(g):
        return jnp.swapaxes(g.reshape(3, half, width), 1, 2)

    return (
        encoded_out, predicted_out, input_out, heads(enc_gq), hb_enc, enc_gp, enc_g1, b1_enc,
        enc_g2, grad_enc_gains, grad_enc_shifts, heads(reg_gq), hb_reg, reg_gp, reg_g1, b1_reg,
        reg_g2, grad_reg_gains, grad_reg_shifts, grad_pos, token,
    )


def solution(mesh):
    if mesh.shape["dp"] == 16:
        mesh = jax.sharding.Mesh(mesh.devices.reshape(4, 2, 2, 2), (*CHIPS, "tp"))
        dp = CHIPS
    else:
        dp = "dp"
    whole, rows = P(), P(dp, None)
    columns, heads = P(None, "tp"), P(None, None, "tp")
    down = P("tp", None)
    weights = (heads, columns, down, columns, P("tp"), down, whole, whole)
    return jax.shard_map(
        body,
        mesh=mesh,
        in_specs=(rows, rows, *weights, *weights, whole, whole, rows, rows),
        out_specs=(rows, rows, rows, *weights, *weights, whole, whole),
        check_vma=False,
    )
```
